32 devices in a mesh: parts: 2 (over y), ap: 16 (over z, x, core).
Axes of the slice: x: 2, y: 2, z: 4, core: 2. Of those that a mesh axis runs over, the one named last changes fastest.
Arguments:
- channel: bfloat16 [32, 12, 2, 32, 512], P(('parts', 'ap')), parts along dimension 0, may hold values from -6 to 6
- precoder: bfloat16 [2, 16384, 512], P(None, ('parts', 'ap')), parts along dimension 1
- visible: int32 [32, 12], P(('parts', 'ap')), parts along dimension 0, may hold values from 0 to 15, all different within a row
- cluster: int32 [1024, 4], P('parts'), parts along dimension 0, may hold values from 0 to 15, all different within a row; in each aligned block of 512 rows (0 to 511, 512 to 1023, ...) at most 256 rows name the same one
Outputs:
- effective: float32 [1024, 2, 512], P(('parts', 'ap')), parts along dimension 0
The draws below stay inside these ranges and needn't reach their ends.
There are 2 independent parts, one for each index of `parts`. The reference program is written for one: setup_inputs(seed, part) draws one part's arguments, and reference() takes and returns one part's arrays. A program takes and returns all parts, laid end to end along the dimension named above; each array names one. Nothing has to cross between parts.
Inputs may be any that keep to these rules, and one draw needn't show every extreme that they name: `visible`: each row names 12 different user groups, and every user group is named by some AP group. `cluster`: each row names 4 different AP groups; every AP group serves some planned user, at most 256 of them, and some AP group serves exactly 256.
All inputs are finite; a program needn't handle non-finite values.
Results may differ from the reference program's by a relative error of at most 0.0029.
Values sent between devices are 32-bit elements; how exact they have to be, the bound alone decides.
No kernel may reach another device: no remote copies, remote signals or barrier semaphores. Data moves between devices by JAX's collectives and lax.ppermute only.
A program may use at most 128 MiB of HBM per device.

```python
import math
import jax
import jax.numpy as jnp
import numpy as np
from jax import lax

GROUP_USERS = 32
HELD_GROUPS = 12
PRECODER_COLUMNS = 512
CL = 4
SERVE = 256
GROUP_ANTENNAS = 512
ANTENNA_TOTAL = 8192
USERS = 512
N_AP = 16


def draw_precoder(key, part):
    key = jax.random.fold_in(key, 11)
    first_random_key, second_random_key = jax.random.split(key)
    user_position = jnp.arange(ANTENNA_TOTAL, dtype=jnp.float32) / max(ANTENNA_TOTAL - 1, 1)
    spread_values = jnp.exp(jax.random.uniform(second_random_key, (ANTENNA_TOTAL,), jnp.float32, 0.0, math.log(10.0)))
    factor = (1.0 + 2.0 * user_position) * spread_values
    base_offset = jax.random.normal(first_random_key, (2, ANTENNA_TOTAL, PRECODER_COLUMNS), jnp.float32)
    return (base_offset * factor[None, :, None]).astype(jnp.bfloat16)


def block_scale(stream_key, extent, pieces, low, top_value):
    def one(position, blocks):
        draws = jax.random.uniform(jax.random.fold_in(jax.random.fold_in(stream_key, 6), position), (blocks,), jnp.float32, low / len(pieces), top_value / len(pieces))
        return jnp.repeat(jnp.exp(draws), extent[position] // blocks).reshape((-1,) + (1,) * (len(extent) - position - 1))

    loudness = one(*pieces[0])
    for cut in pieces[1:]:
        loudness = loudness * one(*cut)
    return loudness


def choose_distinct(own_key, rows, count, top, lift):
    order = jax.random.permutation(jax.random.fold_in(own_key, 1), count)
    favour = order
    for power in range(3):
        favour = favour * favour // count
    favour = favour * lift // count
    tickets = jax.random.randint(jax.random.fold_in(own_key, 2), (rows, count), 0, 4096) + favour
    fixed_rows = jax.random.permutation(jax.random.fold_in(own_key, 3), rows)[jnp.arange(count) % rows]
    tickets = jnp.where(jnp.arange(rows)[:, None] == fixed_rows[None, :], 1 << 14, tickets)
    priority = tickets * count + jnp.arange(count)
    return lax.top_k(priority.astype(jnp.int32), top)[1].astype(jnp.int32)


def routed_block(rng, own, number, rows, number_of, top, reach, lean):
    ranking = jax.random.permutation(rng, number_of)
    heavy_load, ordinary = portions_of(number_of, rows * top, reach, lean, True), portions_of(number_of, rows * top, reach, lean, False)
    places = jnp.arange(number_of)

    def named(lengths, turn):
        used = int((lengths > 0).sum())
        fixed = max(1, used // 4)
        passed = fixed + (places - fixed + turn * (used - fixed)) % max(1, number_of - fixed)
        return jnp.zeros((number_of,), jnp.int32).at[ranking[jnp.where(places < fixed, places, passed)]].set(jnp.asarray(lengths, jnp.int32))

    lengths = jnp.where(number % 4 == 0, named(heavy_load, number // 4), named(ordinary, number - number // 4 - 1))
    mixed = jax.random.permutation(jax.random.fold_in(own, 3), number_of)
    giver, sink = mixed[0:number_of // 2 * 2:2], mixed[1:number_of // 2 * 2:2]
    room = jnp.minimum(lengths[giver] - 1, reach - lengths[sink]) // 2
    room = jnp.where((giver == ranking[0]) | (sink == ranking[0]) | (lengths[sink] == 0), 0, jnp.maximum(room, 0))
    passed = jax.random.randint(jax.random.fold_in(own, 4), (number_of // 2,), 0, 1 << 20) % (room + 1)
    lengths = lengths.at[giver].add(-passed).at[sink].add(passed)
    labels = jnp.searchsorted(jnp.cumsum(lengths), jnp.arange(rows * top), side="right").astype(jnp.int32)
    grid = labels.reshape(top, rows).T
    grid = grid[jax.random.permutation(jax.random.fold_in(own, 1), rows)]
    turn = jax.random.randint(jax.random.fold_in(own, 2), (rows, 1), 0, top)
    return jnp.take_along_axis(grid, (jnp.arange(top)[None, :] + turn) % top, axis=1)


def portions_of(count, total, bound, skew, full):
    weights = [(1 << 20) // math.isqrt(standing ** skew) + 1 for standing in range(1, count + 1)]
    largest = bound if full else min(bound, max(-(-total // count), total * weights[0] // sum(weights)))
    least = 1 if total - largest >= count - 1 else 0
    counts, rest = [largest] + [least] * (count - 1), total - largest - least * (count - 1)
    while rest > 0:
        candidates = [i for i in range(1, count) if counts[i] < largest] or [i for i in range(1, count) if counts[i] < bound]
        mass, left = sum([weights[i] for i in candidates]), rest
        for i in candidates:
            addition = min(bound - counts[i], max(1, left * weights[i] // mass), rest)
            counts[i] = counts[i] + addition
            rest = rest - addition
    return np.array(counts)


def bell_draw(own_key, extent, spread, most, cuts=(), held_as=jnp.bfloat16):
    values = jax.random.normal(own_key, extent, jnp.float32) * spread
    if len(cuts) > 0:
        values = block_scale(own_key, extent, cuts, -0.22, 0.18) * values
    return jnp.clip(values, min=-most, max=most).astype(held_as)


def setup_inputs(seed: int = 0, part: int = 0) -> dict:
    key_of = jax.random.split(jax.random.key(seed), 5)
    own_keys = jax.random.split(jax.random.fold_in(key_of[4], part), 5)
    channel = bell_draw(own_keys[0], (N_AP, HELD_GROUPS, 2, GROUP_USERS, GROUP_ANTENNAS), 1.0, 6.0, ((0, 16),))
    precoder = draw_precoder(jax.random.fold_in(jax.random.fold_in(key_of[4], part), 71), part)
    visible = choose_distinct(own_keys[2], N_AP, N_AP, HELD_GROUPS, 12000)
    cluster_keys = jax.random.split(jax.random.fold_in(own_keys[3], 1), PRECODER_COLUMNS // PRECODER_COLUMNS)
    cluster_turns = jax.random.permutation(jax.random.fold_in(own_keys[3], 3), PRECODER_COLUMNS // PRECODER_COLUMNS)
    cluster = jax.vmap(lambda own, number: routed_block(jax.random.fold_in(own_keys[3], 2), own, number, PRECODER_COLUMNS, N_AP, CL, SERVE, 1))(cluster_keys, cluster_turns).reshape((PRECODER_COLUMNS, CL))
    return {"channel": channel, "precoder": precoder, "visible": visible, "cluster": cluster}


epsilon = 1e-06

def reference(channel, precoder, visible, cluster):
    owners = jnp.arange(N_AP, dtype=jnp.int32)
    served_mask = jnp.any(cluster[None, :, :] == owners[:, None, None], axis=2).astype(jnp.float32)
    masked_channel = precoder.astype(jnp.float32).reshape(2, N_AP, GROUP_ANTENNAS, PRECODER_COLUMNS) * served_mask[None, :, None, :]
    power = lax.optimization_barrier(jnp.sum(masked_channel * masked_channel, axis=(0, 1, 2)))
    scaled = (masked_channel * lax.rsqrt(power + epsilon)).astype(jnp.bfloat16)
    first = jnp.concatenate([scaled[0], scaled[1]], axis=-1)
    second = jnp.concatenate([scaled[1], -scaled[0]], axis=-1)

    def one_group(total, inputs):
        chan, left, right, groups = inputs
        term = jnp.einsum('vua,ar->vur', chan[:, 0].astype(jnp.float32), left.astype(jnp.float32), precision=lax.Precision.HIGHEST)
        term = term + jnp.einsum('vua,ar->vur', chan[:, 1].astype(jnp.float32), right.astype(jnp.float32), precision=lax.Precision.HIGHEST)
        return (total.at[groups.astype(jnp.int32)].add(term), None)
    total = jnp.zeros((N_AP, GROUP_USERS, 2 * PRECODER_COLUMNS), jnp.float32)
    total, unused = lax.scan(one_group, total, (channel, first, second, visible))
    return total.reshape(USERS, 2, PRECODER_COLUMNS)
```

```python
import functools

import jax
import jax.numpy as jnp
from jax import lax
from jax.experimental import pallas as pl
from jax.experimental.pallas import tpu as pltpu
from jax.sharding import PartitionSpec as P

epsilon = 1e-06
MIB = 1 << 20


def bit_orders(bits):
    first = list(range(bits))
    second = list(first)
    if bits > 2:
        second[1], second[2] = second[2], second[1]
    return first, second


def second_place(place, bits):
    first, second = bit_orders(bits)
    tail = bits - 1
    value = {bit: (place >> (tail - 1 - at)) & 1 for at, bit in enumerate(first[1:])}
    out = 0
    for bit in second[1:]:
        out = out * 2 + value[bit]
    return out


def local_kernel(which, bits, visible, cluster, channel, precoder, out, rows):
    me = lax.axis_index("ap")
    held, users = channel.shape[1], channel.shape[3]
    columns = precoder.shape[2]
    slots = out.shape[0] // (2 * (users // 8) * (columns // 128))
    tiles = (users // 8) * (columns // 128)
    first, _ = bit_orders(bits)
    rows[...] = jnp.zeros_like(rows)

    def place_one(v):
        relative = visible[0, v] ^ me
        place = 0
        for bit in first[1:]:
            place = place * 2 + (1 - ((relative >> bit) & 1))

        @pl.when((relative & 1) == which)
        def _():
            at = pl.ds(pl.multiple_of(place * users, users), users)
            rows[0, at, :] = channel[0, v, 0]
            rows[1, at, :] = channel[0, v, 1]

    for v in range(held):
        place_one(v)

    served = jnp.max((cluster[...] == me).astype(jnp.float32), axis=0, keepdims=True) > 0.0
    real, imag = precoder[0], precoder[1]
    chunk = min(slots, 8)

    def dot(a, b):
        return jnp.dot(a, b, preferred_element_type=jnp.float32)

    for base in range(0, slots, chunk):
        at = slice(base * users, (base + chunk) * users)
        left, right = rows[0, at, :], rows[1, at, :]
        parts = (
            dot(left, real) + dot(right, imag),
            dot(left, imag) - dot(right, real),
        )
        for half, value in enumerate(parts):
            value = jnp.where(served, value, 0.0)
            for slot in range(chunk):
                place = base + slot
                if half == 1:
                    place = slots + second_place(place, bits)
                for block in range(columns // 128):
                    piece = value[slot * users:(slot + 1) * users, block * 128:(block + 1) * 128]
                    start = place * tiles + block * (users // 8)
                    out[start:start + users // 8] = piece.reshape(users // 8, 8, 128)
    power = jnp.zeros((1, columns), jnp.float32)
    for plane in range(2):
        wide = precoder[plane].astype(jnp.float32)
        power = power + jnp.sum(wide * wide, axis=0, keepdims=True)
    power = jnp.where(served, power, 0.0)
    tile = jnp.concatenate(
        [power[:, block * 128:(block + 1) * 128] for block in range(columns // 128)]
        + [jnp.zeros((8 - columns // 128, 128), jnp.float32)],
        axis=0,
    )
    out[2 * slots * tiles] = tile


def local_products(which, bits, visible, cluster, channel, precoder):
    held, users, antennas = channel.shape[1], channel.shape[3], channel.shape[4]
    columns = precoder.shape[2]
    tiles = (users // 8) * (columns // 128)
    slots = 1 << (bits - 1)
    vmem = pl.BlockSpec(memory_space=pltpu.VMEM)
    flops = 8 * slots * users * antennas * columns
    size = channel.size * 2 + precoder.size * 2 + 2 * slots * tiles * 4096
    return pl.pallas_call(
        functools.partial(local_kernel, which, bits),
        out_shape=jax.ShapeDtypeStruct((2 * slots * tiles + 1, 8, 128), jnp.float32),
        in_specs=[pl.BlockSpec(memory_space=pltpu.SMEM), vmem, vmem, vmem],
        out_specs=vmem,
        scratch_shapes=[pltpu.VMEM((2, slots * users, antennas), jnp.bfloat16)],
        compiler_params=pltpu.CompilerParams(vmem_limit_bytes=48 * MIB if slots > 8 else 24 * MIB),
        cost_estimate=pl.CostEstimate(flops=flops, bytes_accessed=size, transcendentals=0),
        name="local_products",
    )(visible, cluster, channel, precoder)


def part_spec(start, count):
    return pl.BlockSpec((count, 8, 128), lambda i: (start // count, 0, 0))


def sum_kernel(halves, terms, with_power, count, *refs):
    out = refs[-1]
    at = 0
    for half in range(halves):
        total = refs[at][...]
        for term in range(1, terms):
            total = total + refs[at + term][...]
        at += terms
        out[half * count:(half + 1) * count] = total
    if with_power:
        total = refs[at][...]
        for term in range(1, terms):
            total = total + refs[at + term][...]
        out[halves * count:] = total


def summed(held, halves, left, tiles, with_power):
    count = left * tiles
    arrays, specs = [], []
    for half in halves:
        for pieces in held:
            array, base, slots = pieces[half]
            arrays.append(array)
            specs.append(part_spec((base + slots - 2 * left) * tiles, count))
    if with_power:
        for pieces in held:
            array = pieces[0][0]
            arrays.append(array)
            specs.append(part_spec(array.shape[0] - 1, 1))
    size = len(halves) * count + int(with_power)
    return pl.pallas_call(
        functools.partial(sum_kernel, len(halves), len(held), with_power, count),
        grid=(1,),
        out_shape=jax.ShapeDtypeStruct((size, 8, 128), jnp.float32),
        in_specs=specs,
        out_specs=pl.BlockSpec((size, 8, 128), lambda i: (0, 0, 0)),
        compiler_params=pltpu.CompilerParams(vmem_limit_bytes=48 * MIB if left > 4 else 24 * MIB),
        cost_estimate=pl.CostEstimate(
            flops=size * 1024 * len(held), bytes_accessed=size * 4096 * (len(held) + 1), transcendentals=0
        ),
        name="summed",
    )(*arrays)


def final_kernel(terms, users, *refs):
    out = refs[-1]
    power = refs[2 * terms][0]
    for term in range(1, terms):
        power = power + refs[2 * terms + term][0]
    scale = lax.rsqrt(power + epsilon)
    blocks = out.shape[2] // 128
    for half in range(2):
        for block in range(blocks):
            at = slice(block * (users // 8), (block + 1) * (users // 8))
            total = refs[half * terms][at]
            for term in range(1, terms):
                total = total + refs[half * terms + term][at]
            factor = scale[block:block + 1, :]
            total = total.reshape(users, 128)
            value = jnp.where(factor > 0.0, total * factor, 0.0)
            out[:, half, block * 128:(block + 1) * 128] = value


def finish(held, tiles, users, columns):
    arrays, specs = [], []
    for half in range(2):
        for pieces in held:
            array, base, slots = pieces[half]
            arrays.append(array)
            specs.append(part_spec((base + slots - 1) * tiles, tiles))
    for pieces in held:
        array = pieces[0][0]
        arrays.append(array)
        specs.append(part_spec(array.shape[0] - 1, 1))
    return pl.pallas_call(
        functools.partial(final_kernel, len(held), users),
        grid=(1,),
        out_shape=jax.ShapeDtypeStruct((users, 2, columns), jnp.float32),
        in_specs=specs,
        out_specs=pl.BlockSpec((users, 2, columns), lambda i: (0, 0, 0)),
        name="finish",
    )(*arrays)


def on_device(channel, precoder, visible, cluster):
    devices = lax.axis_size("ap")
    bits = devices.bit_length() - 1
    users, columns = channel.shape[3], precoder.shape[2]
    tiles = (users // 8) * (columns // 128)
    orders = bit_orders(bits)
    turned = cluster.T

    def swap(value, bit):
        return lax.ppermute(value, "ap", [(i, i ^ (1 << bit)) for i in range(devices)])

    slots = devices // 2
    sent = local_products(1, bits, visible, turned, channel, precoder)
    got = swap(sent, 0)
    kept = local_products(0, bits, visible, turned, channel, precoder)
    held = [
        ((kept, 0, slots), (kept, slots, slots)),
        ((got, 0, slots), (got, slots, slots)),
    ]
    for step in range(1, bits):
        slots //= 2
        if orders[0][step] == orders[1][step]:
            sent = summed(held, (0, 1), slots, tiles, True)
            got = swap(sent, orders[0][step])
            held.append(((got, 0, slots), (got, slots, slots)))
        else:
            sent = [summed(held, (half,), slots, tiles, half == 0) for half in range(2)]
            got = [swap(sent[half], orders[half][step]) for half in range(2)]
            held.append(((got[0], 0, slots), (got[1], 0, slots)))
    return finish(held, tiles, users, columns)


def solution(mesh):
    in_specs = (
        P(("parts", "ap"), None, None, None, None),
        P(None, ("parts", "ap"), None),
        P(("parts", "ap"), None),
        P("parts", None),
    )
    out_specs = P(("parts", "ap"), None, None)
    return jax.shard_map(
        on_device, mesh=mesh, in_specs=in_specs, out_specs=out_specs, check_vma=False
    )
```

```python
import functools

import jax
import jax.numpy as jnp
from jax import lax
from jax.experimental import pallas as pl
from jax.experimental.pallas import tpu as pltpu
from jax.sharding import PartitionSpec as P

epsilon = 1e-06
MIB = 1 << 20
CHUNKS = 2


def bit_orders(bits):
    first = list(range(bits))
    second = list(first)
    if bits > 2:
        second[1], second[2] = second[2], second[1]
    return first, second


def second_place(place, bits):
    first, second = bit_orders(bits)
    tail = bits - 1
    value = {bit: (place >> (tail - 1 - at)) & 1 for at, bit in enumerate(first[1:])}
    out = 0
    for bit in second[1:]:
        out = out * 2 + value[bit]
    return out


def write_products(bits, slots, rows, weights, served, out):
    users = rows.shape[0] // slots
    antennas = rows.shape[1] // 2
    width = weights.shape[1]
    blocks, steps = width // 128, users // 8
    tiles = blocks * steps
    group = min(slots, 8)
    for base in range(0, slots, group):
        plain = rows[base * users:(base + group) * users, :]
        turned = jnp.concatenate([-plain[:, antennas:], plain[:, :antennas]], axis=1)
        both = jnp.concatenate([plain, turned], axis=0)
        value = jnp.dot(both, weights, preferred_element_type=jnp.float32)
        value = jnp.where(served, value, 0.0)
        for half in range(2):
            for slot in range(group):
                place = base + slot
                if half == 1:
                    place = slots + second_place(place, bits)
                top = (half * group + slot) * users
                for block in range(blocks):
                    piece = value[top:top + users, block * 128:(block + 1) * 128]
                    start = place * tiles + block * steps
                    out[start:start + steps] = piece.reshape(steps, 8, 128)


def power_tile(weights, served):
    wide = weights.astype(jnp.float32)
    power = jnp.sum(wide * wide, axis=0, keepdims=True)
    power = jnp.where(served, power, 0.0)
    blocks = power.shape[1] // 128
    pieces = [power[:, block * 128:(block + 1) * 128] for block in range(blocks)]
    return jnp.concatenate(pieces + [jnp.zeros((8 - blocks, 128), jnp.float32)], axis=0)


def first_kernel(
    bits, visible, cluster, channel, precoder,
    out, rows, weights, served,
    seen, names, raw, sems,
):
    me = lax.axis_index("ap")
    held, users, antennas = raw.shape[1], raw.shape[3], raw.shape[4]
    columns = weights.shape[1]
    width = columns // CHUNKS
    slots = rows.shape[1] // users
    first, _ = bit_orders(bits)
    loads = [
        pltpu.make_async_copy(visible, seen, sems.at[0]),
        pltpu.make_async_copy(cluster, names, sems.at[1]),
        pltpu.make_async_copy(channel, raw, sems.at[2]),
    ]
    for chunk in range(CHUNKS):
        at = pl.ds(chunk * width, width)
        loads.append(
            pltpu.make_async_copy(precoder.at[:, at], weights.at[:, at], sems.at[3 + chunk])
        )
    for load in loads:
        load.start()
    rows[...] = jnp.zeros_like(rows)
    loads[0].wait()
    loads[1].wait()
    mask = jnp.max((names[...] == me).astype(jnp.float32), axis=0, keepdims=True)
    served[...] = mask
    loads[2].wait()
    for v in range(held):
        relative = seen[0, v] ^ me
        place = 0
        for bit in first[1:]:
            place = place * 2 + (1 - ((relative >> bit) & 1))
        which = 1 - (relative & 1)
        at = pl.ds(pl.multiple_of(place * users, users), users)
        rows[which, at, 0:antennas] = raw[0, v, 0]
        rows[which, at, antennas:2 * antennas] = raw[0, v, 1]
    loads[3].wait()
    mine = mask[:, 0:width] > 0.0
    chosen = weights[:, 0:width]
    write_products(bits, slots, rows.at[0], chosen, mine, out)
    out[out.shape[0] - 1] = power_tile(chosen, mine)
    for load in loads[4:]:
        load.wait()


def next_kernel(bits, which, chunk, rows, weights, served, out):
    width = weights.shape[1] // CHUNKS
    at = slice(chunk * width, (chunk + 1) * width)
    mine = served[:, at] > 0.0
    chosen = weights[:, at]
    slots = 1 << (bits - 1)
    write_products(bits, slots, rows.at[which], chosen, mine, out)
    out[out.shape[0] - 1] = power_tile(chosen, mine)


def message(tiles):
    return jax.ShapeDtypeStruct((tiles, 8, 128), jnp.float32)


def estimate(slots, users, antennas, columns):
    return pl.CostEstimate(
        flops=8 * slots * users * antennas * columns,
        bytes_accessed=slots * users * (antennas * 4 + columns * 8) + antennas * columns * 4,
        transcendentals=0,
    )


def first_products(bits, visible, cluster, channel, precoder):
    held, users, antennas = channel.shape[1], channel.shape[3], channel.shape[4]
    columns = precoder.shape[1]
    slots = 1 << (bits - 1)
    tiles = (users // 8) * (columns // CHUNKS // 128)
    hbm = pl.BlockSpec(memory_space=pltpu.HBM)
    vmem = pl.BlockSpec(memory_space=pltpu.VMEM)
    return pl.pallas_call(
        functools.partial(first_kernel, bits),
        out_shape=(
            message(2 * slots * tiles + 1),
            jax.ShapeDtypeStruct((2, slots * users, 2 * antennas), jnp.bfloat16),
            jax.ShapeDtypeStruct(precoder.shape, jnp.bfloat16),
            jax.ShapeDtypeStruct((1, columns), jnp.float32),
        ),
        in_specs=[hbm] * 4,
        out_specs=(vmem,) * 4,
        scratch_shapes=[
            pltpu.SMEM(visible.shape, jnp.int32),
            pltpu.VMEM(cluster.shape, jnp.int32),
            pltpu.VMEM(channel.shape, jnp.bfloat16),
            pltpu.SemaphoreType.DMA((3 + CHUNKS,)),
        ],
        compiler_params=pltpu.CompilerParams(vmem_limit_bytes=48 * MIB if slots > 8 else 24 * MIB),
        cost_estimate=estimate(slots, users, antennas, columns // CHUNKS),
        name="first_products",
    )(*[pltpu.with_memory_space_constraint(a, pltpu.HBM) for a in (visible, cluster, channel, precoder)])


def next_products(bits, which, chunk, rows, weights, served, users):
    slots = 1 << (bits - 1)
    antennas, columns = weights.shape[0] // 2, weights.shape[1]
    tiles = (users // 8) * (columns // CHUNKS // 128)
    vmem = pl.BlockSpec(memory_space=pltpu.VMEM)
    return pl.pallas_call(
        functools.partial(next_kernel, bits, which, chunk),
        out_shape=message(2 * slots * tiles + 1),
        in_specs=[vmem] * 3,
        out_specs=vmem,
        compiler_params=pltpu.CompilerParams(vmem_limit_bytes=48 * MIB if slots > 8 else 16 * MIB),
        cost_estimate=estimate(slots, users, antennas, columns // CHUNKS),
        name="next_products",
    )(rows, weights, served)


def part_spec(start, count):
    return pl.BlockSpec((count, 8, 128), lambda i: (start // count, 0, 0))


def sum_kernel(halves, terms, with_power, count, *refs):
    out = refs[-1]
    at = 0
    for half in range(halves):
        total = refs[at][...]
        for term in range(1, terms):
            total = total + refs[at + term][...]
        at += terms
        out[half * count:(half + 1) * count] = total
    if with_power:
        total = refs[at][...]
        for term in range(1, terms):
            total = total + refs[at + term][...]
        out[halves * count:] = total


def summed(held, halves, left, tiles, with_power):
    count = left * tiles
    arrays, specs = [], []
    for half in halves:
        for pieces in held:
            array, base, slots = pieces[half]
            arrays.append(array)
            specs.append(part_spec((base + slots - 2 * left) * tiles, count))
    if with_power:
        for pieces in held:
            array = pieces[0][0]
            arrays.append(array)
            specs.append(part_spec(array.shape[0] - 1, 1))
    size = len(halves) * count + int(with_power)
    return pl.pallas_call(
        functools.partial(sum_kernel, len(halves), len(held), with_power, count),
        grid=(1,),
        out_shape=message(size),
        in_specs=specs,
        out_specs=pl.BlockSpec((size, 8, 128), lambda i: (0, 0, 0)),
        compiler_params=pltpu.CompilerParams(vmem_limit_bytes=48 * MIB if left > 4 else 8 * MIB),
        cost_estimate=pl.CostEstimate(
            flops=size * 1024 * len(held), bytes_accessed=size * 4096 * (len(held) + 1), transcendentals=0
        ),
        name="summed",
    )(*arrays)


def final_kernel(terms, users, *refs):
    out = refs[-1]
    blocks = out.shape[2] // 128 // CHUNKS
    steps = users // 8
    for chunk in range(CHUNKS):
        mine = refs[chunk * 3 * terms:(chunk + 1) * 3 * terms]
        power = mine[2 * terms][0]
        for term in range(1, terms):
            power = power + mine[2 * terms + term][0]
        scale = lax.rsqrt(power + epsilon)
        for half in range(2):
            for block in range(blocks):
                at = slice(block * steps, (block + 1) * steps)
                total = mine[half * terms][at]
                for term in range(1, terms):
                    total = total + mine[half * terms + term][at]
                factor = scale[block:block + 1, :]
                total = total.reshape(users, 128)
                value = jnp.where(factor > 0.0, total * factor, 0.0)
                left = (chunk * blocks + block) * 128
                out[:, half, left:left + 128] = value


def finish(helds, tiles, users, columns):
    arrays, specs = [], []
    for held in helds:
        for half in range(2):
            for pieces in held:
                array, base, slots = pieces[half]
                arrays.append(array)
                specs.append(part_spec((base + slots - 1) * tiles, tiles))
        for pieces in held:
            array = pieces[0][0]
            arrays.append(array)
            specs.append(part_spec(array.shape[0] - 1, 1))
    return pl.pallas_call(
        functools.partial(final_kernel, len(helds[0]), users),
        grid=(1,),
        out_shape=jax.ShapeDtypeStruct((users, 2, columns), jnp.float32),
        in_specs=specs,
        out_specs=pl.BlockSpec((users, 2, columns), lambda i: (0, 0, 0)),
        compiler_params=pltpu.CompilerParams(vmem_limit_bytes=8 * MIB),
        name="finish",
    )(*arrays)


def on_device(channel, precoder, visible, cluster):
    devices = lax.axis_size("ap")
    bits = devices.bit_length() - 1
    users, columns = channel.shape[3], precoder.shape[2]
    tiles = (users // 8) * (columns // CHUNKS // 128)
    orders = bit_orders(bits)
    flat = precoder.reshape(-1, columns)

    def swap(value, bit):
        return lax.ppermute(value, "ap", [(i, i ^ (1 << bit)) for i in range(devices)])

    slots = devices // 2
    sent, rows, weights, served = first_products(bits, visible, cluster.T, channel, flat)
    got = [swap(sent, 0)]
    for chunk in range(1, CHUNKS):
        got.append(swap(next_products(bits, 0, chunk, rows, weights, served, users), 0))
    helds = []
    for chunk in range(CHUNKS):
        kept = next_products(bits, 1, chunk, rows, weights, served, users)
        helds.append([
            ((kept, 0, slots), (kept, slots, slots)),
            ((got[chunk], 0, slots), (got[chunk], slots, slots)),
        ])
    for step in range(1, bits):
        slots //= 2
        for held in helds:
            if orders[0][step] == orders[1][step]:
                sent = summed(held, (0, 1), slots, tiles, True)
                got = swap(sent, orders[0][step])
                held.append(((got, 0, slots), (got, slots, slots)))
            else:
                sent = [summed(held, (half,), slots, tiles, half == 0) for half in range(2)]
                got = [swap(sent[half], orders[half][step]) for half in range(2)]
                held.append(((got[0], 0, slots), (got[1], 0, slots)))
    return finish(helds, tiles, users, columns)


def solution(mesh):
    in_specs = (
        P(("parts", "ap"), None, None, None, None),
        P(None, ("parts", "ap"), None),
        P(("parts", "ap"), None),
        P("parts", None),
    )
    out_specs = P(("parts", "ap"), None, None)
    return jax.shard_map(
        on_device, mesh=mesh, in_specs=in_specs, out_specs=out_specs, check_vma=False
    )
```

```python
import functools

import jax
import jax.numpy as jnp
from jax import lax
from jax.experimental import pallas as pl
from jax.experimental.pallas import tpu as pltpu
from jax.sharding import PartitionSpec as P

epsilon = 1e-06
MIB = 1 << 20
CHUNKS = 2


def quad_bits(bits):
    return (1, 2) if bits > 2 else ()


def place_of(group, me, bits):
    quad = quad_bits(bits)
    place = 0
    for bit in reversed(quad):
        place = place * 2 + ((group >> bit) & 1)
    for bit in range(1, bits):
        if bit not in quad:
            place = place * 2 + (1 - (((group ^ me) >> bit) & 1))
    return place


def write_products(slots, rows, weights, served, out):
    users = rows.shape[0] // slots
    antennas = rows.shape[1] // 2
    blocks, steps = weights.shape[1] // 128, users // 8
    group = min(slots, 8)
    for base in range(0, slots, group):
        plain = rows[base * users:(base + group) * users, :]
        turned = jnp.concatenate([-plain[:, antennas:], plain[:, :antennas]], axis=1)
        both = jnp.concatenate([plain, turned], axis=0)
        value = jnp.dot(both, weights, preferred_element_type=jnp.float32)
        value = jnp.where(served, value, 0.0)
        for half in range(2):
            for slot in range(group):
                top = (half * group + slot) * users
                for block in range(blocks):
                    piece = value[top:top + users, block * 128:(block + 1) * 128]
                    start = (((base + slot) * 2 + half) * blocks + block) * steps
                    out[start:start + steps] = piece.reshape(steps, 8, 128)


def power_tile(weights, served):
    wide = weights.astype(jnp.float32)
    power = jnp.sum(wide * wide, axis=0, keepdims=True)
    power = jnp.where(served, power, 0.0)
    blocks = power.shape[1] // 128
    pieces = [power[:, block * 128:(block + 1) * 128] for block in range(blocks)]
    return jnp.concatenate(pieces + [jnp.zeros((8 - blocks, 128), jnp.float32)], axis=0)


def first_kernel(
    bits, visible, cluster, channel, precoder,
    out, rows, weights, served,
    seen, names, raw, sems,
):
    me = lax.axis_index("ap")
    held, users, antennas = raw.shape[1], raw.shape[3], raw.shape[4]
    columns = weights.shape[1]
    width = columns // CHUNKS
    slots = rows.shape[1] // users
    loads = [
        pltpu.make_async_copy(visible, seen, sems.at[0]),
        pltpu.make_async_copy(cluster, names, sems.at[1]),
        pltpu.make_async_copy(channel, raw, sems.at[2]),
    ]
    for chunk in range(CHUNKS):
        at = pl.ds(chunk * width, width)
        loads.append(
            pltpu.make_async_copy(precoder.at[:, at], weights.at[:, at], sems.at[3 + chunk])
        )
    for load in loads:
        load.start()
    rows[...] = jnp.zeros_like(rows)
    loads[0].wait()
    loads[1].wait()
    mask = jnp.max((names[...] == me).astype(jnp.float32), axis=0, keepdims=True)
    served[...] = mask
    loads[2].wait()
    for v in range(held):
        which = 1 - ((seen[0, v] ^ me) & 1)
        place = place_of(seen[0, v], me, bits)
        at = pl.ds(pl.multiple_of(place * users, users), users)
        rows[which, at, 0:antennas] = raw[0, v, 0]
        rows[which, at, antennas:2 * antennas] = raw[0, v, 1]
    loads[3].wait()
    mine = mask[:, 0:width] > 0.0
    chosen = weights[:, 0:width]
    write_products(slots, rows.at[0], chosen, mine, out)
    out[out.shape[0] - 1] = power_tile(chosen, mine)
    for load in loads[4:]:
        load.wait()


def next_kernel(bits, which, chunk, rows, weights, served, out):
    width = weights.shape[1] // CHUNKS
    at = slice(chunk * width, (chunk + 1) * width)
    mine = served[:, at] > 0.0
    chosen = weights[:, at]
    slots = 1 << (bits - 1)
    write_products(slots, rows.at[which], chosen, mine, out)
    out[out.shape[0] - 1] = power_tile(chosen, mine)


def message(tiles):
    return jax.ShapeDtypeStruct((tiles, 8, 128), jnp.float32)


def estimate(slots, users, antennas, columns):
    return pl.CostEstimate(
        flops=8 * slots * users * antennas * columns,
        bytes_accessed=slots * users * (antennas * 4 + columns * 8) + antennas * columns * 4,
        transcendentals=0,
    )


def first_products(bits, visible, cluster, channel, precoder):
    held, users, antennas = channel.shape[1], channel.shape[3], channel.shape[4]
    columns = precoder.shape[1]
    slots = 1 << (bits - 1)
    tiles = (users // 8) * (columns // CHUNKS // 128)
    hbm = pl.BlockSpec(memory_space=pltpu.HBM)
    vmem = pl.BlockSpec(memory_space=pltpu.VMEM)
    return pl.pallas_call(
        functools.partial(first_kernel, bits),
        out_shape=(
            message(2 * slots * tiles + 1),
            jax.ShapeDtypeStruct((2, slots * users, 2 * antennas), jnp.bfloat16),
            jax.ShapeDtypeStruct(precoder.shape, jnp.bfloat16),
            jax.ShapeDtypeStruct((1, columns), jnp.float32),
        ),
        in_specs=[hbm] * 4,
        out_specs=(vmem,) * 4,
        scratch_shapes=[
            pltpu.SMEM(visible.shape, jnp.int32),
            pltpu.VMEM(cluster.shape, jnp.int32),
            pltpu.VMEM(channel.shape, jnp.bfloat16),
            pltpu.SemaphoreType.DMA((3 + CHUNKS,)),
        ],
        compiler_params=pltpu.CompilerParams(vmem_limit_bytes=48 * MIB if slots > 8 else 24 * MIB),
        cost_estimate=estimate(slots, users, antennas, columns // CHUNKS),
        name="first_products",
    )(*[pltpu.with_memory_space_constraint(a, pltpu.HBM) for a in (visible, cluster, channel, precoder)])


def next_products(bits, which, chunk, rows, weights, served, users):
    slots = 1 << (bits - 1)
    antennas, columns = weights.shape[0] // 2, weights.shape[1]
    tiles = (users // 8) * (columns // CHUNKS // 128)
    vmem = pl.BlockSpec(memory_space=pltpu.VMEM)
    return pl.pallas_call(
        functools.partial(next_kernel, bits, which, chunk),
        out_shape=message(2 * slots * tiles + 1),
        in_specs=[vmem] * 3,
        out_specs=vmem,
        compiler_params=pltpu.CompilerParams(vmem_limit_bytes=48 * MIB if slots > 8 else 16 * MIB),
        cost_estimate=estimate(slots, users, antennas, columns // CHUNKS),
        name="next_products",
    )(rows, weights, served)


def add_up(refs, terms, count):
    total = refs[terms[0][0]][terms[0][1]:terms[0][1] + count]
    for ref, start in terms[1:]:
        total = total + refs[ref][start:start + count]
    return total


def sum_kernel(jobs, *refs):
    at = 0
    for terms, count in jobs:
        refs[-1][at:at + count] = add_up(refs, terms, count)
        at += count


def summed(arrays, jobs):
    size = sum(count for _, count in jobs)
    vmem = pl.BlockSpec(memory_space=pltpu.VMEM)
    reads = sum(len(terms) * count for terms, count in jobs)
    return pl.pallas_call(
        functools.partial(sum_kernel, jobs),
        out_shape=message(size),
        in_specs=[vmem] * len(arrays),
        out_specs=vmem,
        compiler_params=pltpu.CompilerParams(vmem_limit_bytes=8 * MIB),
        cost_estimate=pl.CostEstimate(
            flops=reads * 1024, bytes_accessed=(reads + size) * 4096, transcendentals=0
        ),
        name="summed",
    )(*arrays)


def final_kernel(jobs, users, *refs):
    out = refs[-1]
    blocks, steps = out.shape[2] // 128 // CHUNKS, users // 8
    for chunk, (terms, powers) in enumerate(jobs):
        scale = lax.rsqrt(add_up(refs, powers, 1)[0] + epsilon)
        total = add_up(refs, terms, 2 * blocks * steps)
        for half in range(2):
            for block in range(blocks):
                start = (half * blocks + block) * steps
                value = total[start:start + steps].reshape(users, 128)
                factor = scale[block:block + 1, :]
                value = jnp.where(factor > 0.0, value * factor, 0.0)
                left = (chunk * blocks + block) * 128
                out[:, half, left:left + 128] = value


def finish(arrays, jobs, users, columns):
    vmem = pl.BlockSpec(memory_space=pltpu.VMEM)
    return pl.pallas_call(
        functools.partial(final_kernel, jobs, users),
        out_shape=jax.ShapeDtypeStruct((users, 2, columns), jnp.float32),
        in_specs=[vmem] * len(arrays),
        out_specs=vmem,
        compiler_params=pltpu.CompilerParams(vmem_limit_bytes=8 * MIB),
        name="finish",
    )(*arrays)


def on_device(channel, precoder, visible, cluster):
    devices = lax.axis_size("ap")
    bits = devices.bit_length() - 1
    users, columns = channel.shape[3], precoder.shape[2]
    tiles = (users // 8) * (columns // CHUNKS // 128) * 2
    quad = quad_bits(bits)
    flat = precoder.reshape(-1, columns)

    def swap(value, bit):
        return lax.ppermute(value, "ap", [(i, i ^ (1 << bit)) for i in range(devices)])

    def square(value):
        low = 1 << quad[0]
        groups = [
            [i + low * member for member in range(4)]
            for i in range(devices) if (i >> quad[0]) & 3 == 0
        ]
        return lax.all_to_all(
            value, "ap", split_axis=0, concat_axis=0, axis_index_groups=groups, tiled=True
        )

    half = devices // 2
    sent, rows, weights, served = first_products(bits, visible, cluster.T, channel, flat)
    got = [swap(sent, 0)]
    for chunk in range(1, CHUNKS):
        got.append(swap(next_products(bits, 0, chunk, rows, weights, served, users), 0))
    lasts, jobs, base = [], [], 0
    for chunk in range(CHUNKS):
        kept = next_products(bits, 1, chunk, rows, weights, served, users)
        members = 4 if quad else 1
        slots = half // members
        count = slots * tiles
        power = ([(0, half * tiles), (1, half * tiles)], 1)
        sums = []
        for member in range(members):
            sums += [([(0, member * count), (1, member * count)], count), power]
        got_all = summed([kept, got[chunk]], sums)
        if quad:
            got_all = square(got_all)
        held = [got_all]
        left = [(0, member * (count + 1)) for member in range(members)]
        powers = [(0, member * (count + 1) + count) for member in range(members)]
        for bit in range(1, bits):
            if bit in quad:
                continue
            slots //= 2
            count = slots * tiles
            came = swap(summed(held, [(left, count), (powers, 1)]), bit)
            left = [(array, start + count) for array, start in left] + [(len(held), 0)]
            powers = powers + [(len(held), count)]
            held = held + [came]
        jobs.append((
            [(base + array, start) for array, start in left],
            [(base + array, start) for array, start in powers],
        ))
        base += len(held)
        lasts += held
    return finish(lasts, jobs, users, columns)


def solution(mesh):
    in_specs = (
        P(("parts", "ap"), None, None, None, None),
        P(None, ("parts", "ap"), None),
        P(("parts", "ap"), None),
        P("parts", None),
    )
    out_specs = P(("parts", "ap"), None, None)
    return jax.shard_map(
        on_device, mesh=mesh, in_specs=in_specs, out_specs=out_specs, check_vma=False
    )
```

```python
import functools

import jax
import jax.numpy as jnp
from jax import lax
from jax.experimental import pallas as pl
from jax.experimental.pallas import tpu as pltpu
from jax.sharding import PartitionSpec as P

epsilon = 1e-06
MIB = 1 << 20
CHUNKS = 2


def chip_orders(bits):
    first = list(range(1, bits))
    second = list(first)
    if bits > 2:
        second[0], second[1] = second[1], second[0]
    return first, second


def place_of(group, me, core, bits):
    away = [1 - (((group ^ me) >> bit) & 1) for bit in range(1, bits)]
    if bits > 2:
        swapped = core == 1
        away[:2] = [jnp.where(swapped, away[1], away[0]), jnp.where(swapped, away[0], away[1])]
    place = 0
    for value in away:
        place = place * 2 + value
    return place * 2 + (1 - ((group ^ core) & 1))


def write_products(slots, rows, weights, served, out):
    users = rows.shape[0] // slots
    antennas = rows.shape[1] // 2
    blocks, steps = weights.shape[1] // 128, users // 8
    group = min(slots, 16)
    for base in range(0, slots, group):
        plain = rows[base * users:(base + group) * users, :]
        turned = jnp.concatenate([-plain[:, antennas:], plain[:, :antennas]], axis=1)
        both = jnp.concatenate([plain, turned], axis=0)
        value = jnp.dot(both, weights, preferred_element_type=jnp.float32)
        value = jnp.where(served, value, 0.0)
        for half in range(2):
            for slot in range(group):
                top = (half * group + slot) * users
                for block in range(blocks):
                    piece = value[top:top + users, block * 128:(block + 1) * 128]
                    start = (((base + slot) * 2 + half) * blocks + block) * steps
                    out[start:start + steps] = piece.reshape(steps, 8, 128)


def power_tile(weights, served):
    wide = weights.astype(jnp.float32)
    power = jnp.sum(wide * wide, axis=0, keepdims=True)
    power = jnp.where(served, power, 0.0)
    blocks = power.shape[1] // 128
    pieces = [power[:, block * 128:(block + 1) * 128] for block in range(blocks)]
    return jnp.concatenate(pieces + [jnp.zeros((8 - blocks, 128), jnp.float32)], axis=0)


def first_kernel(
    bits, visible, cluster, channel, precoder,
    out, rows, weights, served,
    seen, names, raw, sems,
):
    me = lax.axis_index("ap")
    core = me & 1
    held, users, antennas = raw.shape[1], raw.shape[3], raw.shape[4]
    width = weights.shape[2]
    slots = 1 << bits
    mine = users // CHUNKS
    loads = [
        pltpu.make_async_copy(visible, seen, sems.at[0]),
        pltpu.make_async_copy(channel, raw, sems.at[1]),
    ]
    for keep in range(2):
        start = pl.multiple_of((core if keep else 1 - core) * width, width)
        at = pl.ds(start, width)
        loads.append(pltpu.make_async_copy(cluster.at[:, at], names.at[keep], sems.at[2 + 2 * keep]))
        loads.append(pltpu.make_async_copy(precoder.at[:, at], weights.at[keep], sems.at[3 + 2 * keep]))
    for load in loads:
        load.start()
    rows[...] = jnp.zeros_like(rows)
    loads[0].wait()
    loads[1].wait()
    for v in range(held):
        for keep in range(2):
            place = place_of(seen[0, v], me, core if keep else 1 - core, bits)
            at = pl.ds(pl.multiple_of(place * mine, mine), mine)
            for chunk in range(CHUNKS):
                part = slice(chunk * mine, (chunk + 1) * mine)
                rows[keep, chunk, at, 0:antennas] = raw[0, v, 0, part]
                rows[keep, chunk, at, antennas:2 * antennas] = raw[0, v, 1, part]
    for keep in range(2):
        loads[2 + 2 * keep].wait()
        here = (names[keep] == me).astype(jnp.float32)
        served[keep] = jnp.max(here, axis=0, keepdims=True)
    loads[3].wait()
    chosen, mask = weights[0], served[0] > 0.0
    write_products(slots, rows.at[0, 0], chosen, mask, out)
    out[out.shape[0] - 1] = power_tile(chosen, mask)
    loads[5].wait()


def next_kernel(bits, keep, chunk, rows, weights, served, out):
    chosen, mask = weights[keep], served[keep] > 0.0
    write_products(1 << bits, rows.at[keep, chunk], chosen, mask, out)
    if chunk == 0:
        out[out.shape[0] - 1] = power_tile(chosen, mask)


def message(tiles):
    return jax.ShapeDtypeStruct((tiles, 8, 128), jnp.float32)


def estimate(rows, weights):
    return pl.CostEstimate(
        flops=8 * rows[2] * rows[3] * weights[2],
        bytes_accessed=rows[2] * (rows[3] * 2 + weights[2] * 8) + weights[1] * weights[2] * 2,
        transcendentals=0,
    )


def first_products(bits, visible, cluster, channel, precoder):
    users, antennas = channel.shape[3], channel.shape[4]
    width = precoder.shape[1] // 2
    slots = 1 << bits
    tiles = (users // CHUNKS // 8) * (width // 128) * 2
    rows = (2, CHUNKS, slots * users // CHUNKS, 2 * antennas)
    weights = (2, precoder.shape[0], width)
    vmem = pl.BlockSpec(memory_space=pltpu.VMEM)
    hbm = pl.BlockSpec(memory_space=pltpu.HBM)
    operands = (visible, cluster, channel, precoder)
    return pl.pallas_call(
        functools.partial(first_kernel, bits),
        out_shape=(
            message(slots * tiles + 1),
            jax.ShapeDtypeStruct(rows, jnp.bfloat16),
            jax.ShapeDtypeStruct(weights, jnp.bfloat16),
            jax.ShapeDtypeStruct((2, 1, width), jnp.float32),
        ),
        in_specs=[hbm] * 4,
        out_specs=(vmem,) * 4,
        scratch_shapes=[
            pltpu.SMEM(visible.shape, jnp.int32),
            pltpu.VMEM((2, cluster.shape[0], width), jnp.int32),
            pltpu.VMEM(channel.shape, jnp.bfloat16),
            pltpu.SemaphoreType.DMA((6,)),
        ],
        compiler_params=pltpu.CompilerParams(vmem_limit_bytes=52 * MIB if slots > 16 else 24 * MIB),
        cost_estimate=estimate(rows, weights),
        name="first_products",
    )(*[pltpu.with_memory_space_constraint(operand, pltpu.HBM) for operand in operands])


def next_products(bits, keep, chunk, rows, weights, served):
    slots = 1 << bits
    users = rows.shape[2] // slots
    tiles = (users // 8) * (weights.shape[2] // 128) * 2
    vmem = pl.BlockSpec(memory_space=pltpu.VMEM)
    return pl.pallas_call(
        functools.partial(next_kernel, bits, keep, chunk),
        out_shape=message(slots * tiles + (chunk == 0)),
        in_specs=[vmem] * 3,
        out_specs=vmem,
        compiler_params=pltpu.CompilerParams(vmem_limit_bytes=48 * MIB if slots > 16 else 16 * MIB),
        cost_estimate=estimate(rows.shape, weights.shape),
        name="next_products",
    )(rows, weights, served)


def add_up(refs, terms, count):
    total = refs[terms[0][0]][terms[0][1]:terms[0][1] + count]
    for ref, start in terms[1:]:
        total = total + refs[ref][start:start + count]
    return total


def sum_kernel(jobs, *refs):
    at = 0
    for terms, count in jobs:
        refs[-1][at:at + count] = add_up(refs, terms, count)
        at += count


def summed(arrays, jobs):
    size = sum(count for _, count in jobs)
    vmem = pl.BlockSpec(memory_space=pltpu.VMEM)
    reads = sum(len(terms) * count for terms, count in jobs)
    return pl.pallas_call(
        functools.partial(sum_kernel, jobs),
        out_shape=message(size),
        in_specs=[vmem] * len(arrays),
        out_specs=vmem,
        compiler_params=pltpu.CompilerParams(vmem_limit_bytes=8 * MIB),
        cost_estimate=pl.CostEstimate(
            flops=reads * 1024, bytes_accessed=(reads + size) * 4096, transcendentals=0
        ),
        name="summed",
    )(*arrays)


def scaled_slot(refs, terms, powers, blocks, steps):
    scale = lax.rsqrt(add_up(refs, powers, 1)[0] + epsilon)
    total = add_up(refs, terms, 2 * blocks * steps)
    pieces = []
    for half in range(2):
        for block in range(blocks):
            start = (half * blocks + block) * steps
            factor = scale[block:block + 1, :].reshape(1, 1, 128)
            piece = total[start:start + steps]
            pieces.append(jnp.where(factor > 0.0, piece * factor, 0.0))
    return jnp.concatenate(pieces, axis=0)


def cross_kernel(jobs, powers, blocks, steps, *refs):
    tiles = 2 * blocks * steps
    for chunk, terms in enumerate(jobs):
        refs[-1][chunk * tiles:(chunk + 1) * tiles] = scaled_slot(refs, terms, powers, blocks, steps)


def final_kernel(jobs, powers, blocks, steps, *refs):
    crossed, out = refs[-2], refs[-1]
    core = lax.axis_index("ap") & 1
    tiles, users = 2 * blocks * steps, steps * 8
    for chunk, terms in enumerate(jobs):
        own = scaled_slot(refs, terms, powers, blocks, steps)
        other = crossed[chunk * tiles:(chunk + 1) * tiles]
        for side, value in ((core, own), (1 - core, other)):
            for half in range(2):
                for block in range(blocks):
                    start = (half * blocks + block) * steps
                    left = pl.multiple_of((side * blocks + block) * 128, 128)
                    piece = value[start:start + steps].reshape(users, 128)
                    out[chunk * users:(chunk + 1) * users, half, pl.ds(left, 128)] = piece


def finished(body, name, arrays, shape):
    vmem = pl.BlockSpec(memory_space=pltpu.VMEM)
    return pl.pallas_call(
        body,
        out_shape=shape,
        in_specs=[vmem] * len(arrays),
        out_specs=vmem,
        compiler_params=pltpu.CompilerParams(vmem_limit_bytes=8 * MIB),
        name=name,
    )(*arrays)


def on_device(channel, precoder, visible, cluster):
    devices = lax.axis_size("ap")
    bits = devices.bit_length() - 1
    users, columns = channel.shape[3], precoder.shape[2]
    steps, blocks = users // CHUNKS // 8, columns // 2 // 128
    tiles = 2 * blocks * steps
    orders = chip_orders(bits)
    flat = precoder.reshape(-1, columns)

    def swap(value, bit_of):
        return lax.ppermute(value, "ap", [(i, i ^ (1 << bit_of[i & 1])) for i in range(devices)])

    sent, rows, weights, served = first_products(bits, visible, cluster.T, channel, flat)
    got = [swap(sent, (0, 0))]
    for chunk in range(1, CHUNKS):
        got.append(swap(next_products(bits, 0, chunk, rows, weights, served), (0, 0)))
    held = [
        [next_products(bits, 1, chunk, rows, weights, served), got[chunk]] for chunk in range(CHUNKS)
    ]
    slots = devices
    left = [[(0, 0), (1, 0)] for _ in range(CHUNKS)]
    powers = [(0, slots * tiles), (1, slots * tiles)]
    for step in range(bits - 1):
        slots //= 2
        count = slots * tiles
        for chunk in range(CHUNKS):
            jobs = [(left[chunk], count)] + ([(powers, 1)] if chunk == 0 else [])
            came = swap(summed(held[chunk], jobs), (orders[0][step], orders[1][step]))
            left[chunk] = [(array, start + count) for array, start in left[chunk]]
            left[chunk].append((len(held[chunk]), 0))
            held[chunk].append(came)
        powers = powers + [(step + 2, count)]
    arrays = [array for mine in held for array in mine]
    other, own, base = [], [], 0
    for chunk in range(CHUNKS):
        other.append([(base + array, start) for array, start in left[chunk]])
        own.append([(base + array, start + tiles) for array, start in left[chunk]])
        base += len(held[chunk])
    cross = finished(
        functools.partial(cross_kernel, other, powers, blocks, steps),
        "cross", arrays, message(CHUNKS * tiles),
    )
    crossed = swap(cross, (0, 0))
    return finished(
        functools.partial(final_kernel, own, powers, blocks, steps),
        "finish", arrays + [crossed], jax.ShapeDtypeStruct((users, 2, columns), jnp.float32),
    )


def solution(mesh):
    in_specs = (
        P(("parts", "ap"), None, None, None, None),
        P(None, ("parts", "ap"), None),
        P(("parts", "ap"), None),
        P("parts", None),
    )
    out_specs = P(("parts", "ap"), None, None)
    return jax.shard_map(
        on_device, mesh=mesh, in_specs=in_specs, out_specs=out_specs, check_vma=False
    )
```

```python
import functools

import jax
import jax.numpy as jnp
from jax import lax
from jax.experimental import pallas as pl
from jax.experimental.pallas import tpu as pltpu
from jax.sharding import PartitionSpec as P

epsilon = 1e-06
MIB = 1 << 20
CHUNKS = 2


def chip_orders(bits):
    first = list(range(1, bits))
    second = list(first)
    if bits > 2:
        second[0], second[1] = second[1], second[0]
    return second, first


def place_of(group, me, core, bits):
    away = [1 - (((group ^ me) >> bit) & 1) for bit in range(1, bits)]
    if bits > 2:
        swapped = core == 0
        away[:2] = [jnp.where(swapped, away[1], away[0]), jnp.where(swapped, away[0], away[1])]
    place = 0
    for value in away:
        place = place * 2 + value
    return place * 2 + (1 - ((group ^ core) & 1))


def write_products(slots, rows, weights, served, out):
    users = rows.shape[0] // slots
    antennas = rows.shape[1] // 2
    blocks, steps = weights.shape[1] // 128, users // 8
    group = min(slots, 16)
    for base in range(0, slots, group):
        plain = rows[base * users:(base + group) * users, :]
        turned = jnp.concatenate([-plain[:, antennas:], plain[:, :antennas]], axis=1)
        both = jnp.concatenate([plain, turned], axis=0)
        value = jnp.dot(both, weights, preferred_element_type=jnp.float32)
        value = jnp.where(served, value, 0.0)
        for half in range(2):
            for slot in range(group):
                top = (half * group + slot) * users
                for block in range(blocks):
                    piece = value[top:top + users, block * 128:(block + 1) * 128]
                    start = (((base + slot) * 2 + half) * blocks + block) * steps
                    out[start:start + steps] = piece.reshape(steps, 8, 128)


def power_tile(weights, served):
    wide = weights.astype(jnp.float32)
    power = jnp.sum(wide * wide, axis=0, keepdims=True)
    power = jnp.where(served, power, 0.0)
    blocks = power.shape[1] // 128
    pieces = [power[:, block * 128:(block + 1) * 128] for block in range(blocks)]
    return jnp.concatenate(pieces + [jnp.zeros((8 - blocks, 128), jnp.float32)], axis=0)


def first_kernel(
    bits, visible, cluster, channel, precoder,
    out, rows, weights, served,
    seen, names, raw, sems,
):
    me = lax.axis_index("ap")
    core = me & 1
    held, users, antennas = raw.shape[1], raw.shape[3], raw.shape[4]
    width = weights.shape[2]
    slots = 1 << bits
    mine = users // CHUNKS
    loads = [
        pltpu.make_async_copy(visible, seen, sems.at[0]),
        pltpu.make_async_copy(channel, raw, sems.at[1]),
    ]
    for keep in range(2):
        start = pl.multiple_of((core if keep else 1 - core) * width, width)
        at = pl.ds(start, width)
        loads.append(pltpu.make_async_copy(cluster.at[:, at], names.at[keep], sems.at[2 + 2 * keep]))
        loads.append(pltpu.make_async_copy(precoder.at[:, at], weights.at[keep], sems.at[3 + 2 * keep]))
    for load in loads:
        load.start()
    rows[...] = jnp.zeros_like(rows)
    loads[0].wait()
    loads[1].wait()
    for v in range(held):
        for keep in range(2):
            place = place_of(seen[0, v], me, core if keep else 1 - core, bits)
            at = pl.ds(pl.multiple_of(place * mine, mine), mine)
            for chunk in range(CHUNKS):
                part = slice(chunk * mine, (chunk + 1) * mine)
                rows[keep, chunk, at, 0:antennas] = raw[0, v, 0, part]
                rows[keep, chunk, at, antennas:2 * antennas] = raw[0, v, 1, part]
    for keep in range(2):
        loads[2 + 2 * keep].wait()
        here = (names[keep] == me).astype(jnp.float32)
        served[keep] = jnp.max(here, axis=0, keepdims=True)
    loads[3].wait()
    chosen, mask = weights[0], served[0] > 0.0
    write_products(slots, rows.at[0, 0], chosen, mask, out)
    out[out.shape[0] - 1] = power_tile(chosen, mask)
    loads[5].wait()


def next_kernel(bits, keep, chunk, rows, weights, served, out):
    chosen, mask = weights[keep], served[keep] > 0.0
    write_products(1 << bits, rows.at[keep, chunk], chosen, mask, out)
    if chunk == 0:
        out[out.shape[0] - 1] = power_tile(chosen, mask)


def message(tiles):
    return jax.ShapeDtypeStruct((tiles, 8, 128), jnp.float32)


def estimate(rows, weights):
    return pl.CostEstimate(
        flops=8 * rows[2] * rows[3] * weights[2],
        bytes_accessed=rows[2] * (rows[3] * 2 + weights[2] * 8) + weights[1] * weights[2] * 2,
        transcendentals=0,
    )


def first_products(bits, visible, cluster, channel, precoder):
    users, antennas = channel.shape[3], channel.shape[4]
    width = precoder.shape[1] // 2
    slots = 1 << bits
    tiles = (users // CHUNKS // 8) * (width // 128) * 2
    rows = (2, CHUNKS, slots * users // CHUNKS, 2 * antennas)
    weights = (2, precoder.shape[0], width)
    vmem = pl.BlockSpec(memory_space=pltpu.VMEM)
    hbm = pl.BlockSpec(memory_space=pltpu.HBM)
    operands = (visible, cluster, channel, precoder)
    return pl.pallas_call(
        functools.partial(first_kernel, bits),
        out_shape=(
            message(slots * tiles + 1),
            jax.ShapeDtypeStruct(rows, jnp.bfloat16),
            jax.ShapeDtypeStruct(weights, jnp.bfloat16),
            jax.ShapeDtypeStruct((2, 1, width), jnp.float32),
        ),
        in_specs=[hbm] * 4,
        out_specs=(vmem,) * 4,
        scratch_shapes=[
            pltpu.SMEM(visible.shape, jnp.int32),
            pltpu.VMEM((2, cluster.shape[0], width), jnp.int32),
            pltpu.VMEM(channel.shape, jnp.bfloat16),
            pltpu.SemaphoreType.DMA((6,)),
        ],
        compiler_params=pltpu.CompilerParams(vmem_limit_bytes=52 * MIB if slots > 16 else 24 * MIB),
        cost_estimate=estimate(rows, weights),
        name="first_products",
    )(*[pltpu.with_memory_space_constraint(operand, pltpu.HBM) for operand in operands])


def next_products(bits, keep, chunk, rows, weights, served):
    slots = 1 << bits
    users = rows.shape[2] // slots
    tiles = (users // 8) * (weights.shape[2] // 128) * 2
    vmem = pl.BlockSpec(memory_space=pltpu.VMEM)
    return pl.pallas_call(
        functools.partial(next_kernel, bits, keep, chunk),
        out_shape=message(slots * tiles + (chunk == 0)),
        in_specs=[vmem] * 3,
        out_specs=vmem,
        compiler_params=pltpu.CompilerParams(vmem_limit_bytes=48 * MIB if slots > 16 else 16 * MIB),
        cost_estimate=estimate(rows.shape, weights.shape),
        name="next_products",
    )(rows, weights, served)


def add_up(refs, terms, count):
    total = refs[terms[0][0]][terms[0][1]:terms[0][1] + count]
    for ref, start in terms[1:]:
        total = total + refs[ref][start:start + count]
    return total


def sum_kernel(jobs, *refs):
    at = 0
    for terms, count in jobs:
        refs[-1][at:at + count] = add_up(refs, terms, count)
        at += count


def summed(arrays, jobs):
    size = sum(count for _, count in jobs)
    vmem = pl.BlockSpec(memory_space=pltpu.VMEM)
    reads = sum(len(terms) * count for terms, count in jobs)
    return pl.pallas_call(
        functools.partial(sum_kernel, jobs),
        out_shape=message(size),
        in_specs=[vmem] * len(arrays),
        out_specs=vmem,
        compiler_params=pltpu.CompilerParams(vmem_limit_bytes=8 * MIB),
        cost_estimate=pl.CostEstimate(
            flops=reads * 1024, bytes_accessed=(reads + size) * 4096, transcendentals=0
        ),
        name="summed",
    )(*arrays)


def scaled_slot(refs, terms, powers, blocks, steps):
    scale = lax.rsqrt(add_up(refs, powers, 1)[0] + epsilon)
    total = add_up(refs, terms, 2 * blocks * steps)
    pieces = []
    for half in range(2):
        for block in range(blocks):
            start = (half * blocks + block) * steps
            factor = scale[block:block + 1, :].reshape(1, 1, 128)
            piece = total[start:start + steps]
            pieces.append(jnp.where(factor > 0.0, piece * factor, 0.0))
    return jnp.concatenate(pieces, axis=0)


def cross_kernel(jobs, powers, blocks, steps, *refs):
    tiles = 2 * blocks * steps
    for chunk, terms in enumerate(jobs):
        refs[-1][chunk * tiles:(chunk + 1) * tiles] = scaled_slot(refs, terms, powers, blocks, steps)


def final_kernel(jobs, powers, blocks, steps, *refs):
    crossed, out = refs[-2], refs[-1]
    core = lax.axis_index("ap") & 1
    tiles, users = 2 * blocks * steps, steps * 8
    for chunk, terms in enumerate(jobs):
        own = scaled_slot(refs, terms, powers, blocks, steps)
        other = crossed[chunk * tiles:(chunk + 1) * tiles]
        for side, value in ((core, own), (1 - core, other)):
            for half in range(2):
                for block in range(blocks):
                    start = (half * blocks + block) * steps
                    left = pl.multiple_of((side * blocks + block) * 128, 128)
                    piece = value[start:start + steps].reshape(users, 128)
                    out[chunk * users:(chunk + 1) * users, half, pl.ds(left, 128)] = piece


def finished(body, name, arrays, shape):
    vmem = pl.BlockSpec(memory_space=pltpu.VMEM)
    return pl.pallas_call(
        body,
        out_shape=shape,
        in_specs=[vmem] * len(arrays),
        out_specs=vmem,
        compiler_params=pltpu.CompilerParams(vmem_limit_bytes=8 * MIB),
        name=name,
    )(*arrays)


def on_device(channel, precoder, visible, cluster):
    devices = lax.axis_size("ap")
    bits = devices.bit_length() - 1
    users, columns = channel.shape[3], precoder.shape[2]
    steps, blocks = users // CHUNKS // 8, columns // 2 // 128
    tiles = 2 * blocks * steps
    orders = chip_orders(bits)
    flat = precoder.reshape(-1, columns)

    def swap(value, bit_of):
        return lax.ppermute(value, "ap", [(i, i ^ (1 << bit_of[i & 1])) for i in range(devices)])

    sent, rows, weights, served = first_products(bits, visible, cluster.T, channel, flat)
    got = [swap(sent, (0, 0))]
    for chunk in range(1, CHUNKS):
        got.append(swap(next_products(bits, 0, chunk, rows, weights, served), (0, 0)))
    held = [
        [next_products(bits, 1, chunk, rows, weights, served), got[chunk]] for chunk in range(CHUNKS)
    ]
    slots = devices
    left = [[(0, 0), (1, 0)] for _ in range(CHUNKS)]
    powers = [(0, slots * tiles), (1, slots * tiles)]
    for step in range(bits - 1):
        slots //= 2
        count = slots * tiles
        for chunk in range(CHUNKS):
            jobs = [(left[chunk], count)] + ([(powers, 1)] if chunk == 0 else [])
            came = swap(summed(held[chunk], jobs), (orders[0][step], orders[1][step]))
            left[chunk] = [(array, start + count) for array, start in left[chunk]]
            left[chunk].append((len(held[chunk]), 0))
            held[chunk].append(came)
        powers = powers + [(step + 2, count)]
    arrays = [array for mine in held for array in mine]
    other, own, base = [], [], 0
    for chunk in range(CHUNKS):
        other.append([(base + array, start) for array, start in left[chunk]])
        own.append([(base + array, start + tiles) for array, start in left[chunk]])
        base += len(held[chunk])
    cross = finished(
        functools.partial(cross_kernel, other, powers, blocks, steps),
        "cross", arrays, message(CHUNKS * tiles),
    )
    crossed = swap(cross, (0, 0))
    return finished(
        functools.partial(final_kernel, own, powers, blocks, steps),
        "finish", arrays + [crossed], jax.ShapeDtypeStruct((users, 2, columns), jnp.float32),
    )


def solution(mesh):
    in_specs = (
        P(("parts", "ap"), None, None, None, None),
        P(None, ("parts", "ap"), None),
        P(("parts", "ap"), None),
        P("parts", None),
    )
    out_specs = P(("parts", "ap"), None, None)
    return jax.shard_map(
        on_device, mesh=mesh, in_specs=in_specs, out_specs=out_specs, check_vma=False
    )
```

```python
import functools

import jax
import jax.numpy as jnp
from jax import lax
from jax.experimental import pallas as pl
from jax.experimental.pallas import tpu as pltpu
from jax.sharding import PartitionSpec as P

epsilon = 1e-06
MIB = 1 << 20
CHUNKS = 2


def chip_orders(bits):
    first = list(range(1, bits))
    second = list(first)
    if bits > 2:
        second[0], second[1] = second[1], second[0]
    return second, first


def place_of(group, me, core, chunk, bits):
    away = [1 - (((group ^ me) >> bit) & 1) for bit in range(1, bits)]
    if bits > 2:
        swapped = core == chunk % 2
        away[:2] = [jnp.where(swapped, away[1], away[0]), jnp.where(swapped, away[0], away[1])]
    place = 0
    for value in away:
        place = place * 2 + value
    return place * 2 + (1 - ((group ^ core) & 1))


def write_products(slots, rows, weights, served, out):
    users = rows.shape[0] // slots
    antennas = rows.shape[1] // 2
    blocks, steps = weights.shape[1] // 128, users // 8
    group = min(slots, 16)
    for base in range(0, slots, group):
        plain = rows[base * users:(base + group) * users, :]
        turned = jnp.concatenate([-plain[:, antennas:], plain[:, :antennas]], axis=1)
        both = jnp.concatenate([plain, turned], axis=0)
        value = jnp.dot(both, weights, preferred_element_type=jnp.float32)
        value = jnp.where(served, value, 0.0)
        for half in range(2):
            for slot in range(group):
                top = (half * group + slot) * users
                for block in range(blocks):
                    piece = value[top:top + users, block * 128:(block + 1) * 128]
                    start = (((base + slot) * 2 + half) * blocks + block) * steps
                    out[start:start + steps] = piece.reshape(steps, 8, 128)


def power_tile(weights, served):
    wide = weights.astype(jnp.float32)
    power = jnp.sum(wide * wide, axis=0, keepdims=True)
    power = jnp.where(served, power, 0.0)
    blocks = power.shape[1] // 128
    pieces = [power[:, block * 128:(block + 1) * 128] for block in range(blocks)]
    return jnp.concatenate(pieces + [jnp.zeros((8 - blocks, 128), jnp.float32)], axis=0)


def first_kernel(
    bits, visible, cluster, channel, precoder,
    out, rows, weights, served,
    seen, names, raw, sems,
):
    me = lax.axis_index("ap")
    core = me & 1
    held, users, antennas = raw.shape[1], raw.shape[3], raw.shape[4]
    width = weights.shape[2]
    slots = 1 << bits
    mine = users // CHUNKS
    loads = [
        pltpu.make_async_copy(visible, seen, sems.at[0]),
        pltpu.make_async_copy(channel, raw, sems.at[1]),
    ]
    for keep in range(2):
        start = pl.multiple_of((core if keep else 1 - core) * width, width)
        at = pl.ds(start, width)
        loads.append(pltpu.make_async_copy(cluster.at[:, at], names.at[keep], sems.at[2 + 2 * keep]))
        loads.append(pltpu.make_async_copy(precoder.at[:, at], weights.at[keep], sems.at[3 + 2 * keep]))
    for load in loads:
        load.start()
    rows[...] = jnp.zeros_like(rows)
    loads[0].wait()
    loads[1].wait()
    for v in range(held):
        for keep in range(2):
            for chunk in range(CHUNKS):
                place = place_of(seen[0, v], me, core if keep else 1 - core, chunk, bits)
                at = pl.ds(pl.multiple_of(place * mine, mine), mine)
                part = slice(chunk * mine, (chunk + 1) * mine)
                rows[keep, chunk, at, 0:antennas] = raw[0, v, 0, part]
                rows[keep, chunk, at, antennas:2 * antennas] = raw[0, v, 1, part]
    for keep in range(2):
        loads[2 + 2 * keep].wait()
        here = (names[keep] == me).astype(jnp.float32)
        served[keep] = jnp.max(here, axis=0, keepdims=True)
    loads[3].wait()
    chosen, mask = weights[0], served[0] > 0.0
    write_products(slots, rows.at[0, 0], chosen, mask, out)
    out[out.shape[0] - 1] = power_tile(chosen, mask)
    loads[5].wait()


def next_kernel(bits, keep, chunk, rows, weights, served, out):
    chosen, mask = weights[keep], served[keep] > 0.0
    write_products(1 << bits, rows.at[keep, chunk], chosen, mask, out)
    if chunk == 0:
        out[out.shape[0] - 1] = power_tile(chosen, mask)


def message(tiles):
    return jax.ShapeDtypeStruct((tiles, 8, 128), jnp.float32)


def estimate(rows, weights):
    return pl.CostEstimate(
        flops=8 * rows[2] * rows[3] * weights[2],
        bytes_accessed=rows[2] * (rows[3] * 2 + weights[2] * 8) + weights[1] * weights[2] * 2,
        transcendentals=0,
    )


def first_products(bits, visible, cluster, channel, precoder):
    users, antennas = channel.shape[3], channel.shape[4]
    width = precoder.shape[1] // 2
    slots = 1 << bits
    tiles = (users // CHUNKS // 8) * (width // 128) * 2
    rows = (2, CHUNKS, slots * users // CHUNKS, 2 * antennas)
    weights = (2, precoder.shape[0], width)
    vmem = pl.BlockSpec(memory_space=pltpu.VMEM)
    hbm = pl.BlockSpec(memory_space=pltpu.HBM)
    operands = (visible, cluster, channel, precoder)
    return pl.pallas_call(
        functools.partial(first_kernel, bits),
        out_shape=(
            message(slots * tiles + 1),
            jax.ShapeDtypeStruct(rows, jnp.bfloat16),
            jax.ShapeDtypeStruct(weights, jnp.bfloat16),
            jax.ShapeDtypeStruct((2, 1, width), jnp.float32),
        ),
        in_specs=[hbm] * 4,
        out_specs=(vmem,) * 4,
        scratch_shapes=[
            pltpu.SMEM(visible.shape, jnp.int32),
            pltpu.VMEM((2, cluster.shape[0], width), jnp.int32),
            pltpu.VMEM(channel.shape, jnp.bfloat16),
            pltpu.SemaphoreType.DMA((6,)),
        ],
        compiler_params=pltpu.CompilerParams(vmem_limit_bytes=52 * MIB if slots > 16 else 24 * MIB),
        cost_estimate=estimate(rows, weights),
        name="first_products",
    )(*[pltpu.with_memory_space_constraint(operand, pltpu.HBM) for operand in operands])


def next_products(bits, keep, chunk, rows, weights, served):
    slots = 1 << bits
    users = rows.shape[2] // slots
    tiles = (users // 8) * (weights.shape[2] // 128) * 2
    vmem = pl.BlockSpec(memory_space=pltpu.VMEM)
    return pl.pallas_call(
        functools.partial(next_kernel, bits, keep, chunk),
        out_shape=message(slots * tiles + (chunk == 0)),
        in_specs=[vmem] * 3,
        out_specs=vmem,
        compiler_params=pltpu.CompilerParams(vmem_limit_bytes=48 * MIB if slots > 16 else 16 * MIB),
        cost_estimate=estimate(rows.shape, weights.shape),
        name="next_products",
    )(rows, weights, served)


def add_up(refs, terms, count):
    total = refs[terms[0][0]][terms[0][1]:terms[0][1] + count]
    for ref, start in terms[1:]:
        total = total + refs[ref][start:start + count]
    return total


def sum_kernel(jobs, *refs):
    at = 0
    for terms, count in jobs:
        refs[-1][at:at + count] = add_up(refs, terms, count)
        at += count


def summed(arrays, jobs):
    size = sum(count for _, count in jobs)
    vmem = pl.BlockSpec(memory_space=pltpu.VMEM)
    reads = sum(len(terms) * count for terms, count in jobs)
    return pl.pallas_call(
        functools.partial(sum_kernel, jobs),
        out_shape=message(size),
        in_specs=[vmem] * len(arrays),
        out_specs=vmem,
        compiler_params=pltpu.CompilerParams(vmem_limit_bytes=8 * MIB),
        cost_estimate=pl.CostEstimate(
            flops=reads * 1024, bytes_accessed=(reads + size) * 4096, transcendentals=0
        ),
        name="summed",
    )(*arrays)


def scaled_slot(refs, terms, powers, blocks, steps):
    scale = lax.rsqrt(add_up(refs, powers, 1)[0] + epsilon)
    total = add_up(refs, terms, 2 * blocks * steps)
    pieces = []
    for half in range(2):
        for block in range(blocks):
            start = (half * blocks + block) * steps
            factor = scale[block:block + 1, :].reshape(1, 1, 128)
            piece = total[start:start + steps]
            pieces.append(jnp.where(factor > 0.0, piece * factor, 0.0))
    return jnp.concatenate(pieces, axis=0)


def cross_kernel(jobs, powers, blocks, steps, *refs):
    tiles = 2 * blocks * steps
    for chunk, terms in enumerate(jobs):
        refs[-1][chunk * tiles:(chunk + 1) * tiles] = scaled_slot(refs, terms, powers, blocks, steps)


def final_kernel(jobs, powers, blocks, steps, *refs):
    crossed, out = refs[-2], refs[-1]
    core = lax.axis_index("ap") & 1
    tiles, users = 2 * blocks * steps, steps * 8
    for chunk, terms in enumerate(jobs):
        own = scaled_slot(refs, terms, powers, blocks, steps)
        other = crossed[chunk * tiles:(chunk + 1) * tiles]
        for side, value in ((core, own), (1 - core, other)):
            for half in range(2):
                for block in range(blocks):
                    start = (half * blocks + block) * steps
                    left = pl.multiple_of((side * blocks + block) * 128, 128)
                    piece = value[start:start + steps].reshape(users, 128)
                    out[chunk * users:(chunk + 1) * users, half, pl.ds(left, 128)] = piece


def finished(body, name, arrays, shape):
    vmem = pl.BlockSpec(memory_space=pltpu.VMEM)
    return pl.pallas_call(
        body,
        out_shape=shape,
        in_specs=[vmem] * len(arrays),
        out_specs=vmem,
        compiler_params=pltpu.CompilerParams(vmem_limit_bytes=8 * MIB),
        name=name,
    )(*arrays)


def on_device(channel, precoder, visible, cluster):
    devices = lax.axis_size("ap")
    bits = devices.bit_length() - 1
    users, columns = channel.shape[3], precoder.shape[2]
    steps, blocks = users // CHUNKS // 8, columns // 2 // 128
    tiles = 2 * blocks * steps
    orders = chip_orders(bits)
    flat = precoder.reshape(-1, columns)

    def swap(value, bit_of):
        return lax.ppermute(value, "ap", [(i, i ^ (1 << bit_of[i & 1])) for i in range(devices)])

    sent, rows, weights, served = first_products(bits, visible, cluster.T, channel, flat)
    got = [swap(sent, (0, 0))]
    for chunk in range(1, CHUNKS):
        got.append(swap(next_products(bits, 0, chunk, rows, weights, served), (0, 0)))
    held = [
        [next_products(bits, 1, chunk, rows, weights, served), got[chunk]] for chunk in range(CHUNKS)
    ]
    slots = devices
    left = [[(0, 0), (1, 0)] for _ in range(CHUNKS)]
    powers = [(0, slots * tiles), (1, slots * tiles)]
    for step in range(bits - 1):
        slots //= 2
        count = slots * tiles
        for chunk in range(CHUNKS):
            jobs = [(left[chunk], count)] + ([(powers, 1)] if chunk == 0 else [])
            came = swap(summed(held[chunk], jobs), (orders[chunk % 2][step], orders[1 - chunk % 2][step]))
            left[chunk] = [(array, start + count) for array, start in left[chunk]]
            left[chunk].append((len(held[chunk]), 0))
            held[chunk].append(came)
        powers = powers + [(step + 2, count)]
    arrays = [array for mine in held for array in mine]
    other, own, base = [], [], 0
    for chunk in range(CHUNKS):
        other.append([(base + array, start) for array, start in left[chunk]])
        own.append([(base + array, start + tiles) for array, start in left[chunk]])
        base += len(held[chunk])
    cross = finished(
        functools.partial(cross_kernel, other, powers, blocks, steps),
        "cross", arrays, message(CHUNKS * tiles),
    )
    crossed = swap(cross, (0, 0))
    return finished(
        functools.partial(final_kernel, own, powers, blocks, steps),
        "finish", arrays + [crossed], jax.ShapeDtypeStruct((users, 2, columns), jnp.float32),
    )


def solution(mesh):
    in_specs = (
        P(("parts", "ap"), None, None, None, None),
        P(None, ("parts", "ap"), None),
        P(("parts", "ap"), None),
        P("parts", None),
    )
    out_specs = P(("parts", "ap"), None, None)
    return jax.shard_map(
        on_device, mesh=mesh, in_specs=in_specs, out_specs=out_specs, check_vma=False
    )
```

```python
import functools

import jax
import jax.numpy as jnp
from jax import lax
from jax.experimental import pallas as pl
from jax.experimental.pallas import tpu as pltpu
from jax.sharding import PartitionSpec as P

epsilon = 1e-06
MIB = 1 << 20


def chip_orders(bits):
    first = list(range(1, bits))
    second = list(first)
    if bits > 2:
        second[0], second[1] = second[1], second[0]
    return second, first


def place_of(group, me, core, bits):
    away = [1 - (((group ^ me) >> bit) & 1) for bit in range(1, bits)]
    if bits > 2:
        swapped = core == 0
        away[:2] = [jnp.where(swapped, away[1], away[0]), jnp.where(swapped, away[0], away[1])]
    place = 0
    for value in away:
        place = place * 2 + value
    return place * 2 + (1 - ((group ^ core) & 1))


def other_place(place, bits):
    away = [(place >> at) & 1 for at in reversed(range(bits))]
    if bits > 2:
        away[0], away[1] = away[1], away[0]
    away[-1] = 1 - away[-1]
    out = 0
    for value in away:
        out = out * 2 + value
    return out


def late_steps(users):
    return max(users // 32, 1)


def write_products(slots, rows, weights, served, out, put_late):
    users = rows.shape[0] // slots
    antennas = rows.shape[1] // 2
    blocks, steps = weights.shape[1] // 128, users // 8
    early = steps - late_steps(users)
    group = min(slots, 16)
    for base in range(0, slots, group):
        plain = rows[base * users:(base + group) * users, :]
        turned = jnp.concatenate([-plain[:, antennas:], plain[:, :antennas]], axis=1)
        both = jnp.concatenate([plain, turned], axis=0)
        value = jnp.dot(both, weights, preferred_element_type=jnp.float32)
        value = jnp.where(served, value, 0.0)
        for half in range(2):
            for slot in range(group):
                top = (half * group + slot) * users
                for block in range(blocks):
                    piece = value[top:top + users, block * 128:(block + 1) * 128]
                    piece = piece.reshape(steps, 8, 128)
                    start = (((base + slot) * 2 + half) * blocks + block) * early
                    out[start:start + early] = piece[:early]
                    put_late(base + slot, half * blocks + block, piece[early:])


def power_tile(weights, served):
    wide = weights.astype(jnp.float32)
    power = jnp.sum(wide * wide, axis=0, keepdims=True)
    power = jnp.where(served, power, 0.0)
    blocks = power.shape[1] // 128
    pieces = [power[:, block * 128:(block + 1) * 128] for block in range(blocks)]
    return jnp.concatenate(pieces + [jnp.zeros((8 - blocks, 128), jnp.float32)], axis=0)


def first_kernel(
    bits, visible, cluster, channel, precoder,
    out, late, rows, weights, served,
    seen, names, raw, sems,
):
    me = lax.axis_index("ap")
    core = me & 1
    held, users, antennas = raw.shape[1], raw.shape[3], raw.shape[4]
    width = weights.shape[2]
    slots = 1 << bits
    loads = [
        pltpu.make_async_copy(visible, seen, sems.at[0]),
        pltpu.make_async_copy(channel, raw, sems.at[1]),
    ]
    for keep in range(2):
        start = pl.multiple_of((core if keep else 1 - core) * width, width)
        at = pl.ds(start, width)
        loads.append(pltpu.make_async_copy(cluster.at[:, at], names.at[keep], sems.at[2 + 2 * keep]))
        loads.append(pltpu.make_async_copy(precoder.at[:, at], weights.at[keep], sems.at[3 + 2 * keep]))
    for load in loads:
        load.start()
    rows[...] = jnp.zeros_like(rows)
    loads[0].wait()
    loads[1].wait()
    for v in range(held):
        for keep in range(2):
            place = place_of(seen[0, v], me, core if keep else 1 - core, bits)
            at = pl.ds(pl.multiple_of(place * users, users), users)
            rows[keep, at, 0:antennas] = raw[0, v, 0]
            rows[keep, at, antennas:2 * antennas] = raw[0, v, 1]
    for keep in range(2):
        loads[2 + 2 * keep].wait()
        here = (names[keep] == me).astype(jnp.float32)
        served[keep] = jnp.max(here, axis=0, keepdims=True)
    loads[3].wait()
    chosen, mask = weights[0], served[0] > 0.0
    count = late.shape[0] // slots

    def put_late(place, block, piece):
        start = place * count + block * piece.shape[0]
        late[start:start + piece.shape[0]] = piece

    write_products(slots, rows.at[0], chosen, mask, out, put_late)
    out[out.shape[0] - 1] = power_tile(chosen, mask)
    loads[5].wait()


def next_kernel(bits, sent, early, rows, weights, served, out, late):
    core = lax.axis_index("ap") & 1
    slots = 1 << bits
    chosen, mask = weights[1], served[1] > 0.0
    count = early.shape[0] // slots

    def put_late(place, block, piece):
        size = piece.shape[0]
        turned = jnp.where(core == 0, other_place(place, bits), place)
        start = turned * (2 * count) + core * count + block * size
        late[pl.ds(start, size)] = piece

    write_products(slots, rows.at[1], chosen, mask, out, put_late)
    for place in range(slots):
        turned = jnp.where(core == 1, other_place(place, bits), place)
        start = turned * (2 * count) + (1 - core) * count
        late[pl.ds(start, count)] = early[place * count:(place + 1) * count]
    own = power_tile(chosen, mask)
    out[out.shape[0] - 1] = own
    late[late.shape[0] - 1] = jnp.where(core == 0, own, sent[sent.shape[0] - 1])


def message(tiles):
    return jax.ShapeDtypeStruct((tiles, 8, 128), jnp.float32)


def estimate(rows, weights):
    return pl.CostEstimate(
        flops=8 * rows[1] * rows[2] * weights[2],
        bytes_accessed=rows[1] * (rows[2] * 2 + weights[2] * 8) + weights[1] * weights[2] * 2,
        transcendentals=0,
    )


def first_products(bits, visible, cluster, channel, precoder):
    users, antennas = channel.shape[3], channel.shape[4]
    width = precoder.shape[1] // 2
    slots = 1 << bits
    late = late_steps(users) * (width // 128) * 2
    early = (users // 8) * (width // 128) * 2 - late
    rows = (2, slots * users, 2 * antennas)
    weights = (2, precoder.shape[0], width)
    vmem = pl.BlockSpec(memory_space=pltpu.VMEM)
    hbm = pl.BlockSpec(memory_space=pltpu.HBM)
    operands = (visible, cluster, channel, precoder)
    return pl.pallas_call(
        functools.partial(first_kernel, bits),
        out_shape=(
            message(slots * early + 1),
            message(slots * late),
            jax.ShapeDtypeStruct(rows, jnp.bfloat16),
            jax.ShapeDtypeStruct(weights, jnp.bfloat16),
            jax.ShapeDtypeStruct((2, 1, width), jnp.float32),
        ),
        in_specs=[hbm] * 4,
        out_specs=(vmem,) * 5,
        scratch_shapes=[
            pltpu.SMEM(visible.shape, jnp.int32),
            pltpu.VMEM((2, cluster.shape[0], width), jnp.int32),
            pltpu.VMEM(channel.shape, jnp.bfloat16),
            pltpu.SemaphoreType.DMA((6,)),
        ],
        compiler_params=pltpu.CompilerParams(vmem_limit_bytes=52 * MIB if slots > 16 else 24 * MIB),
        cost_estimate=estimate(rows, weights),
        name="first_products",
    )(*[pltpu.with_memory_space_constraint(operand, pltpu.HBM) for operand in operands])


def next_products(bits, sent, early, rows, weights, served):
    slots = 1 << bits
    vmem = pl.BlockSpec(memory_space=pltpu.VMEM)
    return pl.pallas_call(
        functools.partial(next_kernel, bits),
        out_shape=(message(sent.shape[0]), message(2 * early.shape[0] + 1)),
        in_specs=[vmem] * 5,
        out_specs=(vmem, vmem),
        compiler_params=pltpu.CompilerParams(vmem_limit_bytes=52 * MIB if slots > 16 else 16 * MIB),
        cost_estimate=estimate(rows.shape, weights.shape),
        name="next_products",
    )(sent, early, rows, weights, served)


def add_up(refs, terms, count):
    total = refs[terms[0][0]][terms[0][1]:terms[0][1] + count]
    for ref, start in terms[1:]:
        total = total + refs[ref][start:start + count]
    return total


def sum_kernel(jobs, *refs):
    at = 0
    for terms, count in jobs:
        refs[-1][at:at + count] = add_up(refs, terms, count)
        at += count


def summed(arrays, jobs):
    size = sum(count for _, count in jobs)
    vmem = pl.BlockSpec(memory_space=pltpu.VMEM)
    reads = sum(len(terms) * count for terms, count in jobs)
    return pl.pallas_call(
        functools.partial(sum_kernel, jobs),
        out_shape=message(size),
        in_specs=[vmem] * len(arrays),
        out_specs=vmem,
        compiler_params=pltpu.CompilerParams(vmem_limit_bytes=8 * MIB),
        cost_estimate=pl.CostEstimate(
            flops=reads * 1024, bytes_accessed=(reads + size) * 4096, transcendentals=0
        ),
        name="summed",
    )(*arrays)


def scaled_slot(refs, terms, scales, blocks, steps):
    total = add_up(refs, terms, 2 * len(scales) * blocks * steps)
    pieces = []
    for side, scale in enumerate(scales):
        for half in range(2):
            for block in range(blocks):
                start = ((side * 2 + half) * blocks + block) * steps
                factor = scale[block:block + 1, :].reshape(1, 1, 128)
                piece = total[start:start + steps]
                pieces.append(jnp.where(factor > 0.0, piece * factor, 0.0))
    return jnp.concatenate(pieces, axis=0)


def column_scale(refs, powers):
    return lax.rsqrt(add_up(refs, powers, 1)[0] + epsilon)


def both_slots(plan, blocks, steps, refs):
    (early, early_powers), (late, late_powers) = plan
    own, first = column_scale(refs, early_powers), column_scale(refs, late_powers)
    return (
        scaled_slot(refs, early, [own], blocks, steps[0]),
        scaled_slot(refs, late, [first, own], blocks, steps[1]),
    )


def cross_kernel(plan, blocks, steps, *refs):
    early, late = both_slots(plan, blocks, steps, refs)
    refs[-1][:early.shape[0]] = early
    refs[-1][early.shape[0]:] = late


def final_kernel(plan, blocks, steps, *refs):
    crossed, out = refs[-2], refs[-1]
    core = lax.axis_index("ap") & 1
    early, late = both_slots(plan, blocks, steps, refs)
    size = early.shape[0]
    late = jnp.where(core == 1, late, crossed[size:size + late.shape[0]])
    middle = steps[0] * 8

    def put(value, side, first, rows):
        count = rows // 8
        for half in range(2):
            for block in range(blocks):
                start = (half * blocks + block) * count
                left = pl.multiple_of((side * blocks + block) * 128, 128)
                piece = value[start:start + count].reshape(rows, 128)
                out[first:first + rows, half, pl.ds(left, 128)] = piece

    put(early, core, 0, middle)
    put(crossed[:size], 1 - core, 0, middle)
    for side in range(2):
        count = late.shape[0] // 2
        put(late[side * count:(side + 1) * count], side, middle, steps[1] * 8)


def finished(body, name, arrays, shape):
    vmem = pl.BlockSpec(memory_space=pltpu.VMEM)
    return pl.pallas_call(
        body,
        out_shape=shape,
        in_specs=[vmem] * len(arrays),
        out_specs=vmem,
        compiler_params=pltpu.CompilerParams(vmem_limit_bytes=8 * MIB),
        name=name,
    )(*arrays)


def on_device(channel, precoder, visible, cluster):
    devices = lax.axis_size("ap")
    bits = devices.bit_length() - 1
    users, columns = channel.shape[3], precoder.shape[2]
    blocks = columns // 2 // 128
    steps = (users // 8 - late_steps(users), late_steps(users))
    tiles = (2 * blocks * steps[0], 4 * blocks * steps[1])
    orders = chip_orders(bits)
    flat = precoder.reshape(-1, columns)

    def swap(value, bit_of, cores=(0, 1)):
        pairs = [(i, i ^ (1 << bit_of[i & 1])) for i in range(devices) if i & 1 in cores]
        return lax.ppermute(value, "ap", pairs)

    sent, early, rows, weights, served = first_products(bits, visible, cluster.T, channel, flat)
    got = swap(sent, (0, 0))
    kept, late = next_products(bits, sent, early, rows, weights, served)
    held = [[kept, got], [late, swap(late, (0, 0), (0,))]]
    slots = devices
    left = [[(0, 0), (1, 0)] for _ in range(2)]
    powers = [[(0, slots * count), (1, slots * count)] for count in tiles]
    for step in range(bits - 1):
        slots //= 2
        for chunk in range(2):
            count = slots * tiles[chunk]
            jobs = [(left[chunk], count), (powers[chunk], 1)]
            came = swap(
                summed(held[chunk], jobs), (orders[0][step], orders[1][step]), (0, 1)[chunk:]
            )
            left[chunk] = [(array, start + count) for array, start in left[chunk]]
            left[chunk].append((len(held[chunk]), 0))
            powers[chunk] = powers[chunk] + [(len(held[chunk]), count)]
            held[chunk].append(came)
    arrays = held[0] + held[1]
    other, own, base = [], [], 0
    for chunk in range(2):
        here = [(base + array, start) for array, start in powers[chunk]]
        other.append(([(base + array, start) for array, start in left[chunk]], here))
        own.append(([(base + array, start + tiles[chunk]) for array, start in left[chunk]], here))
        base += len(held[chunk])
    cross = finished(
        functools.partial(cross_kernel, other, blocks, steps),
        "cross", arrays, message(tiles[0] + tiles[1]),
    )
    crossed = swap(cross, (0, 0))
    return finished(
        functools.partial(final_kernel, own, blocks, steps),
        "finish", arrays + [crossed], jax.ShapeDtypeStruct((users, 2, columns), jnp.float32),
    )


def solution(mesh):
    in_specs = (
        P(("parts", "ap"), None, None, None, None),
        P(None, ("parts", "ap"), None),
        P(("parts", "ap"), None),
        P("parts", None),
    )
    out_specs = P(("parts", "ap"), None, None)
    return jax.shard_map(
        on_device, mesh=mesh, in_specs=in_specs, out_specs=out_specs, check_vma=False
    )
```

```python
import functools

import jax
import jax.numpy as jnp
from jax import lax
from jax.experimental import pallas as pl
from jax.experimental.pallas import tpu as pltpu
from jax.sharding import PartitionSpec as P

epsilon = 1e-06
MIB = 1 << 20
CHUNKS = 2


def chip_orders(bits):
    first = list(range(1, bits))
    second = list(first)
    if bits > 2:
        second[0], second[1] = second[1], second[0]
    return second, first


def place_of(group, me, core, bits):
    away = [1 - (((group ^ me) >> bit) & 1) for bit in range(1, bits)]
    if bits > 2:
        swapped = core == 0
        away[:2] = [jnp.where(swapped, away[1], away[0]), jnp.where(swapped, away[0], away[1])]
    place = 0
    for value in away:
        place = place * 2 + value
    return place


def write_products(slots, rows, weights, served, out):
    users = rows.shape[0] // slots
    antennas = rows.shape[1] // 2
    blocks, steps = weights.shape[1] // 128, users // 8
    group = min(slots, 8)
    for base in range(0, slots, group):
        plain = rows[base * users:(base + group) * users, :]
        turned = jnp.concatenate([-plain[:, antennas:], plain[:, :antennas]], axis=1)
        both = jnp.concatenate([plain, turned], axis=0)
        value = jnp.dot(both, weights, preferred_element_type=jnp.float32)
        value = jnp.where(served, value, 0.0)
        for half in range(2):
            for slot in range(group):
                top = (half * group + slot) * users
                for block in range(blocks):
                    piece = value[top:top + users, block * 128:(block + 1) * 128]
                    start = (((base + slot) * 2 + half) * blocks + block) * steps
                    out[start:start + steps] = piece.reshape(steps, 8, 128)


def power_tile(weights, served):
    wide = weights.astype(jnp.float32)
    power = jnp.sum(wide * wide, axis=0, keepdims=True)
    power = jnp.where(served, power, 0.0)
    blocks = power.shape[1] // 128
    pieces = [power[:, block * 128:(block + 1) * 128] for block in range(blocks)]
    return jnp.concatenate(pieces + [jnp.zeros((8 - blocks, 128), jnp.float32)], axis=0)


def first_kernel(
    bits, visible, cluster, channel, precoder,
    out, rows, weights, served,
    seen, names, raw, sems,
):
    me = lax.axis_index("ap")
    held, users, antennas = raw.shape[1], raw.shape[3], raw.shape[4]
    width = weights.shape[2]
    slots = 1 << (bits - 1)
    loads = [
        pltpu.make_async_copy(visible, seen, sems.at[0]),
        pltpu.make_async_copy(channel, raw, sems.at[1]),
        pltpu.make_async_copy(cluster, names, sems.at[2]),
    ]
    for chunk in range(CHUNKS):
        at = pl.ds(chunk * width, width)
        loads.append(pltpu.make_async_copy(precoder.at[:, at], weights.at[chunk], sems.at[3 + chunk]))
    for load in loads:
        load.start()
    rows[...] = jnp.zeros_like(rows)
    loads[0].wait()
    loads[1].wait()
    for v in range(held):
        core = seen[0, v] & 1
        keep = 1 - (core ^ (me & 1))
        at = pl.ds(pl.multiple_of(place_of(seen[0, v], me, core, bits) * users, users), users)
        rows[keep, at, 0:antennas] = raw[0, v, 0]
        rows[keep, at, antennas:2 * antennas] = raw[0, v, 1]
    loads[2].wait()
    here = jnp.max((names[...] == me).astype(jnp.float32), axis=0, keepdims=True)
    for chunk in range(CHUNKS):
        served[chunk] = here[:, chunk * width:(chunk + 1) * width]
    loads[3].wait()
    chosen, mask = weights[0], served[0] > 0.0
    write_products(slots, rows.at[0], chosen, mask, out)
    out[out.shape[0] - 1] = power_tile(chosen, mask)
    for load in loads[4:]:
        load.wait()


def next_kernel(bits, keep, chunk, rows, weights, served, out):
    chosen, mask = weights[chunk], served[chunk] > 0.0
    write_products(1 << (bits - 1), rows.at[keep], chosen, mask, out)
    out[out.shape[0] - 1] = power_tile(chosen, mask)


def message(tiles):
    return jax.ShapeDtypeStruct((tiles, 8, 128), jnp.float32)


def estimate(rows, weights):
    return pl.CostEstimate(
        flops=8 * rows[1] * rows[2] * weights[2],
        bytes_accessed=rows[1] * (rows[2] * 2 + weights[2] * 8) + weights[1] * weights[2] * 2,
        transcendentals=0,
    )


def first_products(bits, visible, cluster, channel, precoder):
    users, antennas = channel.shape[3], channel.shape[4]
    width = precoder.shape[1] // CHUNKS
    slots = 1 << (bits - 1)
    tiles = (users // 8) * (width // 128) * 2
    rows = (2, slots * users, 2 * antennas)
    weights = (CHUNKS, precoder.shape[0], width)
    vmem = pl.BlockSpec(memory_space=pltpu.VMEM)
    hbm = pl.BlockSpec(memory_space=pltpu.HBM)
    operands = (visible, cluster, channel, precoder)
    return pl.pallas_call(
        functools.partial(first_kernel, bits),
        out_shape=(
            message(slots * tiles + 1),
            jax.ShapeDtypeStruct(rows, jnp.bfloat16),
            jax.ShapeDtypeStruct(weights, jnp.bfloat16),
            jax.ShapeDtypeStruct((CHUNKS, 1, width), jnp.float32),
        ),
        in_specs=[hbm] * 4,
        out_specs=(vmem,) * 4,
        scratch_shapes=[
            pltpu.SMEM(visible.shape, jnp.int32),
            pltpu.VMEM(cluster.shape, jnp.int32),
            pltpu.VMEM(channel.shape, jnp.bfloat16),
            pltpu.SemaphoreType.DMA((3 + CHUNKS,)),
        ],
        compiler_params=pltpu.CompilerParams(vmem_limit_bytes=52 * MIB if slots > 8 else 24 * MIB),
        cost_estimate=estimate(rows, weights),
        name="first_products",
    )(*[pltpu.with_memory_space_constraint(operand, pltpu.HBM) for operand in operands])


def next_products(bits, keep, chunk, rows, weights, served):
    slots = 1 << (bits - 1)
    users = rows.shape[1] // slots
    tiles = (users // 8) * (weights.shape[2] // 128) * 2
    vmem = pl.BlockSpec(memory_space=pltpu.VMEM)
    return pl.pallas_call(
        functools.partial(next_kernel, bits, keep, chunk),
        out_shape=message(slots * tiles + 1),
        in_specs=[vmem] * 3,
        out_specs=vmem,
        compiler_params=pltpu.CompilerParams(vmem_limit_bytes=48 * MIB if slots > 8 else 16 * MIB),
        cost_estimate=estimate(rows.shape, weights.shape),
        name="next_products",
    )(rows, weights, served)


def add_up(refs, terms, count):
    total = refs[terms[0][0]][terms[0][1]:terms[0][1] + count]
    for ref, start in terms[1:]:
        total = total + refs[ref][start:start + count]
    return total


def sum_kernel(jobs, *refs):
    at = 0
    for terms, count in jobs:
        refs[-1][at:at + count] = add_up(refs, terms, count)
        at += count


def summed(arrays, jobs):
    size = sum(count for _, count in jobs)
    vmem = pl.BlockSpec(memory_space=pltpu.VMEM)
    reads = sum(len(terms) * count for terms, count in jobs)
    return pl.pallas_call(
        functools.partial(sum_kernel, jobs),
        out_shape=message(size),
        in_specs=[vmem] * len(arrays),
        out_specs=vmem,
        compiler_params=pltpu.CompilerParams(vmem_limit_bytes=8 * MIB),
        cost_estimate=pl.CostEstimate(
            flops=reads * 1024, bytes_accessed=(reads + size) * 4096, transcendentals=0
        ),
        name="summed",
    )(*arrays)


def final_kernel(jobs, *refs):
    out = refs[-1]
    users, blocks = out.shape[0], out.shape[2] // 128 // CHUNKS
    steps = users // 8
    for chunk, (terms, powers) in enumerate(jobs):
        scale = lax.rsqrt(add_up(refs, powers, 1)[0] + epsilon)
        total = add_up(refs, terms, 2 * blocks * steps)
        for half in range(2):
            for block in range(blocks):
                start = (half * blocks + block) * steps
                value = total[start:start + steps].reshape(users, 128)
                factor = scale[block:block + 1, :]
                value = jnp.where(factor > 0.0, value * factor, 0.0)
                left = (chunk * blocks + block) * 128
                out[:, half, left:left + 128] = value


def finish(arrays, jobs, users, columns):
    vmem = pl.BlockSpec(memory_space=pltpu.VMEM)
    return pl.pallas_call(
        functools.partial(final_kernel, jobs),
        out_shape=jax.ShapeDtypeStruct((users, 2, columns), jnp.float32),
        in_specs=[vmem] * len(arrays),
        out_specs=vmem,
        compiler_params=pltpu.CompilerParams(vmem_limit_bytes=8 * MIB),
        name="finish",
    )(*arrays)


def on_device(channel, precoder, visible, cluster):
    devices = lax.axis_size("ap")
    bits = devices.bit_length() - 1
    users, columns = channel.shape[3], precoder.shape[2]
    tiles = (users // 8) * (columns // CHUNKS // 128) * 2
    orders = chip_orders(bits)
    flat = precoder.reshape(-1, columns)

    def swap(value, bit_of):
        return lax.ppermute(value, "ap", [(i, i ^ (1 << bit_of[i & 1])) for i in range(devices)])

    sent, rows, weights, served = first_products(bits, visible, cluster.T, channel, flat)
    got = [swap(sent, (0, 0))]
    for chunk in range(1, CHUNKS):
        got.append(swap(next_products(bits, 0, chunk, rows, weights, served), (0, 0)))
    held = [
        [next_products(bits, 1, chunk, rows, weights, served), got[chunk]] for chunk in range(CHUNKS)
    ]
    slots = devices // 2
    left = [(0, 0), (1, 0)]
    powers = [(0, slots * tiles), (1, slots * tiles)]
    for step in range(bits - 1):
        slots //= 2
        count = slots * tiles
        for mine in held:
            message_now = summed(mine, [(left, count), (powers, 1)])
            mine.append(swap(message_now, (orders[0][step], orders[1][step])))
        left = [(array, start + count) for array, start in left] + [(step + 2, 0)]
        powers = powers + [(step + 2, count)]
    jobs = []
    for chunk, mine in enumerate(held):
        base = chunk * len(mine)
        jobs.append((
            [(base + array, start) for array, start in left],
            [(base + array, start) for array, start in powers],
        ))
    return finish([array for mine in held for array in mine], jobs, users, columns)


def solution(mesh):
    in_specs = (
        P(("parts", "ap"), None, None, None, None),
        P(None, ("parts", "ap"), None),
        P(("parts", "ap"), None),
        P("parts", None),
    )
    out_specs = P(("parts", "ap"), None, None)
    return jax.shard_map(
        on_device, mesh=mesh, in_specs=in_specs, out_specs=out_specs, check_vma=False
    )
```

```python
import functools

import jax
import jax.numpy as jnp
from jax import lax
from jax.experimental import pallas as pl
from jax.experimental.pallas import tpu as pltpu
from jax.sharding import PartitionSpec as P

epsilon = 1e-06
MIB = 1 << 20
SHARES = (2, 1, 1)


def column_chunks(columns):
    unit = columns // sum(SHARES)
    return [(unit * sum(SHARES[:at]), unit * share) for at, share in enumerate(SHARES)]


def chip_orders(bits):
    first = list(range(1, bits))
    second = list(first)
    if bits > 2:
        second[0], second[1] = second[1], second[0]
    return second, first


def place_of(group, me, core, bits):
    away = [1 - (((group ^ me) >> bit) & 1) for bit in range(1, bits)]
    if bits > 2:
        swapped = core == 0
        away[:2] = [jnp.where(swapped, away[1], away[0]), jnp.where(swapped, away[0], away[1])]
    place = 0
    for value in away:
        place = place * 2 + value
    return place


def write_products(slots, rows, weights, served, out):
    users = rows.shape[0] // slots
    antennas = rows.shape[1] // 2
    blocks, steps = weights.shape[1] // 128, users // 8
    group = min(slots, 8)
    for base in range(0, slots, group):
        plain = rows[base * users:(base + group) * users, :]
        turned = jnp.concatenate([-plain[:, antennas:], plain[:, :antennas]], axis=1)
        both = jnp.concatenate([plain, turned], axis=0)
        value = jnp.dot(both, weights, preferred_element_type=jnp.float32)
        value = jnp.where(served, value, 0.0)
        for half in range(2):
            for slot in range(group):
                top = (half * group + slot) * users
                for block in range(blocks):
                    piece = value[top:top + users, block * 128:(block + 1) * 128]
                    start = (((base + slot) * 2 + half) * blocks + block) * steps
                    out[start:start + steps] = piece.reshape(steps, 8, 128)


def power_tile(weights, served):
    wide = weights.astype(jnp.float32)
    power = jnp.sum(wide * wide, axis=0, keepdims=True)
    power = jnp.where(served, power, 0.0)
    blocks = power.shape[1] // 128
    pieces = [power[:, block * 128:(block + 1) * 128] for block in range(blocks)]
    return jnp.concatenate(pieces + [jnp.zeros((8 - blocks, 128), jnp.float32)], axis=0)


def first_kernel(
    bits, visible, cluster, channel, precoder,
    out, rows, weights, served,
    seen, names, raw, sems,
):
    me = lax.axis_index("ap")
    held, users, antennas = raw.shape[1], raw.shape[3], raw.shape[4]
    chunks = column_chunks(weights.shape[1])
    slots = 1 << (bits - 1)
    loads = [
        pltpu.make_async_copy(visible, seen, sems.at[0]),
        pltpu.make_async_copy(channel, raw, sems.at[1]),
        pltpu.make_async_copy(cluster, names, sems.at[2]),
    ]
    for chunk, (start, width) in enumerate(chunks):
        at = pl.ds(start, width)
        loads.append(
            pltpu.make_async_copy(precoder.at[:, at], weights.at[:, at], sems.at[3 + chunk])
        )
    for load in loads:
        load.start()
    rows[...] = jnp.zeros_like(rows)
    loads[0].wait()
    loads[1].wait()
    for v in range(held):
        core = seen[0, v] & 1
        keep = 1 - (core ^ (me & 1))
        at = pl.ds(pl.multiple_of(place_of(seen[0, v], me, core, bits) * users, users), users)
        rows[keep, at, 0:antennas] = raw[0, v, 0]
        rows[keep, at, antennas:2 * antennas] = raw[0, v, 1]
    loads[2].wait()
    here = jnp.max((names[...] == me).astype(jnp.float32), axis=0, keepdims=True)
    served[...] = here
    loads[3].wait()
    width = chunks[0][1]
    chosen, mask = weights[:, 0:width], here[:, 0:width] > 0.0
    write_products(slots, rows.at[0], chosen, mask, out)
    out[out.shape[0] - 1] = power_tile(chosen, mask)
    for load in loads[4:]:
        load.wait()


def next_kernel(bits, jobs, rows, weights, served, *refs):
    for (keep, chunk), out in zip(jobs, refs[-len(jobs):]):
        start, width = column_chunks(weights.shape[1])[chunk]
        chosen, mask = weights[:, start:start + width], served[:, start:start + width] > 0.0
        write_products(1 << (bits - 1), rows.at[keep], chosen, mask, out)
        out[out.shape[0] - 1] = power_tile(chosen, mask)


def message(tiles):
    return jax.ShapeDtypeStruct((tiles, 8, 128), jnp.float32)


def estimate():
    return pl.CostEstimate(flops=8192, bytes_accessed=8192, transcendentals=0)


def first_products(bits, visible, cluster, channel, precoder):
    users, antennas = channel.shape[3], channel.shape[4]
    columns = precoder.shape[1]
    width = column_chunks(columns)[0][1]
    slots = 1 << (bits - 1)
    tiles = (users // 8) * (width // 128) * 2
    rows = (2, slots * users, 2 * antennas)
    vmem = pl.BlockSpec(memory_space=pltpu.VMEM)
    hbm = pl.BlockSpec(memory_space=pltpu.HBM)
    operands = (visible, cluster, channel, precoder)
    return pl.pallas_call(
        functools.partial(first_kernel, bits),
        out_shape=(
            message(slots * tiles + 1),
            jax.ShapeDtypeStruct(rows, jnp.bfloat16),
            jax.ShapeDtypeStruct(precoder.shape, jnp.bfloat16),
            jax.ShapeDtypeStruct((1, columns), jnp.float32),
        ),
        in_specs=[hbm] * 4,
        out_specs=(vmem,) * 4,
        scratch_shapes=[
            pltpu.SMEM(visible.shape, jnp.int32),
            pltpu.VMEM(cluster.shape, jnp.int32),
            pltpu.VMEM(channel.shape, jnp.bfloat16),
            pltpu.SemaphoreType.DMA((3 + len(SHARES),)),
        ],
        compiler_params=pltpu.CompilerParams(vmem_limit_bytes=52 * MIB if slots > 8 else 24 * MIB),
        cost_estimate=estimate(),
        name="first_products",
    )(*[pltpu.with_memory_space_constraint(operand, pltpu.HBM) for operand in operands])


def next_products(bits, jobs, rows, weights, served, after):
    slots = 1 << (bits - 1)
    users = rows.shape[1] // slots
    widths = [column_chunks(weights.shape[1])[chunk][1] for _, chunk in jobs]
    vmem = pl.BlockSpec(memory_space=pltpu.VMEM)
    return pl.pallas_call(
        functools.partial(next_kernel, bits, jobs),
        out_shape=[message(slots * (users // 8) * (width // 128) * 2 + 1) for width in widths],
        in_specs=[vmem] * (3 + len(after)),
        out_specs=[vmem] * len(jobs),
        compiler_params=pltpu.CompilerParams(vmem_limit_bytes=48 * MIB if slots > 8 else 16 * MIB),
        cost_estimate=estimate(),
        name="next_products",
    )(rows, weights, served, *after)


def add_up(refs, terms, count):
    total = refs[terms[0][0]][terms[0][1]:terms[0][1] + count]
    for ref, start in terms[1:]:
        total = total + refs[ref][start:start + count]
    return total


def sum_kernel(jobs, *refs):
    at = 0
    for terms, count in jobs:
        refs[-1][at:at + count] = add_up(refs, terms, count)
        at += count


def summed(arrays, jobs, after):
    size = sum(count for _, count in jobs)
    vmem = pl.BlockSpec(memory_space=pltpu.VMEM)
    return pl.pallas_call(
        functools.partial(sum_kernel, jobs),
        out_shape=message(size),
        in_specs=[vmem] * (len(arrays) + len(after)),
        out_specs=vmem,
        compiler_params=pltpu.CompilerParams(vmem_limit_bytes=8 * MIB),
        cost_estimate=estimate(),
        name="summed",
    )(*arrays, *after)


def final_kernel(jobs, *refs):
    out = refs[-1]
    users, columns = out.shape[0], out.shape[2]
    steps = users // 8
    for (first, width), (terms, powers) in zip(column_chunks(columns), jobs):
        blocks = width // 128
        scale = lax.rsqrt(add_up(refs, powers, 1)[0] + epsilon)
        total = add_up(refs, terms, 2 * blocks * steps)
        for half in range(2):
            for block in range(blocks):
                start = (half * blocks + block) * steps
                value = total[start:start + steps].reshape(users, 128)
                factor = scale[block:block + 1, :]
                value = jnp.where(factor > 0.0, value * factor, 0.0)
                left = first + block * 128
                out[:, half, left:left + 128] = value


def finish(arrays, jobs, users, columns):
    vmem = pl.BlockSpec(memory_space=pltpu.VMEM)
    return pl.pallas_call(
        functools.partial(final_kernel, jobs),
        out_shape=jax.ShapeDtypeStruct((users, 2, columns), jnp.float32),
        in_specs=[vmem] * len(arrays),
        out_specs=vmem,
        compiler_params=pltpu.CompilerParams(vmem_limit_bytes=8 * MIB),
        name="finish",
    )(*arrays)


def on_device(channel, precoder, visible, cluster):
    devices = lax.axis_size("ap")
    bits = devices.bit_length() - 1
    users, columns = channel.shape[3], precoder.shape[2]
    tiles = [(users // 8) * (width // 128) * 2 for _, width in column_chunks(columns)]
    chunks = range(len(tiles))
    orders = chip_orders(bits)
    flat = precoder.reshape(-1, columns)

    def swap(value, bit_of):
        return lax.ppermute(value, "ap", [(i, i ^ (1 << bit_of[i & 1])) for i in range(devices)])

    sent, rows, weights, served = first_products(bits, visible, cluster.T, channel, flat)
    got, held, after = [swap(sent, (0, 0))], [], []
    left = [[(0, 0), (1, 0)] for _ in chunks]
    powers = [[(0, devices // 2 * tiles[chunk]), (1, devices // 2 * tiles[chunk])] for chunk in chunks]
    slots = devices // 2
    for step in range(bits - 1):
        slots //= 2
        last = step == bits - 2
        for members in [chunks[:-1], chunks[-1:]] if last else [[chunk] for chunk in chunks]:
            if step == 0:
                chunk = members[0]
                wanted = ((0, chunk + 1), (1, chunk)) if chunk + 1 in chunks else ((1, chunk),)
                made = next_products(bits, wanted, rows, weights, served, after)
                if len(made) > 1:
                    got.append(swap(made[0], (0, 0)))
                held.append([made[-1], got[chunk]])
            arrays, parts, starts, size = [], [], [], 0
            for chunk in members:
                count = slots * tiles[chunk]
                for terms, amount in ((left[chunk], count), (powers[chunk], 1)):
                    parts.append(([(len(arrays) + array, start) for array, start in terms], amount))
                arrays = arrays + held[chunk]
                starts.append(size)
                size += count + 1
            message_now = summed(arrays, parts, after)
            came = swap(message_now, (orders[0][step], orders[1][step]))
            after = [message_now]
            for chunk, start in zip(members, starts):
                count = slots * tiles[chunk]
                left[chunk] = [(array, at + count) for array, at in left[chunk]]
                left[chunk].append((len(held[chunk]), start))
                powers[chunk].append((len(held[chunk]), start + count))
                held[chunk].append(came)
    jobs, arrays = [], []
    for chunk in chunks:
        jobs.append(tuple(
            [(len(arrays) + array, start) for array, start in terms]
            for terms in (left[chunk], powers[chunk])
        ))
        arrays = arrays + held[chunk]
    return finish(arrays, jobs, users, columns)


def solution(mesh):
    in_specs = (
        P(("parts", "ap"), None, None, None, None),
        P(None, ("parts", "ap"), None),
        P(("parts", "ap"), None),
        P("parts", None),
    )
    out_specs = P(("parts", "ap"), None, None)
    return jax.shard_map(
        on_device, mesh=mesh, in_specs=in_specs, out_specs=out_specs, check_vma=False
    )
```

```python
import functools

import jax
import jax.numpy as jnp
from jax import lax
from jax.experimental import pallas as pl
from jax.experimental.pallas import tpu as pltpu
from jax.sharding import PartitionSpec as P

epsilon = 1e-06
MIB = 1 << 20
SHARES = (1, 1, 1, 1)
PAIRED = ((0, 1), (2, 3))


def column_chunks(columns):
    unit = columns // sum(SHARES)
    return [(unit * sum(SHARES[:at]), unit * share) for at, share in enumerate(SHARES)]


def chip_orders(bits):
    first = list(range(1, bits))
    second = list(first)
    if bits > 2:
        second[0], second[1] = second[1], second[0]
    return second, first


def place_of(group, me, core, bits):
    away = [1 - (((group ^ me) >> bit) & 1) for bit in range(1, bits)]
    if bits > 2:
        swapped = core == 0
        away[:2] = [jnp.where(swapped, away[1], away[0]), jnp.where(swapped, away[0], away[1])]
    place = 0
    for value in away:
        place = place * 2 + value
    return place


def write_products(slots, rows, weights, served, out):
    users = rows.shape[0] // slots
    antennas = rows.shape[1] // 2
    blocks, steps = weights.shape[1] // 128, users // 8
    group = min(slots, 8)
    for base in range(0, slots, group):
        plain = rows[base * users:(base + group) * users, :]
        turned = jnp.concatenate([-plain[:, antennas:], plain[:, :antennas]], axis=1)
        both = jnp.concatenate([plain, turned], axis=0)
        value = jnp.dot(both, weights, preferred_element_type=jnp.float32)
        value = jnp.where(served, value, 0.0)
        for half in range(2):
            for slot in range(group):
                top = (half * group + slot) * users
                for block in range(blocks):
                    piece = value[top:top + users, block * 128:(block + 1) * 128]
                    start = (((base + slot) * 2 + half) * blocks + block) * steps
                    out[start:start + steps] = piece.reshape(steps, 8, 128)


def power_tile(weights, served):
    wide = weights.astype(jnp.float32)
    power = jnp.sum(wide * wide, axis=0, keepdims=True)
    power = jnp.where(served, power, 0.0)
    blocks = power.shape[1] // 128
    pieces = [power[:, block * 128:(block + 1) * 128] for block in range(blocks)]
    return jnp.concatenate(pieces + [jnp.zeros((8 - blocks, 128), jnp.float32)], axis=0)


def first_kernel(
    bits, visible, cluster, channel, precoder,
    out, rows, weights, served,
    seen, names, raw, sems,
):
    me = lax.axis_index("ap")
    held, users, antennas = raw.shape[1], raw.shape[3], raw.shape[4]
    chunks = column_chunks(weights.shape[1])
    slots = 1 << (bits - 1)
    loads = [
        pltpu.make_async_copy(visible, seen, sems.at[0]),
        pltpu.make_async_copy(channel, raw, sems.at[1]),
        pltpu.make_async_copy(cluster, names, sems.at[2]),
    ]
    for chunk, (start, width) in enumerate(chunks):
        at = pl.ds(start, width)
        loads.append(
            pltpu.make_async_copy(precoder.at[:, at], weights.at[:, at], sems.at[3 + chunk])
        )
    for load in loads:
        load.start()
    rows[...] = jnp.zeros_like(rows)
    loads[0].wait()
    loads[1].wait()
    for v in range(held):
        core = seen[0, v] & 1
        keep = 1 - (core ^ (me & 1))
        at = pl.ds(pl.multiple_of(place_of(seen[0, v], me, core, bits) * users, users), users)
        rows[keep, at, 0:antennas] = raw[0, v, 0]
        rows[keep, at, antennas:2 * antennas] = raw[0, v, 1]
    loads[2].wait()
    here = jnp.max((names[...] == me).astype(jnp.float32), axis=0, keepdims=True)
    served[...] = here
    loads[3].wait()
    width = chunks[0][1]
    chosen, mask = weights[:, 0:width], here[:, 0:width] > 0.0
    write_products(slots, rows.at[0], chosen, mask, out)
    out[out.shape[0] - 1] = power_tile(chosen, mask)
    for load in loads[4:]:
        load.wait()


def next_kernel(bits, jobs, rows, weights, served, *refs):
    for (keep, chunk), out in zip(jobs, refs[-len(jobs):]):
        start, width = column_chunks(weights.shape[1])[chunk]
        chosen, mask = weights[:, start:start + width], served[:, start:start + width] > 0.0
        write_products(1 << (bits - 1), rows.at[keep], chosen, mask, out)
        out[out.shape[0] - 1] = power_tile(chosen, mask)


def message(tiles):
    return jax.ShapeDtypeStruct((tiles, 8, 128), jnp.float32)


def estimate():
    return pl.CostEstimate(flops=8192, bytes_accessed=8192, transcendentals=0)


def first_products(bits, visible, cluster, channel, precoder):
    users, antennas = channel.shape[3], channel.shape[4]
    columns = precoder.shape[1]
    width = column_chunks(columns)[0][1]
    slots = 1 << (bits - 1)
    tiles = (users // 8) * (width // 128) * 2
    rows = (2, slots * users, 2 * antennas)
    vmem = pl.BlockSpec(memory_space=pltpu.VMEM)
    hbm = pl.BlockSpec(memory_space=pltpu.HBM)
    operands = (visible, cluster, channel, precoder)
    return pl.pallas_call(
        functools.partial(first_kernel, bits),
        out_shape=(
            message(slots * tiles + 1),
            jax.ShapeDtypeStruct(rows, jnp.bfloat16),
            jax.ShapeDtypeStruct(precoder.shape, jnp.bfloat16),
            jax.ShapeDtypeStruct((1, columns), jnp.float32),
        ),
        in_specs=[hbm] * 4,
        out_specs=(vmem,) * 4,
        scratch_shapes=[
            pltpu.SMEM(visible.shape, jnp.int32),
            pltpu.VMEM(cluster.shape, jnp.int32),
            pltpu.VMEM(channel.shape, jnp.bfloat16),
            pltpu.SemaphoreType.DMA((3 + len(SHARES),)),
        ],
        compiler_params=pltpu.CompilerParams(vmem_limit_bytes=52 * MIB if slots > 8 else 24 * MIB),
        cost_estimate=estimate(),
        name="first_products",
    )(*[pltpu.with_memory_space_constraint(operand, pltpu.HBM) for operand in operands])


def next_products(bits, jobs, rows, weights, served, after):
    slots = 1 << (bits - 1)
    users = rows.shape[1] // slots
    widths = [column_chunks(weights.shape[1])[chunk][1] for _, chunk in jobs]
    vmem = pl.BlockSpec(memory_space=pltpu.VMEM)
    return pl.pallas_call(
        functools.partial(next_kernel, bits, jobs),
        out_shape=[message(slots * (users // 8) * (width // 128) * 2 + 1) for width in widths],
        in_specs=[vmem] * (3 + len(after)),
        out_specs=[vmem] * len(jobs),
        compiler_params=pltpu.CompilerParams(vmem_limit_bytes=48 * MIB if slots > 8 else 16 * MIB),
        cost_estimate=estimate(),
        name="next_products",
    )(rows, weights, served, *after)


def add_up(refs, terms, count):
    total = refs[terms[0][0]][terms[0][1]:terms[0][1] + count]
    for ref, start in terms[1:]:
        total = total + refs[ref][start:start + count]
    return total


def sum_kernel(jobs, *refs):
    at = 0
    for terms, count in jobs:
        refs[-1][at:at + count] = add_up(refs, terms, count)
        at += count


def summed(arrays, jobs, after):
    size = sum(count for _, count in jobs)
    vmem = pl.BlockSpec(memory_space=pltpu.VMEM)
    return pl.pallas_call(
        functools.partial(sum_kernel, jobs),
        out_shape=message(size),
        in_specs=[vmem] * (len(arrays) + len(after)),
        out_specs=vmem,
        compiler_params=pltpu.CompilerParams(vmem_limit_bytes=8 * MIB),
        cost_estimate=estimate(),
        name="summed",
    )(*arrays, *after)


def final_kernel(jobs, *refs):
    out = refs[-1]
    users, columns = out.shape[0], out.shape[2]
    steps = users // 8
    for (first, width), (terms, powers) in zip(column_chunks(columns), jobs):
        blocks = width // 128
        scale = lax.rsqrt(add_up(refs, powers, 1)[0] + epsilon)
        total = add_up(refs, terms, 2 * blocks * steps)
        for half in range(2):
            for block in range(blocks):
                start = (half * blocks + block) * steps
                value = total[start:start + steps].reshape(users, 128)
                factor = scale[block:block + 1, :]
                value = jnp.where(factor > 0.0, value * factor, 0.0)
                left = first + block * 128
                out[:, half, left:left + 128] = value


def finish(arrays, jobs, users, columns):
    vmem = pl.BlockSpec(memory_space=pltpu.VMEM)
    return pl.pallas_call(
        functools.partial(final_kernel, jobs),
        out_shape=jax.ShapeDtypeStruct((users, 2, columns), jnp.float32),
        in_specs=[vmem] * len(arrays),
        out_specs=vmem,
        compiler_params=pltpu.CompilerParams(vmem_limit_bytes=8 * MIB),
        name="finish",
    )(*arrays)


def on_device(channel, precoder, visible, cluster):
    devices = lax.axis_size("ap")
    bits = devices.bit_length() - 1
    users, columns = channel.shape[3], precoder.shape[2]
    tiles = [(users // 8) * (width // 128) * 2 for _, width in column_chunks(columns)]
    chunks = range(len(tiles))
    orders = chip_orders(bits)
    flat = precoder.reshape(-1, columns)

    def swap(value, bit_of):
        return lax.ppermute(value, "ap", [(i, i ^ (1 << bit_of[i & 1])) for i in range(devices)])

    sent, rows, weights, served = first_products(bits, visible, cluster.T, channel, flat)
    got, held, after = [swap(sent, (0, 0))], [], []
    left = [[(0, 0), (1, 0)] for _ in chunks]
    powers = [[(0, devices // 2 * tiles[chunk]), (1, devices // 2 * tiles[chunk])] for chunk in chunks]
    slots = devices // 2
    for step in range(bits - 1):
        slots //= 2
        for members in PAIRED if step > 0 else [(chunk,) for chunk in chunks]:
            if step == 0:
                chunk = members[0]
                wanted = ((0, chunk + 1), (1, chunk)) if chunk + 1 in chunks else ((1, chunk),)
                made = next_products(bits, wanted, rows, weights, served, after)
                if len(made) > 1:
                    got.append(swap(made[0], (0, 0)))
                held.append([made[-1], got[chunk]])
            arrays, parts, starts, size = [], [], [], 0
            for chunk in members:
                count = slots * tiles[chunk]
                for terms, amount in ((left[chunk], count), (powers[chunk], 1)):
                    parts.append(([(len(arrays) + array, start) for array, start in terms], amount))
                arrays = arrays + held[chunk]
                starts.append(size)
                size += count + 1
            message_now = summed(arrays, parts, after)
            came = swap(message_now, (orders[0][step], orders[1][step]))
            after = [message_now]
            for chunk, start in zip(members, starts):
                count = slots * tiles[chunk]
                left[chunk] = [(array, at + count) for array, at in left[chunk]]
                left[chunk].append((len(held[chunk]), start))
                powers[chunk].append((len(held[chunk]), start + count))
                held[chunk].append(came)
    jobs, arrays = [], []
    for chunk in chunks:
        jobs.append(tuple(
            [(len(arrays) + array, start) for array, start in terms]
            for terms in (left[chunk], powers[chunk])
        ))
        arrays = arrays + held[chunk]
    return finish(arrays, jobs, users, columns)


def solution(mesh):
    in_specs = (
        P(("parts", "ap"), None, None, None, None),
        P(None, ("parts", "ap"), None),
        P(("parts", "ap"), None),
        P("parts", None),
    )
    out_specs = P(("parts", "ap"), None, None)
    return jax.shard_map(
        on_device, mesh=mesh, in_specs=in_specs, out_specs=out_specs, check_vma=False
    )
```

```python
import functools

import jax
import jax.numpy as jnp
from jax import lax
from jax.experimental import pallas as pl
from jax.experimental.pallas import tpu as pltpu
from jax.sharding import PartitionSpec as P

epsilon = 1e-06
MIB = 1 << 20
SHARES = (1, 1)
PAIRED = ((0,), (1,))


def column_chunks(columns):
    unit = columns // sum(SHARES)
    return [(unit * sum(SHARES[:at]), unit * share) for at, share in enumerate(SHARES)]


def chip_orders(bits):
    first = list(range(1, bits))
    second = list(first)
    if bits > 2:
        second[0], second[1] = second[1], second[0]
    return second, first


def place_of(group, me, core, bits):
    away = [1 - (((group ^ me) >> bit) & 1) for bit in range(1, bits)]
    if bits > 2:
        swapped = core == 0
        away[:2] = [jnp.where(swapped, away[1], away[0]), jnp.where(swapped, away[0], away[1])]
    place = 0
    for value in away:
        place = place * 2 + value
    return place


def write_products(slots, rows, weights, served, out):
    users = rows.shape[0] // slots
    antennas = rows.shape[1] // 2
    blocks, steps = weights.shape[1] // 128, users // 8
    group = min(slots, 8)
    for base in range(0, slots, group):
        plain = rows[base * users:(base + group) * users, :]
        turned = jnp.concatenate([-plain[:, antennas:], plain[:, :antennas]], axis=1)
        both = jnp.concatenate([plain, turned], axis=0)
        value = jnp.dot(both, weights, preferred_element_type=jnp.float32)
        value = jnp.where(served, value, 0.0)
        for half in range(2):
            for slot in range(group):
                top = (half * group + slot) * users
                for block in range(blocks):
                    piece = value[top:top + users, block * 128:(block + 1) * 128]
                    start = (((base + slot) * 2 + half) * blocks + block) * steps
                    out[start:start + steps] = piece.reshape(steps, 8, 128)


def power_tile(weights, served):
    wide = weights.astype(jnp.float32)
    power = jnp.sum(wide * wide, axis=0, keepdims=True)
    power = jnp.where(served, power, 0.0)
    blocks = power.shape[1] // 128
    pieces = [power[:, block * 128:(block + 1) * 128] for block in range(blocks)]
    return jnp.concatenate(pieces + [jnp.zeros((8 - blocks, 128), jnp.float32)], axis=0)


def first_kernel(
    bits, visible, cluster, channel, precoder,
    out, rows, weights, served,
    seen, names, raw, sems,
):
    me = lax.axis_index("ap")
    held, users, antennas = raw.shape[1], raw.shape[3], raw.shape[4]
    chunks = column_chunks(weights.shape[1])
    slots = 1 << (bits - 1)
    loads = [
        pltpu.make_async_copy(visible, seen, sems.at[0]),
        pltpu.make_async_copy(channel, raw, sems.at[1]),
        pltpu.make_async_copy(cluster, names, sems.at[2]),
    ]
    for chunk, (start, width) in enumerate(chunks):
        at = pl.ds(start, width)
        loads.append(
            pltpu.make_async_copy(precoder.at[:, at], weights.at[:, at], sems.at[3 + chunk])
        )
    for load in loads:
        load.start()
    rows[...] = jnp.zeros_like(rows)
    loads[0].wait()
    loads[1].wait()
    for v in range(held):
        core = seen[0, v] & 1
        keep = 1 - (core ^ (me & 1))
        at = pl.ds(pl.multiple_of(place_of(seen[0, v], me, core, bits) * users, users), users)
        rows[keep, at, 0:antennas] = raw[0, v, 0]
        rows[keep, at, antennas:2 * antennas] = raw[0, v, 1]
    loads[2].wait()
    here = jnp.max((names[...] == me).astype(jnp.float32), axis=0, keepdims=True)
    served[...] = here
    loads[3].wait()
    width = chunks[0][1]
    chosen, mask = weights[:, 0:width], here[:, 0:width] > 0.0
    write_products(slots, rows.at[0], chosen, mask, out)
    out[out.shape[0] - 1] = power_tile(chosen, mask)
    for load in loads[4:]:
        load.wait()


def next_kernel(bits, jobs, rows, weights, served, *refs):
    for (keep, chunk), out in zip(jobs, refs[-len(jobs):]):
        start, width = column_chunks(weights.shape[1])[chunk]
        chosen, mask = weights[:, start:start + width], served[:, start:start + width] > 0.0
        write_products(1 << (bits - 1), rows.at[keep], chosen, mask, out)
        out[out.shape[0] - 1] = power_tile(chosen, mask)


def message(tiles):
    return jax.ShapeDtypeStruct((tiles, 8, 128), jnp.float32)


def estimate():
    return pl.CostEstimate(flops=8192, bytes_accessed=8192, transcendentals=0)


def first_products(bits, visible, cluster, channel, precoder):
    users, antennas = channel.shape[3], channel.shape[4]
    columns = precoder.shape[1]
    width = column_chunks(columns)[0][1]
    slots = 1 << (bits - 1)
    tiles = (users // 8) * (width // 128) * 2
    rows = (2, slots * users, 2 * antennas)
    vmem = pl.BlockSpec(memory_space=pltpu.VMEM)
    hbm = pl.BlockSpec(memory_space=pltpu.HBM)
    operands = (visible, cluster, channel, precoder)
    return pl.pallas_call(
        functools.partial(first_kernel, bits),
        out_shape=(
            message(slots * tiles + 1),
            jax.ShapeDtypeStruct(rows, jnp.bfloat16),
            jax.ShapeDtypeStruct(precoder.shape, jnp.bfloat16),
            jax.ShapeDtypeStruct((1, columns), jnp.float32),
        ),
        in_specs=[hbm] * 4,
        out_specs=(vmem,) * 4,
        scratch_shapes=[
            pltpu.SMEM(visible.shape, jnp.int32),
            pltpu.VMEM(cluster.shape, jnp.int32),
            pltpu.VMEM(channel.shape, jnp.bfloat16),
            pltpu.SemaphoreType.DMA((3 + len(SHARES),)),
        ],
        compiler_params=pltpu.CompilerParams(vmem_limit_bytes=52 * MIB if slots > 8 else 24 * MIB),
        cost_estimate=estimate(),
        name="first_products",
    )(*[pltpu.with_memory_space_constraint(operand, pltpu.HBM) for operand in operands])


def next_products(bits, jobs, rows, weights, served, after):
    slots = 1 << (bits - 1)
    users = rows.shape[1] // slots
    widths = [column_chunks(weights.shape[1])[chunk][1] for _, chunk in jobs]
    vmem = pl.BlockSpec(memory_space=pltpu.VMEM)
    return pl.pallas_call(
        functools.partial(next_kernel, bits, jobs),
        out_shape=[message(slots * (users // 8) * (width // 128) * 2 + 1) for width in widths],
        in_specs=[vmem] * (3 + len(after)),
        out_specs=[vmem] * len(jobs),
        compiler_params=pltpu.CompilerParams(vmem_limit_bytes=48 * MIB if slots > 8 else 16 * MIB),
        cost_estimate=estimate(),
        name="next_products",
    )(rows, weights, served, *after)


def add_up(refs, terms, count):
    total = refs[terms[0][0]][terms[0][1]:terms[0][1] + count]
    for ref, start in terms[1:]:
        total = total + refs[ref][start:start + count]
    return total


def sum_kernel(jobs, *refs):
    at = 0
    for terms, count in jobs:
        refs[-1][at:at + count] = add_up(refs, terms, count)
        at += count


def summed(arrays, jobs, after):
    size = sum(count for _, count in jobs)
    vmem = pl.BlockSpec(memory_space=pltpu.VMEM)
    return pl.pallas_call(
        functools.partial(sum_kernel, jobs),
        out_shape=message(size),
        in_specs=[vmem] * (len(arrays) + len(after)),
        out_specs=vmem,
        compiler_params=pltpu.CompilerParams(vmem_limit_bytes=8 * MIB),
        cost_estimate=estimate(),
        name="summed",
    )(*arrays, *after)


def final_kernel(jobs, *refs):
    out = refs[-1]
    users, columns = out.shape[0], out.shape[2]
    steps = users // 8
    for (first, width), (terms, powers) in zip(column_chunks(columns), jobs):
        blocks = width // 128
        scale = lax.rsqrt(add_up(refs, powers, 1)[0] + epsilon)
        total = add_up(refs, terms, 2 * blocks * steps)
        for half in range(2):
            for block in range(blocks):
                start = (half * blocks + block) * steps
                value = total[start:start + steps].reshape(users, 128)
                factor = scale[block:block + 1, :]
                value = jnp.where(factor > 0.0, value * factor, 0.0)
                left = first + block * 128
                out[:, half, left:left + 128] = value


def finish(arrays, jobs, users, columns):
    vmem = pl.BlockSpec(memory_space=pltpu.VMEM)
    return pl.pallas_call(
        functools.partial(final_kernel, jobs),
        out_shape=jax.ShapeDtypeStruct((users, 2, columns), jnp.float32),
        in_specs=[vmem] * len(arrays),
        out_specs=vmem,
        compiler_params=pltpu.CompilerParams(vmem_limit_bytes=8 * MIB),
        name="finish",
    )(*arrays)


def on_device(channel, precoder, visible, cluster):
    devices = lax.axis_size("ap")
    bits = devices.bit_length() - 1
    users, columns = channel.shape[3], precoder.shape[2]
    tiles = [(users // 8) * (width // 128) * 2 for _, width in column_chunks(columns)]
    chunks = range(len(tiles))
    orders = chip_orders(bits)
    flat = precoder.reshape(-1, columns)

    def swap(value, bit_of):
        return lax.ppermute(value, "ap", [(i, i ^ (1 << bit_of[i & 1])) for i in range(devices)])

    sent, rows, weights, served = first_products(bits, visible, cluster.T, channel, flat)
    got, held, after = [swap(sent, (0, 0))], [], []
    left = [[(0, 0), (1, 0)] for _ in chunks]
    powers = [[(0, devices // 2 * tiles[chunk]), (1, devices // 2 * tiles[chunk])] for chunk in chunks]
    slots = devices // 2
    for step in range(bits - 1):
        slots //= 2
        for members in PAIRED if step > 0 else [(chunk,) for chunk in chunks]:
            if step == 0:
                chunk = members[0]
                wanted = ((0, chunk + 1), (1, chunk)) if chunk + 1 in chunks else ((1, chunk),)
                made = next_products(bits, wanted, rows, weights, served, after)
                if len(made) > 1:
                    got.append(swap(made[0], (0, 0)))
                held.append([made[-1], got[chunk]])
            arrays, parts, starts, size = [], [], [], 0
            for chunk in members:
                count = slots * tiles[chunk]
                for terms, amount in ((left[chunk], count), (powers[chunk], 1)):
                    parts.append(([(len(arrays) + array, start) for array, start in terms], amount))
                arrays = arrays + held[chunk]
                starts.append(size)
                size += count + 1
            message_now = summed(arrays, parts, after)
            came = swap(message_now, (orders[0][step], orders[1][step]))
            after = [message_now]
            for chunk, start in zip(members, starts):
                count = slots * tiles[chunk]
                left[chunk] = [(array, at + count) for array, at in left[chunk]]
                left[chunk].append((len(held[chunk]), start))
                powers[chunk].append((len(held[chunk]), start + count))
                held[chunk].append(came)
    jobs, arrays = [], []
    for chunk in chunks:
        jobs.append(tuple(
            [(len(arrays) + array, start) for array, start in terms]
            for terms in (left[chunk], powers[chunk])
        ))
        arrays = arrays + held[chunk]
    return finish(arrays, jobs, users, columns)


def solution(mesh):
    in_specs = (
        P(("parts", "ap"), None, None, None, None),
        P(None, ("parts", "ap"), None),
        P(("parts", "ap"), None),
        P("parts", None),
    )
    out_specs = P(("parts", "ap"), None, None)
    return jax.shard_map(
        on_device, mesh=mesh, in_specs=in_specs, out_specs=out_specs, check_vma=False
    )
```

```python
import functools

import jax
import jax.numpy as jnp
from jax import lax
from jax.experimental import pallas as pl
from jax.experimental.pallas import tpu as pltpu
from jax.sharding import PartitionSpec as P

epsilon = 1e-06
MIB = 1 << 20


def chip_orders(bits):
    first = list(range(1, bits))
    second = list(first)
    if bits > 2:
        second[0], second[1] = second[1], second[0]
    return second, first


def place_of(group, me, core, bits):
    away = [1 - (((group ^ me) >> bit) & 1) for bit in range(1, bits)]
    if bits > 2:
        swapped = core == 0
        away[:2] = [jnp.where(swapped, away[1], away[0]), jnp.where(swapped, away[0], away[1])]
    place = 0
    for value in away:
        place = place * 2 + value
    return place


def write_products(users, rows, weights, served, out):
    slots, antennas = rows.shape[0] // users, rows.shape[1] // 2
    blocks, steps = weights.shape[1] // 128, users // 8
    group = min(slots, 8)
    for base in range(0, slots, group):
        plain = rows[base * users:(base + group) * users, :]
        turned = jnp.concatenate([-plain[:, antennas:], plain[:, :antennas]], axis=1)
        both = jnp.concatenate([plain, turned], axis=0)
        value = jnp.dot(both, weights, preferred_element_type=jnp.float32)
        value = jnp.where(served, value, 0.0)
        for half in range(2):
            for slot in range(group):
                top = (half * group + slot) * users
                for block in range(blocks):
                    piece = value[top:top + users, block * 128:(block + 1) * 128]
                    start = (((base + slot) * 2 + half) * blocks + block) * steps
                    out[start:start + steps] = piece.reshape(steps, 8, 128)


def power_tile(weights, served):
    wide = weights.astype(jnp.float32)
    power = jnp.sum(wide * wide, axis=0, keepdims=True)
    power = jnp.where(served, power, 0.0)
    blocks = power.shape[1] // 128
    pieces = [power[:, block * 128:(block + 1) * 128] for block in range(blocks)]
    return jnp.concatenate(pieces + [jnp.zeros((8 - blocks, 128), jnp.float32)], axis=0)


def first_kernel(
    bits, visible, cluster, channel, precoder,
    out, rows, weights, served,
    seen, names, raw, sems,
):
    me = lax.axis_index("ap")
    held, users, antennas = raw.shape[1], raw.shape[3], raw.shape[4]
    loads = [
        pltpu.make_async_copy(visible, seen, sems.at[0]),
        pltpu.make_async_copy(channel, raw, sems.at[1]),
        pltpu.make_async_copy(cluster, names, sems.at[2]),
        pltpu.make_async_copy(precoder, weights, sems.at[3]),
    ]
    for load in loads:
        load.start()
    rows[...] = jnp.zeros_like(rows)
    loads[0].wait()
    loads[1].wait()
    for v in range(held):
        core = seen[0, v] & 1
        keep = 1 - (core ^ (me & 1))
        at = pl.ds(pl.multiple_of(place_of(seen[0, v], me, core, bits) * users, users), users)
        rows[keep, at, 0:antennas] = raw[0, v, 0]
        rows[keep, at, antennas:2 * antennas] = raw[0, v, 1]
    loads[2].wait()
    here = jnp.max((names[...] == me).astype(jnp.float32), axis=0, keepdims=True)
    served[...] = here
    loads[3].wait()
    mask = here > 0.0
    write_products(users, rows.at[0, 0:rows.shape[1] // 2], weights[...], mask, out)
    out[out.shape[0] - 1] = power_tile(weights[...], mask)


def next_kernel(users, keep, region, rows, weights, served, *refs):
    size = rows.shape[1] // 2
    mine = rows.at[keep, region * size:(region + 1) * size]
    write_products(users, mine, weights[...], served[...] > 0.0, refs[-1])


def message(tiles):
    return jax.ShapeDtypeStruct((tiles, 8, 128), jnp.float32)


def estimate(size=8192):
    return pl.CostEstimate(flops=size, bytes_accessed=size, transcendentals=0)


def first_products(bits, visible, cluster, channel, precoder):
    users, antennas = channel.shape[3], channel.shape[4]
    columns = precoder.shape[1]
    slots = 1 << (bits - 1)
    vmem = pl.BlockSpec(memory_space=pltpu.VMEM)
    hbm = pl.BlockSpec(memory_space=pltpu.HBM)
    operands = (visible, cluster, channel, precoder)
    return pl.pallas_call(
        functools.partial(first_kernel, bits),
        out_shape=(
            message(slots * (users // 8) * (columns // 128) + 1),
            jax.ShapeDtypeStruct((2, slots * users, 2 * antennas), jnp.bfloat16),
            jax.ShapeDtypeStruct(precoder.shape, jnp.bfloat16),
            jax.ShapeDtypeStruct((1, columns), jnp.float32),
        ),
        in_specs=[hbm] * 4,
        out_specs=(vmem,) * 4,
        scratch_shapes=[
            pltpu.SMEM(visible.shape, jnp.int32),
            pltpu.VMEM(cluster.shape, jnp.int32),
            pltpu.VMEM(channel.shape, jnp.bfloat16),
            pltpu.SemaphoreType.DMA((4,)),
        ],
        compiler_params=pltpu.CompilerParams(vmem_limit_bytes=52 * MIB if slots > 8 else 24 * MIB),
        cost_estimate=estimate(),
        name="first_products",
    )(*[pltpu.with_memory_space_constraint(operand, pltpu.HBM) for operand in operands])


def next_products(users, keep, region, rows, weights, served):
    slots = rows.shape[1] // users
    vmem = pl.BlockSpec(memory_space=pltpu.VMEM)
    return pl.pallas_call(
        functools.partial(next_kernel, users, keep, region),
        out_shape=message(slots * (users // 8) * (weights.shape[1] // 128)),
        in_specs=[vmem] * 3,
        out_specs=vmem,
        compiler_params=pltpu.CompilerParams(vmem_limit_bytes=48 * MIB if slots > 8 else 16 * MIB),
        cost_estimate=estimate(),
        name="next_products",
    )(rows, weights, served)


def add_up(refs, terms, count):
    total = refs[terms[0][0]][terms[0][1]:terms[0][1] + count]
    for ref, start in terms[1:]:
        total = total + refs[ref][start:start + count]
    return total


def sum_kernel(jobs, *refs):
    at = 0
    for terms, count in jobs:
        refs[-1][at:at + count] = add_up(refs, terms, count)
        at += count


def summed(arrays, jobs, cost):
    size = sum(count for _, count in jobs)
    vmem = pl.BlockSpec(memory_space=pltpu.VMEM)
    return pl.pallas_call(
        functools.partial(sum_kernel, jobs),
        out_shape=message(size),
        in_specs=[vmem] * len(arrays),
        out_specs=vmem,
        compiler_params=pltpu.CompilerParams(vmem_limit_bytes=8 * MIB),
        cost_estimate=estimate(cost),
        name="summed",
    )(*arrays)


def final_kernel(terms, powers, *refs):
    out = refs[-1]
    users, blocks = out.shape[0], out.shape[2] // 128
    steps = users // 8
    scale = lax.rsqrt(add_up(refs, powers, 1)[0] + epsilon)
    total = add_up(refs, terms, 2 * blocks * steps)
    for half in range(2):
        for block in range(blocks):
            start = (half * blocks + block) * steps
            value = total[start:start + steps].reshape(users, 128)
            factor = scale[block:block + 1, :]
            value = jnp.where(factor > 0.0, value * factor, 0.0)
            out[:, half, block * 128:(block + 1) * 128] = value


def finish(arrays, terms, powers, users, columns):
    vmem = pl.BlockSpec(memory_space=pltpu.VMEM)
    return pl.pallas_call(
        functools.partial(final_kernel, terms, powers),
        out_shape=jax.ShapeDtypeStruct((users, 2, columns), jnp.float32),
        in_specs=[vmem] * len(arrays),
        out_specs=vmem,
        compiler_params=pltpu.CompilerParams(vmem_limit_bytes=8 * MIB),
        name="finish",
    )(*arrays)


def message_order(chips):
    steps = []
    for step in range(chips):
        size = 1 << (chips - 1 - step)
        first = (1 << chips) - 2 * size
        steps.append(list(range(first, first + size)))
    if chips < 3:
        return [(step, slots) for step, slots in enumerate(steps)]
    quarter, half = len(steps[0]) // 4, len(steps[1]) // 2
    order = [
        (0, steps[0][:quarter]),
        (0, steps[0][quarter:3 * quarter]),
        (1, steps[1][:half]),
        (0, steps[0][3 * quarter:]),
        (1, steps[1][half:]),
    ]
    return order + [(step, steps[step]) for step in range(2, chips)]


def on_device(channel, precoder, visible, cluster):
    devices = lax.axis_size("ap")
    bits = devices.bit_length() - 1
    users, columns = channel.shape[3], precoder.shape[2]
    tiles = (users // 8) * (columns // 128) * 2
    orders = chip_orders(bits)
    flat = precoder.reshape(-1, columns)
    half = devices // 4

    def swap(value, bit_of):
        return lax.ppermute(value, "ap", [(i, i ^ (1 << bit_of[i & 1])) for i in range(devices)])

    arrays = []
    terms = [[] for _ in range(2 * half)]
    powers = []

    def add(array, slots, power):
        for at, slot in enumerate(slots):
            terms[slot].append((len(arrays), at * tiles))
        if power:
            powers.append((len(arrays), len(slots) * tiles))
        arrays.append(array)

    def total(slots, power, cost=8192):
        jobs = [(list(terms[slot]), tiles) for slot in slots] + ([(list(powers), 1)] if power else [])
        used = sorted({array for parts, _ in jobs for array, _ in parts})
        jobs = [([(used.index(array), start) for array, start in parts], count) for parts, count in jobs]
        return summed([arrays[array] for array in used], jobs, cost)

    sent, rows, weights, served = first_products(bits, visible, cluster.T, channel, flat)
    came = swap(sent, (0, 0))
    later = next_products(users, 0, 1, rows, weights, served)
    came_later = swap(later, (0, 0))
    add(sent, [], False)
    powers.append((0, half * tiles))
    add(next_products(users, 1, 0, rows, weights, served), range(half), False)
    add(came, range(half), True)
    add(next_products(users, 1, 1, rows, weights, served), range(half, 2 * half), False)
    add(came_later, range(half, 2 * half), False)
    with_power = set()
    last = 2 * half - 1
    for step, slots in message_order(bits - 1):
        power = step not in with_power
        with_power.add(step)
        came = swap(total(slots, power), (orders[0][step], orders[1][step]))
        slots = [slot + (1 << (bits - 2 - step)) for slot in slots]
        add(came, slots, power)
        if last in slots and step < bits - 2:
            own = total([last], False, 64 * MIB)
            terms[last] = []
            add(own, [last], False)
    used = sorted({array for array, _ in terms[last] + powers})
    return finish(
        [arrays[array] for array in used],
        [(used.index(array), start) for array, start in terms[last]],
        [(used.index(array), start) for array, start in powers],
        users, columns,
    )


def solution(mesh):
    in_specs = (
        P(("parts", "ap"), None, None, None, None),
        P(None, ("parts", "ap"), None),
        P(("parts", "ap"), None),
        P("parts", None),
    )
    out_specs = P(("parts", "ap"), None, None)
    return jax.shard_map(
        on_device, mesh=mesh, in_specs=in_specs, out_specs=out_specs, check_vma=False
    )
```

```python
import functools

import jax
import jax.numpy as jnp
from jax import lax
from jax.experimental import pallas as pl
from jax.experimental.pallas import tpu as pltpu
from jax.sharding import PartitionSpec as P

epsilon = 1e-06
MIB = 1 << 20


def chip_orders(bits):
    first = list(range(1, bits))
    second = list(first)
    if bits > 2:
        second[0], second[1] = second[1], second[0]
    return second, first


def place_of(group, me, core, bits):
    away = [1 - (((group ^ me) >> bit) & 1) for bit in range(1, bits)]
    if bits > 2:
        swapped = core == 0
        away[:2] = [jnp.where(swapped, away[1], away[0]), jnp.where(swapped, away[0], away[1])]
    place = 0
    for value in away:
        place = place * 2 + value
    return place


def write_products(users, rows, weights, served, out):
    slots, antennas = rows.shape[0] // users, rows.shape[1] // 2
    blocks, steps = weights.shape[1] // 128, users // 8
    group = min(slots, 8)
    for base in range(0, slots, group):
        plain = rows[base * users:(base + group) * users, :]
        turned = jnp.concatenate([-plain[:, antennas:], plain[:, :antennas]], axis=1)
        both = jnp.concatenate([plain, turned], axis=0)
        value = jnp.dot(both, weights, preferred_element_type=jnp.float32)
        value = jnp.where(served, value, 0.0)
        for half in range(2):
            for slot in range(group):
                top = (half * group + slot) * users
                for block in range(blocks):
                    piece = value[top:top + users, block * 128:(block + 1) * 128]
                    start = (((base + slot) * 2 + half) * blocks + block) * steps
                    out[start:start + steps] = piece.reshape(steps, 8, 128)


def power_tile(weights, served):
    wide = weights.astype(jnp.float32)
    power = jnp.sum(wide * wide, axis=0, keepdims=True)
    power = jnp.where(served, power, 0.0)
    blocks = power.shape[1] // 128
    pieces = [power[:, block * 128:(block + 1) * 128] for block in range(blocks)]
    return jnp.concatenate(pieces + [jnp.zeros((8 - blocks, 128), jnp.float32)], axis=0)


def first_kernel(
    bits, visible, cluster, channel, precoder,
    out, rows, weights, served,
    seen, names, raw, sems,
):
    me = lax.axis_index("ap")
    held, users, antennas = raw.shape[1], raw.shape[3], raw.shape[4]
    loads = [
        pltpu.make_async_copy(visible, seen, sems.at[0]),
        pltpu.make_async_copy(channel, raw, sems.at[1]),
        pltpu.make_async_copy(cluster, names, sems.at[2]),
        pltpu.make_async_copy(precoder, weights, sems.at[3]),
    ]
    for load in loads:
        load.start()
    rows[...] = jnp.zeros_like(rows)
    loads[0].wait()
    loads[1].wait()
    for v in range(held):
        core = seen[0, v] & 1
        keep = 1 - (core ^ (me & 1))
        at = pl.ds(pl.multiple_of(place_of(seen[0, v], me, core, bits) * users, users), users)
        rows[keep, at, 0:antennas] = raw[0, v, 0]
        rows[keep, at, antennas:2 * antennas] = raw[0, v, 1]
    loads[2].wait()
    here = jnp.max((names[...] == me).astype(jnp.float32), axis=0, keepdims=True)
    served[...] = here
    loads[3].wait()
    mask = here > 0.0
    write_products(users, rows.at[0, 0:rows.shape[1] // 2], weights[...], mask, out)
    out[out.shape[0] - 1] = power_tile(weights[...], mask)


def next_kernel(users, keep, region, rows, weights, served, *refs):
    size = rows.shape[1] // 2
    mine = rows.at[keep, region * size:(region + 1) * size]
    write_products(users, mine, weights[...], served[...] > 0.0, refs[-1])


def message(tiles):
    return jax.ShapeDtypeStruct((tiles, 8, 128), jnp.float32)


def estimate(size=8192):
    return pl.CostEstimate(flops=size, bytes_accessed=size, transcendentals=0)


def first_products(bits, visible, cluster, channel, precoder):
    users, antennas = channel.shape[3], channel.shape[4]
    columns = precoder.shape[1]
    slots = 1 << (bits - 1)
    vmem = pl.BlockSpec(memory_space=pltpu.VMEM)
    hbm = pl.BlockSpec(memory_space=pltpu.HBM)
    operands = (visible, cluster, channel, precoder)
    return pl.pallas_call(
        functools.partial(first_kernel, bits),
        out_shape=(
            message(slots * (users // 8) * (columns // 128) + 1),
            jax.ShapeDtypeStruct((2, slots * users, 2 * antennas), jnp.bfloat16),
            jax.ShapeDtypeStruct(precoder.shape, jnp.bfloat16),
            jax.ShapeDtypeStruct((1, columns), jnp.float32),
        ),
        in_specs=[hbm] * 4,
        out_specs=(vmem,) * 4,
        scratch_shapes=[
            pltpu.SMEM(visible.shape, jnp.int32),
            pltpu.VMEM(cluster.shape, jnp.int32),
            pltpu.VMEM(channel.shape, jnp.bfloat16),
            pltpu.SemaphoreType.DMA((4,)),
        ],
        compiler_params=pltpu.CompilerParams(vmem_limit_bytes=52 * MIB if slots > 8 else 24 * MIB),
        cost_estimate=estimate(),
        name="first_products",
    )(*[pltpu.with_memory_space_constraint(operand, pltpu.HBM) for operand in operands])


def next_products(users, keep, region, rows, weights, served):
    slots = rows.shape[1] // users
    vmem = pl.BlockSpec(memory_space=pltpu.VMEM)
    return pl.pallas_call(
        functools.partial(next_kernel, users, keep, region),
        out_shape=message(slots * (users // 8) * (weights.shape[1] // 128)),
        in_specs=[vmem] * 3,
        out_specs=vmem,
        compiler_params=pltpu.CompilerParams(vmem_limit_bytes=48 * MIB if slots > 8 else 16 * MIB),
        cost_estimate=estimate(),
        name="next_products",
    )(rows, weights, served)


def add_up(refs, terms, count):
    total = refs[terms[0][0]][terms[0][1]:terms[0][1] + count]
    for ref, start in terms[1:]:
        total = total + refs[ref][start:start + count]
    return total


def sum_kernel(jobs, *refs):
    at = 0
    for terms, count in jobs:
        refs[-1][at:at + count] = add_up(refs, terms, count)
        at += count


def summed(arrays, jobs, cost, after):
    size = sum(count for _, count in jobs)
    vmem = pl.BlockSpec(memory_space=pltpu.VMEM)
    return pl.pallas_call(
        functools.partial(sum_kernel, jobs),
        out_shape=message(size),
        in_specs=[vmem] * (len(arrays) + len(after)),
        out_specs=vmem,
        compiler_params=pltpu.CompilerParams(vmem_limit_bytes=8 * MIB),
        cost_estimate=estimate(cost),
        name="summed",
    )(*arrays, *after)


def final_kernel(terms, powers, *refs):
    out = refs[-1]
    users, blocks = out.shape[0], out.shape[2] // 128
    steps = users // 8
    scale = lax.rsqrt(add_up(refs, powers, 1)[0] + epsilon)
    for half in range(2):
        total = add_up(refs, terms[half], blocks * steps)
        for block in range(blocks):
            start = block * steps
            value = total[start:start + steps].reshape(users, 128)
            factor = scale[block:block + 1, :]
            value = jnp.where(factor > 0.0, value * factor, 0.0)
            out[:, half, block * 128:(block + 1) * 128] = value


def finish(arrays, terms, powers, users, columns):
    vmem = pl.BlockSpec(memory_space=pltpu.VMEM)
    return pl.pallas_call(
        functools.partial(final_kernel, terms, powers),
        out_shape=jax.ShapeDtypeStruct((users, 2, columns), jnp.float32),
        in_specs=[vmem] * len(arrays),
        out_specs=vmem,
        compiler_params=pltpu.CompilerParams(vmem_limit_bytes=8 * MIB),
        name="finish",
    )(*arrays)


def message_order(chips):
    steps = []
    for step in range(chips):
        size = 1 << (chips - 1 - step)
        first = (1 << chips) - 2 * size
        steps.append([(slot, part) for slot in range(first, first + size) for part in range(2)])
    if chips < 3:
        return [(step, pieces) for step, pieces in enumerate(steps)]
    quarter, half = len(steps[0]) // 4, len(steps[1]) // 2
    parts = [steps[0][at * quarter:(at + 1) * quarter] for at in range(4)]
    order = [
        (0, parts[0]),
        (0, parts[2] + parts[1][::2]),
        (1, steps[1][:half]),
        (0, parts[1][1::2] + parts[3]),
        (2, steps[2]),
        (1, steps[1][half:]),
    ]
    return order + [(step, steps[step]) for step in range(3, chips)]


def on_device(channel, precoder, visible, cluster):
    devices = lax.axis_size("ap")
    bits = devices.bit_length() - 1
    users, columns = channel.shape[3], precoder.shape[2]
    tiles = (users // 8) * (columns // 128)
    orders = chip_orders(bits)
    flat = precoder.reshape(-1, columns)
    half = devices // 4

    def swap(value, bit_of):
        return lax.ppermute(value, "ap", [(i, i ^ (1 << bit_of[i & 1])) for i in range(devices)])

    arrays = []
    terms = {(slot, part): [] for slot in range(2 * half) for part in range(2)}
    powers = []

    def add(array, pieces, power):
        for at, piece in enumerate(pieces):
            terms[piece].append((len(arrays), at * tiles))
        if power:
            powers.append((len(arrays), len(pieces) * tiles))
        arrays.append(array)

    def total(pieces, power, cost, after):
        jobs = [(list(terms[piece]), tiles) for piece in pieces]
        jobs += [(list(powers), 1)] * int(power)
        used = sorted({array for parts, _ in jobs for array, _ in parts})
        jobs = [([(used.index(array), start) for array, start in parts], count) for parts, count in jobs]
        return summed([arrays[array] for array in used], jobs, cost, after)

    def region(first):
        return [(slot, part) for slot in range(first, first + half) for part in range(2)]

    sent, rows, weights, served = first_products(bits, visible, cluster.T, channel, flat)
    came = swap(sent, (0, 0))
    later = next_products(users, 0, 1, rows, weights, served)
    came_later = swap(later, (0, 0))
    add(sent, [], False)
    powers.append((0, 2 * half * tiles))
    add(next_products(users, 1, 0, rows, weights, served), region(0), False)
    add(came, region(0), True)
    add(next_products(users, 1, 1, rows, weights, served), region(half), False)
    add(came_later, region(half), False)
    last = [(2 * half - 1, 0), (2 * half - 1, 1)]
    with_power, after = set(), []
    for step, pieces in message_order(bits - 1):
        power = step not in with_power
        with_power.add(step)
        now = total(pieces, power, 4096 * MIB if step == 2 else 8192, after)
        came = swap(now, (orders[0][step], orders[1][step]))
        after = [now] if step > 0 else []
        pieces = [(slot + (1 << (bits - 2 - step)), part) for slot, part in pieces]
        add(came, pieces, power)
    jobs = [(terms[piece], tiles) for piece in last]
    used = sorted({array for parts, _ in jobs + [(powers, 1)] for array, _ in parts})
    return finish(
        [arrays[array] for array in used],
        [[(used.index(array), start) for array, start in parts] for parts, _ in jobs],
        [(used.index(array), start) for array, start in powers],
        users, columns,
    )


def solution(mesh):
    in_specs = (
        P(("parts", "ap"), None, None, None, None),
        P(None, ("parts", "ap"), None),
        P(("parts", "ap"), None),
        P("parts", None),
    )
    out_specs = P(("parts", "ap"), None, None)
    return jax.shard_map(
        on_device, mesh=mesh, in_specs=in_specs, out_specs=out_specs, check_vma=False
    )
```

```python
import functools

import jax
import jax.numpy as jnp
from jax import lax
from jax.experimental import pallas as pl
from jax.experimental.pallas import tpu as pltpu
from jax.sharding import PartitionSpec as P

epsilon = 1e-06
MIB = 1 << 20


def chip_orders(bits):
    first = list(range(1, bits))
    second = list(first)
    if bits > 2:
        second[0], second[1] = second[1], second[0]
    return second, first


def place_of(group, me, core, bits):
    away = [1 - (((group ^ me) >> bit) & 1) for bit in range(1, bits)]
    if bits > 2:
        swapped = core == 0
        away[:2] = [jnp.where(swapped, away[1], away[0]), jnp.where(swapped, away[0], away[1])]
    place = 0
    for value in away:
        place = place * 2 + value
    return place


def write_products(users, rows, weights, served, out):
    slots, antennas = rows.shape[0] // users, rows.shape[1] // 2
    blocks, steps = weights.shape[1] // 128, users // 8
    group = max(size for size in range(1, 9) if slots % size == 0)
    for base in range(0, slots, group):
        plain = rows[base * users:(base + group) * users, :]
        turned = jnp.concatenate([-plain[:, antennas:], plain[:, :antennas]], axis=1)
        both = jnp.concatenate([plain, turned], axis=0)
        value = jnp.dot(both, weights, preferred_element_type=jnp.float32)
        value = jnp.where(served, value, 0.0)
        for half in range(2):
            for slot in range(group):
                top = (half * group + slot) * users
                for block in range(blocks):
                    piece = value[top:top + users, block * 128:(block + 1) * 128]
                    start = (((base + slot) * 2 + half) * blocks + block) * steps
                    out[start:start + steps] = piece.reshape(steps, 8, 128)


def power_tile(weights, served):
    wide = weights.astype(jnp.float32)
    power = jnp.sum(wide * wide, axis=0, keepdims=True)
    power = jnp.where(served, power, 0.0)
    blocks = power.shape[1] // 128
    pieces = [power[:, block * 128:(block + 1) * 128] for block in range(blocks)]
    return jnp.concatenate(pieces + [jnp.zeros((8 - blocks, 128), jnp.float32)], axis=0)


def first_kernel(
    bits, visible, cluster, channel, precoder,
    out, kept, rows, weights, served,
    seen, names, raw, sems,
):
    me = lax.axis_index("ap")
    held, users, antennas = raw.shape[1], raw.shape[3], raw.shape[4]
    loads = [
        pltpu.make_async_copy(visible, seen, sems.at[0]),
        pltpu.make_async_copy(channel, raw, sems.at[1]),
        pltpu.make_async_copy(cluster, names, sems.at[2]),
        pltpu.make_async_copy(precoder, weights, sems.at[3]),
    ]
    for load in loads:
        load.start()
    rows[...] = jnp.zeros_like(rows)
    loads[0].wait()
    loads[1].wait()
    for v in range(held):
        core = seen[0, v] & 1
        keep = 1 - (core ^ (me & 1))
        at = pl.ds(pl.multiple_of(place_of(seen[0, v], me, core, bits) * users, users), users)
        rows[keep, at, 0:antennas] = raw[0, v, 0]
        rows[keep, at, antennas:2 * antennas] = raw[0, v, 1]
    loads[2].wait()
    here = jnp.max((names[...] == me).astype(jnp.float32), axis=0, keepdims=True)
    served[...] = here
    loads[3].wait()
    mask = here > 0.0
    size = (kept.shape[0] // (weights.shape[1] // 128) // 2) * 8
    write_products(users, rows.at[0, 0:size], weights[...], mask, out)
    out[out.shape[0] - 1] = power_tile(weights[...], mask)
    write_products(users, rows.at[1, 0:size], weights[...], mask, kept)


def next_kernel(users, keep, first, slots, rows, weights, served, *refs):
    mine = rows.at[keep, first * users:(first + slots) * users]
    write_products(users, mine, weights[...], served[...] > 0.0, refs[-1])


def message(tiles):
    return jax.ShapeDtypeStruct((tiles, 8, 128), jnp.float32)


def estimate(size=8192):
    return pl.CostEstimate(flops=size, bytes_accessed=size, transcendentals=0)


def first_products(bits, first, visible, cluster, channel, precoder):
    users, antennas = channel.shape[3], channel.shape[4]
    columns = precoder.shape[1]
    slots = 1 << (bits - 1)
    tiles = first * (users // 8) * (columns // 128) * 2
    vmem = pl.BlockSpec(memory_space=pltpu.VMEM)
    hbm = pl.BlockSpec(memory_space=pltpu.HBM)
    operands = (visible, cluster, channel, precoder)
    return pl.pallas_call(
        functools.partial(first_kernel, bits),
        out_shape=(
            message(tiles + 1),
            message(tiles),
            jax.ShapeDtypeStruct((2, slots * users, 2 * antennas), jnp.bfloat16),
            jax.ShapeDtypeStruct(precoder.shape, jnp.bfloat16),
            jax.ShapeDtypeStruct((1, columns), jnp.float32),
        ),
        in_specs=[hbm] * 4,
        out_specs=(vmem,) * 5,
        scratch_shapes=[
            pltpu.SMEM(visible.shape, jnp.int32),
            pltpu.VMEM(cluster.shape, jnp.int32),
            pltpu.VMEM(channel.shape, jnp.bfloat16),
            pltpu.SemaphoreType.DMA((4,)),
        ],
        compiler_params=pltpu.CompilerParams(vmem_limit_bytes=52 * MIB if slots > 8 else 24 * MIB),
        cost_estimate=estimate(),
        name="first_products",
    )(*[pltpu.with_memory_space_constraint(operand, pltpu.HBM) for operand in operands])


def next_products(users, keep, first, slots, rows, weights, served):
    vmem = pl.BlockSpec(memory_space=pltpu.VMEM)
    big = slots > 8
    return pl.pallas_call(
        functools.partial(next_kernel, users, keep, first, slots),
        out_shape=message(slots * (users // 8) * (weights.shape[1] // 128) * 2),
        in_specs=[vmem] * 3,
        out_specs=vmem,
        compiler_params=pltpu.CompilerParams(vmem_limit_bytes=48 * MIB if big else 16 * MIB),
        cost_estimate=estimate(),
        name="next_products",
    )(rows, weights, served)


def add_up(refs, terms, count):
    total = refs[terms[0][0]][terms[0][1]:terms[0][1] + count]
    for ref, start in terms[1:]:
        total = total + refs[ref][start:start + count]
    return total


def sum_kernel(jobs, *refs):
    at = 0
    for terms, count in jobs:
        refs[-1][at:at + count] = add_up(refs, terms, count)
        at += count


def summed(arrays, jobs, cost):
    size = sum(count for _, count in jobs)
    vmem = pl.BlockSpec(memory_space=pltpu.VMEM)
    return pl.pallas_call(
        functools.partial(sum_kernel, jobs),
        out_shape=message(size),
        in_specs=[vmem] * len(arrays),
        out_specs=vmem,
        compiler_params=pltpu.CompilerParams(vmem_limit_bytes=8 * MIB),
        cost_estimate=estimate(cost),
        name="summed",
    )(*arrays)


def final_kernel(terms, powers, *refs):
    out = refs[-1]
    users, blocks = out.shape[0], out.shape[2] // 128
    steps = users // 8
    scale = lax.rsqrt(add_up(refs, powers, 1)[0] + epsilon)
    total = add_up(refs, terms, 2 * blocks * steps)
    for half in range(2):
        for block in range(blocks):
            start = (half * blocks + block) * steps
            value = total[start:start + steps].reshape(users, 128)
            factor = scale[block:block + 1, :]
            value = jnp.where(factor > 0.0, value * factor, 0.0)
            out[:, half, block * 128:(block + 1) * 128] = value


def finish(arrays, terms, powers, users, columns):
    vmem = pl.BlockSpec(memory_space=pltpu.VMEM)
    return pl.pallas_call(
        functools.partial(final_kernel, terms, powers),
        out_shape=jax.ShapeDtypeStruct((users, 2, columns), jnp.float32),
        in_specs=[vmem] * len(arrays),
        out_specs=vmem,
        compiler_params=pltpu.CompilerParams(vmem_limit_bytes=8 * MIB),
        name="finish",
    )(*arrays)


def message_order(chips):
    steps = []
    for step in range(chips):
        size = 1 << (chips - 1 - step)
        first = (1 << chips) - 2 * size
        steps.append(list(range(first, first + size)))
    if chips < 3:
        return [(step, slots) for step, slots in enumerate(steps)]
    quarter, half = len(steps[0]) // 4, len(steps[1]) // 2
    order = [
        (0, steps[0][:quarter]),
        (0, steps[0][quarter:3 * quarter]),
        (1, steps[1][:half]),
        (0, steps[0][3 * quarter:]),
        (1, steps[1][half:]),
    ]
    return order + [(step, steps[step]) for step in range(2, chips)]


def on_device(channel, precoder, visible, cluster):
    devices = lax.axis_size("ap")
    bits = devices.bit_length() - 1
    users, columns = channel.shape[3], precoder.shape[2]
    tiles = (users // 8) * (columns // 128) * 2
    orders = chip_orders(bits)
    flat = precoder.reshape(-1, columns)
    half = devices // 4

    def swap(value, bit_of):
        return lax.ppermute(value, "ap", [(i, i ^ (1 << bit_of[i & 1])) for i in range(devices)])

    arrays = []
    terms = [[] for _ in range(2 * half)]
    powers = []

    def add(array, slots, power):
        for at, slot in enumerate(slots):
            terms[slot].append((len(arrays), at * tiles))
        if power:
            powers.append((len(arrays), len(slots) * tiles))
        arrays.append(array)

    def total(slots, power, cost=8192):
        jobs = [(list(terms[slot]), tiles) for slot in slots] + ([(list(powers), 1)] if power else [])
        used = sorted({array for parts, _ in jobs for array, _ in parts})
        jobs = [([(used.index(array), start) for array, start in parts], count) for parts, count in jobs]
        return summed([arrays[array] for array in used], jobs, cost)

    quarter = half // 4
    sent, kept, rows, weights, served = first_products(
        bits, quarter, visible, cluster.T, channel, flat
    )
    came = swap(sent, (0, 0))
    add(sent, [], False)
    powers.append((0, quarter * tiles))
    add(kept, range(quarter), False)
    add(came, range(quarter), True)
    products = functools.partial(next_products, users, rows=rows, weights=weights, served=served)
    rest = range(quarter, 2 * half)
    later = swap(products(0, quarter, len(rest)), (0, 0))
    add(products(1, quarter, len(rest)), rest, False)
    add(later, rest, False)
    with_power = set()
    last = 2 * half - 1
    for number, (step, slots) in enumerate(message_order(bits - 1)):
        power = step not in with_power
        with_power.add(step)
        now = total(slots, power, 65536 * MIB if number == 0 else 8192)
        came = swap(now, (orders[0][step], orders[1][step]))
        slots = [slot + (1 << (bits - 2 - step)) for slot in slots]
        add(came, slots, power)
        if last in slots and step < bits - 2:
            own = total([last], False, 64 * MIB)
            terms[last] = []
            add(own, [last], False)
    used = sorted({array for array, _ in terms[last] + powers})
    return finish(
        [arrays[array] for array in used],
        [(used.index(array), start) for array, start in terms[last]],
        [(used.index(array), start) for array, start in powers],
        users, columns,
    )


def solution(mesh):
    in_specs = (
        P(("parts", "ap"), None, None, None, None),
        P(None, ("parts", "ap"), None),
        P(("parts", "ap"), None),
        P("parts", None),
    )
    out_specs = P(("parts", "ap"), None, None)
    return jax.shard_map(
        on_device, mesh=mesh, in_specs=in_specs, out_specs=out_specs, check_vma=False
    )
```

```python
import functools

import jax
import jax.numpy as jnp
from jax import lax
from jax.experimental import pallas as pl
from jax.experimental.pallas import tpu as pltpu
from jax.sharding import PartitionSpec as P

epsilon = 1e-06
MIB = 1 << 20


def chip_orders(bits):
    first = list(range(1, bits))
    second = list(first)
    if bits > 2:
        second[0], second[1] = second[1], second[0]
    return second, first


def place_of(group, me, core, bits):
    away = [1 - (((group ^ me) >> bit) & 1) for bit in range(1, bits)]
    if bits > 2:
        swapped = core == 0
        away[:2] = [jnp.where(swapped, away[1], away[0]), jnp.where(swapped, away[0], away[1])]
    place = 0
    for value in away:
        place = place * 2 + value
    return place


def write_products(users, rows, weights, served, out):
    slots, antennas = rows.shape[0] // users, rows.shape[1] // 2
    blocks, steps = weights.shape[1] // 128, users // 8
    group = max(size for size in range(1, 9) if slots % size == 0)
    for base in range(0, slots, group):
        plain = rows[base * users:(base + group) * users, :]
        turned = jnp.concatenate([-plain[:, antennas:], plain[:, :antennas]], axis=1)
        both = jnp.concatenate([plain, turned], axis=0)
        value = jnp.dot(both, weights, preferred_element_type=jnp.float32)
        value = jnp.where(served, value, 0.0)
        for half in range(2):
            for slot in range(group):
                top = (half * group + slot) * users
                for block in range(blocks):
                    piece = value[top:top + users, block * 128:(block + 1) * 128]
                    start = (((base + slot) * 2 + half) * blocks + block) * steps
                    out[start:start + steps] = piece.reshape(steps, 8, 128)


def power_tile(weights, served):
    wide = weights.astype(jnp.float32)
    power = jnp.sum(wide * wide, axis=0, keepdims=True)
    power = jnp.where(served, power, 0.0)
    blocks = power.shape[1] // 128
    pieces = [power[:, block * 128:(block + 1) * 128] for block in range(blocks)]
    return jnp.concatenate(pieces + [jnp.zeros((8 - blocks, 128), jnp.float32)], axis=0)


def first_kernel(
    bits, visible, cluster, channel, precoder,
    out, kept, rows, weights, served,
    seen, names, raw, sems,
):
    me = lax.axis_index("ap")
    held, users, antennas = raw.shape[1], raw.shape[3], raw.shape[4]
    loads = [
        pltpu.make_async_copy(visible, seen, sems.at[0]),
        pltpu.make_async_copy(channel, raw, sems.at[1]),
        pltpu.make_async_copy(cluster, names, sems.at[2]),
        pltpu.make_async_copy(precoder, weights, sems.at[3]),
    ]
    for load in loads:
        load.start()
    rows[...] = jnp.zeros_like(rows)
    loads[0].wait()
    loads[1].wait()
    for v in range(held):
        core = seen[0, v] & 1
        keep = 1 - (core ^ (me & 1))
        at = pl.ds(pl.multiple_of(place_of(seen[0, v], me, core, bits) * users, users), users)
        rows[keep, at, 0:antennas] = raw[0, v, 0]
        rows[keep, at, antennas:2 * antennas] = raw[0, v, 1]
    loads[2].wait()
    here = jnp.max((names[...] == me).astype(jnp.float32), axis=0, keepdims=True)
    served[...] = here
    loads[3].wait()
    mask = here > 0.0
    size = (kept.shape[0] // (weights.shape[1] // 128) // 2) * 8
    write_products(users, rows.at[0, 0:size], weights[...], mask, out)
    out[out.shape[0] - 1] = power_tile(weights[...], mask)
    write_products(users, rows.at[1, 0:size], weights[...], mask, kept)


def next_kernel(users, keep, first, slots, rows, weights, served, *refs):
    mine = rows.at[keep, first * users:(first + slots) * users]
    write_products(users, mine, weights[...], served[...] > 0.0, refs[-1])


def message(tiles):
    return jax.ShapeDtypeStruct((tiles, 8, 128), jnp.float32)


def estimate(size=8192):
    return pl.CostEstimate(flops=size, bytes_accessed=size, transcendentals=0)


def first_products(bits, first, visible, cluster, channel, precoder):
    users, antennas = channel.shape[3], channel.shape[4]
    columns = precoder.shape[1]
    slots = 1 << (bits - 1)
    tiles = first * (users // 8) * (columns // 128) * 2
    vmem = pl.BlockSpec(memory_space=pltpu.VMEM)
    hbm = pl.BlockSpec(memory_space=pltpu.HBM)
    operands = (visible, cluster, channel, precoder)
    return pl.pallas_call(
        functools.partial(first_kernel, bits),
        out_shape=(
            message(tiles + 1),
            message(tiles),
            jax.ShapeDtypeStruct((2, slots * users, 2 * antennas), jnp.bfloat16),
            jax.ShapeDtypeStruct(precoder.shape, jnp.bfloat16),
            jax.ShapeDtypeStruct((1, columns), jnp.float32),
        ),
        in_specs=[hbm] * 4,
        out_specs=(vmem,) * 5,
        scratch_shapes=[
            pltpu.SMEM(visible.shape, jnp.int32),
            pltpu.VMEM(cluster.shape, jnp.int32),
            pltpu.VMEM(channel.shape, jnp.bfloat16),
            pltpu.SemaphoreType.DMA((4,)),
        ],
        compiler_params=pltpu.CompilerParams(vmem_limit_bytes=52 * MIB if slots > 8 else 24 * MIB),
        cost_estimate=estimate(),
        name="first_products",
    )(*[pltpu.with_memory_space_constraint(operand, pltpu.HBM) for operand in operands])


def next_products(users, keep, first, slots, rows, weights, served):
    vmem = pl.BlockSpec(memory_space=pltpu.VMEM)
    big = slots > 8
    return pl.pallas_call(
        functools.partial(next_kernel, users, keep, first, slots),
        out_shape=message(slots * (users // 8) * (weights.shape[1] // 128) * 2),
        in_specs=[vmem] * 3,
        out_specs=vmem,
        compiler_params=pltpu.CompilerParams(vmem_limit_bytes=48 * MIB if big else 16 * MIB),
        cost_estimate=estimate(),
        name="next_products",
    )(rows, weights, served)


def add_up(refs, terms, count):
    total = refs[terms[0][0]][terms[0][1]:terms[0][1] + count]
    for ref, start in terms[1:]:
        total = total + refs[ref][start:start + count]
    return total


def sum_kernel(jobs, *refs):
    at = 0
    for terms, count in jobs:
        refs[-1][at:at + count] = add_up(refs, terms, count)
        at += count


def summed(arrays, jobs, cost, after):
    size = sum(count for _, count in jobs)
    vmem = pl.BlockSpec(memory_space=pltpu.VMEM)
    return pl.pallas_call(
        functools.partial(sum_kernel, jobs),
        out_shape=message(size),
        in_specs=[vmem] * (len(arrays) + len(after)),
        out_specs=vmem,
        compiler_params=pltpu.CompilerParams(vmem_limit_bytes=8 * MIB),
        cost_estimate=estimate(cost),
        name="summed",
    )(*arrays, *after)


def final_kernel(terms, powers, *refs):
    out = refs[-1]
    users, blocks = out.shape[0], out.shape[2] // 128
    steps = users // 8
    scale = lax.rsqrt(add_up(refs, powers, 1)[0] + epsilon)
    total = add_up(refs, terms, 2 * blocks * steps)
    for half in range(2):
        for block in range(blocks):
            start = (half * blocks + block) * steps
            value = total[start:start + steps].reshape(users, 128)
            factor = scale[block:block + 1, :]
            value = jnp.where(factor > 0.0, value * factor, 0.0)
            out[:, half, block * 128:(block + 1) * 128] = value


def finish(arrays, terms, powers, users, columns):
    vmem = pl.BlockSpec(memory_space=pltpu.VMEM)
    return pl.pallas_call(
        functools.partial(final_kernel, terms, powers),
        out_shape=jax.ShapeDtypeStruct((users, 2, columns), jnp.float32),
        in_specs=[vmem] * len(arrays),
        out_specs=vmem,
        compiler_params=pltpu.CompilerParams(vmem_limit_bytes=8 * MIB),
        name="finish",
    )(*arrays)


def message_order(chips):
    steps = []
    for step in range(chips):
        size = 1 << (chips - 1 - step)
        first = (1 << chips) - 2 * size
        steps.append(list(range(first, first + size)))
    if chips < 3:
        return [(step, slots) for step, slots in enumerate(steps)]
    quarter, half = len(steps[0]) // 4, len(steps[1]) // 2
    order = [
        (0, steps[0][:quarter]),
        (0, steps[0][quarter:3 * quarter]),
        (1, steps[1][:half]),
        (0, steps[0][3 * quarter:]),
        (2, steps[2]),
        (1, steps[1][half:]),
    ]
    return order + [(step, steps[step]) for step in range(3, chips)]


def on_device(channel, precoder, visible, cluster):
    devices = lax.axis_size("ap")
    bits = devices.bit_length() - 1
    users, columns = channel.shape[3], precoder.shape[2]
    tiles = (users // 8) * (columns // 128) * 2
    orders = chip_orders(bits)
    flat = precoder.reshape(-1, columns)
    half = devices // 4

    def swap(value, bit_of):
        return lax.ppermute(value, "ap", [(i, i ^ (1 << bit_of[i & 1])) for i in range(devices)])

    arrays = []
    terms = [[] for _ in range(2 * half)]
    powers = []

    def add(array, slots, power):
        for at, slot in enumerate(slots):
            terms[slot].append((len(arrays), at * tiles))
        if power:
            powers.append((len(arrays), len(slots) * tiles))
        arrays.append(array)

    def total(slots, power, cost=8192, after=()):
        jobs = [(list(terms[slot]), tiles) for slot in slots] + ([(list(powers), 1)] if power else [])
        used = sorted({array for parts, _ in jobs for array, _ in parts})
        jobs = [([(used.index(array), start) for array, start in parts], count) for parts, count in jobs]
        return summed([arrays[array] for array in used], jobs, cost, after)

    quarter = half // 4
    sent, kept, rows, weights, served = first_products(
        bits, quarter, visible, cluster.T, channel, flat
    )
    came = swap(sent, (0, 0))
    add(sent, [], False)
    powers.append((0, quarter * tiles))
    add(kept, range(quarter), False)
    add(came, range(quarter), True)
    products = functools.partial(next_products, users, rows=rows, weights=weights, served=served)
    rest = range(quarter, 2 * half)
    later = swap(products(0, quarter, len(rest)), (0, 0))
    add(products(1, quarter, len(rest)), rest, False)
    add(later, rest, False)
    with_power = set()
    last = 2 * half - 1
    for number, (step, slots) in enumerate(message_order(bits - 1)):
        power = step not in with_power
        with_power.add(step)
        after = [now] if number == 5 else []
        now = total(slots, power, 65536 * MIB if number == 0 else 8192, after)
        came = swap(now, (orders[0][step], orders[1][step]))
        slots = [slot + (1 << (bits - 2 - step)) for slot in slots]
        add(came, slots, power)
        if last in slots and number == 3:
            own = total([last], False, 256 * MIB)
            terms[last] = []
            add(own, [last], False)
    used = sorted({array for array, _ in terms[last] + powers})
    return finish(
        [arrays[array] for array in used],
        [(used.index(array), start) for array, start in terms[last]],
        [(used.index(array), start) for array, start in powers],
        users, columns,
    )


def solution(mesh):
    in_specs = (
        P(("parts", "ap"), None, None, None, None),
        P(None, ("parts", "ap"), None),
        P(("parts", "ap"), None),
        P("parts", None),
    )
    out_specs = P(("parts", "ap"), None, None)
    return jax.shard_map(
        on_device, mesh=mesh, in_specs=in_specs, out_specs=out_specs, check_vma=False
    )
```

```python
import functools

import jax
import jax.numpy as jnp
from jax import lax
from jax.experimental import pallas as pl
from jax.experimental.pallas import tpu as pltpu
from jax.sharding import PartitionSpec as P

epsilon = 1e-06
MIB = 1 << 20


COSTS = (8192, 64 * MIB, 65536 * MIB, 8192 * MIB) + (
    64 * MIB, 1024 * MIB, 1024 * MIB, 65536 * MIB, 1024 * MIB, 8192 * MIB
)


def chip_orders(bits):
    first = list(range(1, bits))
    second = list(first)
    if bits > 2:
        second[0], second[1] = second[1], second[0]
    return second, first


def place_of(group, me, core, bits):
    away = [1 - (((group ^ me) >> bit) & 1) for bit in range(1, bits)]
    if bits > 2:
        swapped = core == 0
        away[:2] = [jnp.where(swapped, away[1], away[0]), jnp.where(swapped, away[0], away[1])]
    place = 0
    for value in away:
        place = place * 2 + value
    return place


def write_products(users, rows, weights, served, out):
    slots, antennas = rows.shape[0] // users, rows.shape[1] // 2
    blocks, steps = weights.shape[1] // 128, users // 8
    group = max(size for size in range(1, 9) if slots % size == 0)
    for base in range(0, slots, group):
        plain = rows[base * users:(base + group) * users, :]
        turned = jnp.concatenate([-plain[:, antennas:], plain[:, :antennas]], axis=1)
        both = jnp.concatenate([plain, turned], axis=0)
        value = jnp.dot(both, weights, preferred_element_type=jnp.float32)
        value = jnp.where(served, value, 0.0)
        for half in range(2):
            for slot in range(group):
                top = (half * group + slot) * users
                for block in range(blocks):
                    piece = value[top:top + users, block * 128:(block + 1) * 128]
                    start = (((base + slot) * 2 + half) * blocks + block) * steps
                    out[start:start + steps] = piece.reshape(steps, 8, 128)


def power_tile(weights, served):
    wide = weights.astype(jnp.float32)
    power = jnp.sum(wide * wide, axis=0, keepdims=True)
    power = jnp.where(served, power, 0.0)
    blocks = power.shape[1] // 128
    pieces = [power[:, block * 128:(block + 1) * 128] for block in range(blocks)]
    return jnp.concatenate(pieces + [jnp.zeros((8 - blocks, 128), jnp.float32)], axis=0)


def first_kernel(
    bits, visible, cluster, channel, precoder,
    out, kept, rows, weights, served,
    seen, names, raw, sems,
):
    me = lax.axis_index("ap")
    held, users, antennas = raw.shape[1], raw.shape[3], raw.shape[4]
    loads = [
        pltpu.make_async_copy(visible, seen, sems.at[0]),
        pltpu.make_async_copy(channel, raw, sems.at[1]),
        pltpu.make_async_copy(cluster, names, sems.at[2]),
        pltpu.make_async_copy(precoder, weights, sems.at[3]),
    ]
    for load in loads:
        load.start()
    rows[...] = jnp.zeros_like(rows)
    loads[0].wait()
    loads[1].wait()
    for v in range(held):
        core = seen[0, v] & 1
        keep = 1 - (core ^ (me & 1))
        at = pl.ds(pl.multiple_of(place_of(seen[0, v], me, core, bits) * users, users), users)
        rows[keep, at, 0:antennas] = raw[0, v, 0]
        rows[keep, at, antennas:2 * antennas] = raw[0, v, 1]
    loads[2].wait()
    here = jnp.max((names[...] == me).astype(jnp.float32), axis=0, keepdims=True)
    served[...] = here
    loads[3].wait()
    mask = here > 0.0
    size = (kept.shape[0] // (weights.shape[1] // 128) // 2) * 8
    write_products(users, rows.at[0, 0:size], weights[...], mask, out)
    out[out.shape[0] - 1] = power_tile(weights[...], mask)
    write_products(users, rows.at[1, 0:size], weights[...], mask, kept)


def next_kernel(users, keep, first, slots, rows, weights, served, *refs):
    mine = rows.at[keep, first * users:(first + slots) * users]
    write_products(users, mine, weights[...], served[...] > 0.0, refs[-1])


def message(tiles):
    return jax.ShapeDtypeStruct((tiles, 8, 128), jnp.float32)


def estimate(size=8192):
    return pl.CostEstimate(flops=size, bytes_accessed=size, transcendentals=0)


def first_products(bits, first, visible, cluster, channel, precoder):
    users, antennas = channel.shape[3], channel.shape[4]
    columns = precoder.shape[1]
    slots = 1 << (bits - 1)
    tiles = first * (users // 8) * (columns // 128) * 2
    vmem = pl.BlockSpec(memory_space=pltpu.VMEM)
    hbm = pl.BlockSpec(memory_space=pltpu.HBM)
    operands = (visible, cluster, channel, precoder)
    return pl.pallas_call(
        functools.partial(first_kernel, bits),
        out_shape=(
            message(tiles + 1),
            message(tiles),
            jax.ShapeDtypeStruct((2, slots * users, 2 * antennas), jnp.bfloat16),
            jax.ShapeDtypeStruct(precoder.shape, jnp.bfloat16),
            jax.ShapeDtypeStruct((1, columns), jnp.float32),
        ),
        in_specs=[hbm] * 4,
        out_specs=(vmem,) * 5,
        scratch_shapes=[
            pltpu.SMEM(visible.shape, jnp.int32),
            pltpu.VMEM(cluster.shape, jnp.int32),
            pltpu.VMEM(channel.shape, jnp.bfloat16),
            pltpu.SemaphoreType.DMA((4,)),
        ],
        compiler_params=pltpu.CompilerParams(vmem_limit_bytes=52 * MIB if slots > 8 else 24 * MIB),
        cost_estimate=estimate(),
        name="first_products",
    )(*[pltpu.with_memory_space_constraint(operand, pltpu.HBM) for operand in operands])


def next_products(users, keep, first, slots, cost, rows, weights, served):
    vmem = pl.BlockSpec(memory_space=pltpu.VMEM)
    big = slots > 8
    return pl.pallas_call(
        functools.partial(next_kernel, users, keep, first, slots),
        out_shape=message(slots * (users // 8) * (weights.shape[1] // 128) * 2),
        in_specs=[vmem] * 3,
        out_specs=vmem,
        compiler_params=pltpu.CompilerParams(vmem_limit_bytes=48 * MIB if big else 16 * MIB),
        cost_estimate=estimate(cost),
        name="next_products",
    )(rows, weights, served)


def add_up(refs, terms, count):
    total = refs[terms[0][0]][terms[0][1]:terms[0][1] + count]
    for ref, start in terms[1:]:
        total = total + refs[ref][start:start + count]
    return total


def sum_kernel(jobs, *refs):
    at = 0
    for terms, count in jobs:
        refs[-1][at:at + count] = add_up(refs, terms, count)
        at += count


def summed(arrays, jobs, cost, after):
    size = sum(count for _, count in jobs)
    vmem = pl.BlockSpec(memory_space=pltpu.VMEM)
    return pl.pallas_call(
        functools.partial(sum_kernel, jobs),
        out_shape=message(size),
        in_specs=[vmem] * (len(arrays) + len(after)),
        out_specs=vmem,
        compiler_params=pltpu.CompilerParams(vmem_limit_bytes=8 * MIB),
        cost_estimate=estimate(cost),
        name="summed",
    )(*arrays, *after)


def final_kernel(terms, powers, *refs):
    out = refs[-1]
    users, blocks = out.shape[0], out.shape[2] // 128
    steps = users // 8
    scale = lax.rsqrt(add_up(refs, powers, 1)[0] + epsilon)
    total = add_up(refs, terms, 2 * blocks * steps)
    for half in range(2):
        for block in range(blocks):
            start = (half * blocks + block) * steps
            value = total[start:start + steps].reshape(users, 128)
            factor = scale[block:block + 1, :]
            value = jnp.where(factor > 0.0, value * factor, 0.0)
            out[:, half, block * 128:(block + 1) * 128] = value


def finish(arrays, terms, powers, users, columns):
    vmem = pl.BlockSpec(memory_space=pltpu.VMEM)
    return pl.pallas_call(
        functools.partial(final_kernel, terms, powers),
        out_shape=jax.ShapeDtypeStruct((users, 2, columns), jnp.float32),
        in_specs=[vmem] * len(arrays),
        out_specs=vmem,
        compiler_params=pltpu.CompilerParams(vmem_limit_bytes=8 * MIB),
        name="finish",
    )(*arrays)


def message_order(chips):
    steps = []
    for step in range(chips):
        size = 1 << (chips - 1 - step)
        first = (1 << chips) - 2 * size
        steps.append(list(range(first, first + size)))
    if chips < 3:
        return [(step, slots) for step, slots in enumerate(steps)]
    quarter, half = len(steps[0]) // 4, len(steps[1]) // 2
    parts = [steps[0][at * quarter:(at + 1) * quarter] for at in range(4)]
    order = [
        (0, parts[0]),
        (0, parts[2]),
        (1, steps[1][:half]),
        (0, parts[1] + parts[3]),
        (2, steps[2]),
        (1, steps[1][half:]),
    ]
    return order + [(step, steps[step]) for step in range(3, chips)]


def on_device(channel, precoder, visible, cluster):
    devices = lax.axis_size("ap")
    bits = devices.bit_length() - 1
    users, columns = channel.shape[3], precoder.shape[2]
    tiles = (users // 8) * (columns // 128) * 2
    orders = chip_orders(bits)
    flat = precoder.reshape(-1, columns)
    half = devices // 4

    def swap(value, bit_of):
        return lax.ppermute(value, "ap", [(i, i ^ (1 << bit_of[i & 1])) for i in range(devices)])

    arrays = []
    terms = [[] for _ in range(2 * half)]
    powers = []

    def add(array, slots, power):
        for at, slot in enumerate(slots):
            terms[slot].append((len(arrays), at * tiles))
        if power:
            powers.append((len(arrays), len(slots) * tiles))
        arrays.append(array)

    def total(slots, power, cost=8192, after=()):
        jobs = [(list(terms[slot]), tiles) for slot in slots] + ([(list(powers), 1)] if power else [])
        used = sorted({array for parts, _ in jobs for array, _ in parts})
        jobs = [([(used.index(array), start) for array, start in parts], count) for parts, count in jobs]
        return summed([arrays[array] for array in used], jobs, cost, after)

    quarter = half // 4
    sent, kept, rows, weights, served = first_products(
        bits, quarter, visible, cluster.T, channel, flat
    )
    came = swap(sent, (0, 0))
    add(sent, [], False)
    powers.append((0, quarter * tiles))
    add(kept, range(quarter), False)
    add(came, range(quarter), True)
    products = functools.partial(next_products, users, rows=rows, weights=weights, served=served)
    for at, (first, count) in enumerate(((quarter, 4 * quarter), (5 * quarter, 3 * quarter))):
        slots = range(first, first + count)
        come = swap(products(0, first, count, cost=COSTS[2 * at]), (0, 0))
        add(products(1, first, count, cost=COSTS[2 * at + 1]), slots, False)
        add(come, slots, False)
    with_power = set()
    last = 2 * half - 1
    for number, (step, slots) in enumerate(message_order(bits - 1)):
        power = step not in with_power
        with_power.add(step)
        after = [now] if number in (3, 5) else []
        now = total(slots, power, COSTS[4 + number] if number < 6 else 8192, after)
        came = swap(now, (orders[0][step], orders[1][step]))
        slots = [slot + (1 << (bits - 2 - step)) for slot in slots]
        add(came, slots, power)
    used = sorted({array for array, _ in terms[last] + powers})
    return finish(
        [arrays[array] for array in used],
        [(used.index(array), start) for array, start in terms[last]],
        [(used.index(array), start) for array, start in powers],
        users, columns,
    )


def solution(mesh):
    in_specs = (
        P(("parts", "ap"), None, None, None, None),
        P(None, ("parts", "ap"), None),
        P(("parts", "ap"), None),
        P("parts", None),
    )
    out_specs = P(("parts", "ap"), None, None)
    return jax.shard_map(
        on_device, mesh=mesh, in_specs=in_specs, out_specs=out_specs, check_vma=False
    )
```

```python
import functools

import jax
import jax.numpy as jnp
from jax import lax
from jax.experimental import pallas as pl
from jax.experimental.pallas import tpu as pltpu
from jax.sharding import PartitionSpec as P

epsilon = 1e-06
MIB = 1 << 20


COSTS = (8192, 64 * MIB, 65536 * MIB, 8192 * MIB) + (
    64 * MIB, 1024 * MIB, 1024 * MIB, 65536 * MIB, 1024 * MIB, 8192 * MIB
)


def place_of(group, me, bits):
    place = 0
    for bit in range(1, bits):
        place = place * 2 + (1 - (((group ^ me) >> bit) & 1))
    return place


def write_products(users, rows, weights, served, out):
    slots, antennas = rows.shape[0] // users, rows.shape[1] // 2
    blocks, steps = weights.shape[1] // 128, users // 8
    group = max(size for size in range(1, 9) if slots % size == 0)
    for base in range(0, slots, group):
        plain = rows[base * users:(base + group) * users, :]
        turned = jnp.concatenate([-plain[:, antennas:], plain[:, :antennas]], axis=1)
        both = jnp.concatenate([plain, turned], axis=0)
        value = jnp.dot(both, weights, preferred_element_type=jnp.float32)
        value = jnp.where(served, value, 0.0)
        for half in range(2):
            for slot in range(group):
                top = (half * group + slot) * users
                for block in range(blocks):
                    piece = value[top:top + users, block * 128:(block + 1) * 128]
                    start = (((base + slot) * 2 + half) * blocks + block) * steps
                    out[start:start + steps] = piece.reshape(steps, 8, 128)


def power_tile(weights, served):
    wide = weights.astype(jnp.float32)
    power = jnp.sum(wide * wide, axis=0, keepdims=True)
    power = jnp.where(served, power, 0.0)
    blocks = power.shape[1] // 128
    pieces = [power[:, block * 128:(block + 1) * 128] for block in range(blocks)]
    return jnp.concatenate(pieces + [jnp.zeros((8 - blocks, 128), jnp.float32)], axis=0)


def first_kernel(
    bits, visible, cluster, channel, precoder,
    out, kept, rows, weights, served,
    seen, names, raw, sems,
):
    me = lax.axis_index("ap")
    held, users, antennas = raw.shape[1], raw.shape[3], raw.shape[4]
    loads = [
        pltpu.make_async_copy(visible, seen, sems.at[0]),
        pltpu.make_async_copy(channel, raw, sems.at[1]),
        pltpu.make_async_copy(cluster, names, sems.at[2]),
        pltpu.make_async_copy(precoder, weights, sems.at[3]),
    ]
    for load in loads:
        load.start()
    rows[...] = jnp.zeros_like(rows)
    loads[0].wait()
    loads[1].wait()
    for v in range(held):
        keep = 1 - ((seen[0, v] ^ me) & 1)
        at = pl.ds(pl.multiple_of(place_of(seen[0, v], me, bits) * users, users), users)
        rows[keep, at, 0:antennas] = raw[0, v, 0]
        rows[keep, at, antennas:2 * antennas] = raw[0, v, 1]
    loads[2].wait()
    here = jnp.max((names[...] == me).astype(jnp.float32), axis=0, keepdims=True)
    served[...] = here
    loads[3].wait()
    mask = here > 0.0
    size = (kept.shape[0] // (weights.shape[1] // 128) // 2) * 8
    write_products(users, rows.at[0, 0:size], weights[...], mask, out)
    out[out.shape[0] - 1] = power_tile(weights[...], mask)
    write_products(users, rows.at[1, 0:size], weights[...], mask, kept)


def next_kernel(users, keep, first, slots, rows, weights, served, *refs):
    mine = rows.at[keep, first * users:(first + slots) * users]
    write_products(users, mine, weights[...], served[...] > 0.0, refs[-1])


def message(tiles):
    return jax.ShapeDtypeStruct((tiles, 8, 128), jnp.float32)


def estimate(size=8192):
    return pl.CostEstimate(flops=size, bytes_accessed=size, transcendentals=0)


def first_products(bits, first, visible, cluster, channel, precoder):
    users, antennas = channel.shape[3], channel.shape[4]
    columns = precoder.shape[1]
    slots = 1 << (bits - 1)
    tiles = first * (users // 8) * (columns // 128) * 2
    vmem = pl.BlockSpec(memory_space=pltpu.VMEM)
    hbm = pl.BlockSpec(memory_space=pltpu.HBM)
    operands = (visible, cluster, channel, precoder)
    return pl.pallas_call(
        functools.partial(first_kernel, bits),
        out_shape=(
            message(tiles + 1),
            message(tiles),
            jax.ShapeDtypeStruct((2, slots * users, 2 * antennas), jnp.bfloat16),
            jax.ShapeDtypeStruct(precoder.shape, jnp.bfloat16),
            jax.ShapeDtypeStruct((1, columns), jnp.float32),
        ),
        in_specs=[hbm] * 4,
        out_specs=(vmem,) * 5,
        scratch_shapes=[
            pltpu.SMEM(visible.shape, jnp.int32),
            pltpu.VMEM(cluster.shape, jnp.int32),
            pltpu.VMEM(channel.shape, jnp.bfloat16),
            pltpu.SemaphoreType.DMA((4,)),
        ],
        compiler_params=pltpu.CompilerParams(vmem_limit_bytes=52 * MIB if slots > 8 else 24 * MIB),
        cost_estimate=estimate(),
        name="first_products",
    )(*[pltpu.with_memory_space_constraint(operand, pltpu.HBM) for operand in operands])


def next_products(users, keep, first, slots, cost, rows, weights, served):
    vmem = pl.BlockSpec(memory_space=pltpu.VMEM)
    big = slots > 8
    return pl.pallas_call(
        functools.partial(next_kernel, users, keep, first, slots),
        out_shape=message(slots * (users // 8) * (weights.shape[1] // 128) * 2),
        in_specs=[vmem] * 3,
        out_specs=vmem,
        compiler_params=pltpu.CompilerParams(vmem_limit_bytes=48 * MIB if big else 16 * MIB),
        cost_estimate=estimate(cost),
        name="next_products",
    )(rows, weights, served)


def add_up(refs, terms, count):
    total = refs[terms[0][0]][terms[0][1]:terms[0][1] + count]
    for ref, start in terms[1:]:
        total = total + refs[ref][start:start + count]
    return total


def sum_kernel(jobs, *refs):
    at = 0
    for terms, count in jobs:
        refs[-1][at:at + count] = add_up(refs, terms, count)
        at += count


def summed(arrays, jobs, cost, after):
    size = sum(count for _, count in jobs)
    vmem = pl.BlockSpec(memory_space=pltpu.VMEM)
    return pl.pallas_call(
        functools.partial(sum_kernel, jobs),
        out_shape=message(size),
        in_specs=[vmem] * (len(arrays) + len(after)),
        out_specs=vmem,
        compiler_params=pltpu.CompilerParams(vmem_limit_bytes=8 * MIB),
        cost_estimate=estimate(cost),
        name="summed",
    )(*arrays, *after)


def final_kernel(terms, powers, *refs):
    out = refs[-1]
    users, blocks = out.shape[0], out.shape[2] // 128
    steps = users // 8
    scale = lax.rsqrt(add_up(refs, powers, 1)[0] + epsilon)
    total = add_up(refs, terms, 2 * blocks * steps)
    for half in range(2):
        for block in range(blocks):
            start = (half * blocks + block) * steps
            value = total[start:start + steps].reshape(users, 128)
            factor = scale[block:block + 1, :]
            value = jnp.where(factor > 0.0, value * factor, 0.0)
            out[:, half, block * 128:(block + 1) * 128] = value


def finish(arrays, terms, powers, users, columns):
    vmem = pl.BlockSpec(memory_space=pltpu.VMEM)
    return pl.pallas_call(
        functools.partial(final_kernel, terms, powers),
        out_shape=jax.ShapeDtypeStruct((users, 2, columns), jnp.float32),
        in_specs=[vmem] * len(arrays),
        out_specs=vmem,
        compiler_params=pltpu.CompilerParams(vmem_limit_bytes=8 * MIB),
        name="finish",
    )(*arrays)


def message_order(chips):
    steps = []
    for step in range(chips):
        size = 1 << (chips - 1 - step)
        first = (1 << chips) - 2 * size
        steps.append(list(range(first, first + size)))
    if chips < 3:
        return [(step, slots) for step, slots in enumerate(steps)]
    quarter, half = len(steps[0]) // 4, len(steps[1]) // 2
    parts = [steps[0][at * quarter:(at + 1) * quarter] for at in range(4)]
    order = [
        (0, parts[0]),
        (0, parts[2]),
        (1, steps[1][:half]),
        (0, parts[1] + parts[3]),
        (2, steps[2]),
        (1, steps[1][half:]),
    ]
    return order + [(step, steps[step]) for step in range(3, chips)]


def on_device(channel, precoder, visible, cluster):
    devices = lax.axis_size("ap")
    bits = devices.bit_length() - 1
    users, columns = channel.shape[3], precoder.shape[2]
    tiles = (users // 8) * (columns // 128) * 2
    flat = precoder.reshape(-1, columns)
    half = devices // 4

    def swap(value, bit):
        return lax.ppermute(value, "ap", [(i, i ^ (1 << bit)) for i in range(devices)])

    arrays = []
    terms = [[] for _ in range(2 * half)]
    powers = []

    def add(array, slots, power):
        for at, slot in enumerate(slots):
            terms[slot].append((len(arrays), at * tiles))
        if power:
            powers.append((len(arrays), len(slots) * tiles))
        arrays.append(array)

    def total(slots, power, cost=8192, after=()):
        jobs = [(list(terms[slot]), tiles) for slot in slots] + ([(list(powers), 1)] if power else [])
        used = sorted({array for parts, _ in jobs for array, _ in parts})
        jobs = [([(used.index(array), start) for array, start in parts], count) for parts, count in jobs]
        return summed([arrays[array] for array in used], jobs, cost, after)

    quarter = half // 4
    sent, kept, rows, weights, served = first_products(
        bits, quarter, visible, cluster.T, channel, flat
    )
    came = swap(sent, 0)
    add(sent, [], False)
    powers.append((0, quarter * tiles))
    add(kept, range(quarter), False)
    add(came, range(quarter), True)
    products = functools.partial(next_products, users, rows=rows, weights=weights, served=served)
    for at, (first, count) in enumerate(((quarter, 4 * quarter), (5 * quarter, 3 * quarter))):
        slots = range(first, first + count)
        come = swap(products(0, first, count, cost=COSTS[2 * at]), 0)
        add(products(1, first, count, cost=COSTS[2 * at + 1]), slots, False)
        add(come, slots, False)
    with_power = set()
    last = 2 * half - 1
    for number, (step, slots) in enumerate(message_order(bits - 1)):
        power = step not in with_power
        with_power.add(step)
        after = [now] if number in (3, 5) else []
        now = total(slots, power, COSTS[4 + number] if number < 6 else 8192, after)
        came = swap(now, step + 1)
        slots = [slot + (1 << (bits - 2 - step)) for slot in slots]
        add(came, slots, power)
    used = sorted({array for array, _ in terms[last] + powers})
    return finish(
        [arrays[array] for array in used],
        [(used.index(array), start) for array, start in terms[last]],
        [(used.index(array), start) for array, start in powers],
        users, columns,
    )


def solution(mesh):
    in_specs = (
        P(("parts", "ap"), None, None, None, None),
        P(None, ("parts", "ap"), None),
        P(("parts", "ap"), None),
        P("parts", None),
    )
    out_specs = P(("parts", "ap"), None, None)
    return jax.shard_map(
        on_device, mesh=mesh, in_specs=in_specs, out_specs=out_specs, check_vma=False
    )
```

```python
import functools

import jax
import jax.numpy as jnp
from jax import lax
from jax.experimental import pallas as pl
from jax.experimental.pallas import tpu as pltpu
from jax.sharding import PartitionSpec as P

epsilon = 1e-06
MIB = 1 << 20


COSTS = (8192, 64 * MIB, 65536 * MIB, 8192 * MIB) + (
    64 * MIB, 1024 * MIB, 1024 * MIB, 65536 * MIB, 1024 * MIB, 8192 * MIB
)


def chip_orders(bits):
    first = list(range(1, bits))
    second = list(first)
    if bits > 2:
        second[0], second[1] = second[1], second[0]
    return second, first


def place_of(group, me, core, bits):
    away = [1 - (((group ^ me) >> bit) & 1) for bit in range(1, bits)]
    if bits > 2:
        swapped = core == 0
        away[:2] = [jnp.where(swapped, away[1], away[0]), jnp.where(swapped, away[0], away[1])]
    place = 0
    for value in away:
        place = place * 2 + value
    return place


def write_products(users, rows, weights, served, out):
    slots, antennas = rows.shape[0] // users, rows.shape[1] // 2
    blocks, steps = weights.shape[1] // 128, users // 8
    group = max(size for size in range(1, 9) if slots % size == 0)
    for base in range(0, slots, group):
        plain = rows[base * users:(base + group) * users, :]
        turned = jnp.concatenate([-plain[:, antennas:], plain[:, :antennas]], axis=1)
        both = jnp.concatenate([plain, turned], axis=0)
        value = jnp.dot(both, weights, preferred_element_type=jnp.float32)
        value = jnp.where(served, value, 0.0)
        for half in range(2):
            for slot in range(group):
                top = (half * group + slot) * users
                for block in range(blocks):
                    piece = value[top:top + users, block * 128:(block + 1) * 128]
                    start = (((base + slot) * 2 + half) * blocks + block) * steps
                    out[start:start + steps] = piece.reshape(steps, 8, 128)


def power_tile(weights, served):
    wide = weights.astype(jnp.float32)
    power = jnp.sum(wide * wide, axis=0, keepdims=True)
    power = jnp.where(served, power, 0.0)
    blocks = power.shape[1] // 128
    pieces = [power[:, block * 128:(block + 1) * 128] for block in range(blocks)]
    return jnp.concatenate(pieces + [jnp.zeros((8 - blocks, 128), jnp.float32)], axis=0)


def first_kernel(
    bits, visible, cluster, channel, precoder,
    out, rows, weights, served,
    seen, names, raw, sems,
):
    me = lax.axis_index("ap")
    held, users, antennas = raw.shape[1], raw.shape[3], raw.shape[4]
    loads = [
        pltpu.make_async_copy(visible, seen, sems.at[0]),
        pltpu.make_async_copy(channel, raw, sems.at[1]),
        pltpu.make_async_copy(cluster, names, sems.at[2]),
        pltpu.make_async_copy(precoder, weights, sems.at[3]),
    ]
    for load in loads:
        load.start()
    rows[...] = jnp.zeros_like(rows)
    loads[0].wait()
    places = []
    for v in range(held):
        core = seen[0, v] & 1
        places.append((1 - (core ^ (me & 1)), place_of(seen[0, v], me, core, bits) * users))
    loads[1].wait()
    for v, (keep, place) in enumerate(places):
        at = pl.ds(pl.multiple_of(place, users), users)
        rows[keep, at, 0:antennas] = raw[0, v, 0]
        rows[keep, at, antennas:2 * antennas] = raw[0, v, 1]
    loads[2].wait()
    here = jnp.max((names[...] == me).astype(jnp.float32), axis=0, keepdims=True)
    served[...] = here
    loads[3].wait()
    mask = here > 0.0
    size = (out.shape[0] // (weights.shape[1] // 128) // 2) * 8
    write_products(users, rows.at[0, 0:size], weights[...], mask, out)
    out[out.shape[0] - 1] = power_tile(weights[...], mask)


def next_kernel(users, jobs, rows, weights, served, *outs):
    for (keep, first, slots), out in zip(jobs, outs):
        mine = rows.at[keep, first * users:(first + slots) * users]
        write_products(users, mine, weights[...], served[...] > 0.0, out)


def message(tiles):
    return jax.ShapeDtypeStruct((tiles, 8, 128), jnp.float32)


def estimate(size=8192):
    return pl.CostEstimate(flops=size, bytes_accessed=size, transcendentals=0)


def first_products(bits, first, visible, cluster, channel, precoder):
    users, antennas = channel.shape[3], channel.shape[4]
    columns = precoder.shape[1]
    slots = 1 << (bits - 1)
    tiles = first * (users // 8) * (columns // 128) * 2
    vmem = pl.BlockSpec(memory_space=pltpu.VMEM)
    hbm = pl.BlockSpec(memory_space=pltpu.HBM)
    operands = (visible, cluster, channel, precoder)
    return pl.pallas_call(
        functools.partial(first_kernel, bits),
        out_shape=(
            message(tiles + 1),
            jax.ShapeDtypeStruct((2, slots * users, 2 * antennas), jnp.bfloat16),
            jax.ShapeDtypeStruct(precoder.shape, jnp.bfloat16),
            jax.ShapeDtypeStruct((1, columns), jnp.float32),
        ),
        in_specs=[hbm] * 4,
        out_specs=(vmem,) * 4,
        scratch_shapes=[
            pltpu.SMEM(visible.shape, jnp.int32),
            pltpu.VMEM(cluster.shape, jnp.int32),
            pltpu.VMEM(channel.shape, jnp.bfloat16),
            pltpu.SemaphoreType.DMA((4,)),
        ],
        compiler_params=pltpu.CompilerParams(vmem_limit_bytes=52 * MIB if slots > 8 else 24 * MIB),
        cost_estimate=estimate(),
        name="first_products",
    )(*[pltpu.with_memory_space_constraint(operand, pltpu.HBM) for operand in operands])


def next_products(users, jobs, cost, rows, weights, served):
    vmem = pl.BlockSpec(memory_space=pltpu.VMEM)
    big = max(slots for _, _, slots in jobs) > 8
    tiles = (users // 8) * (weights.shape[1] // 128) * 2
    return pl.pallas_call(
        functools.partial(next_kernel, users, jobs),
        out_shape=[message(slots * tiles) for _, _, slots in jobs],
        in_specs=[vmem] * 3,
        out_specs=[vmem] * len(jobs),
        compiler_params=pltpu.CompilerParams(vmem_limit_bytes=48 * MIB if big else 16 * MIB),
        cost_estimate=estimate(cost),
        name="next_products",
    )(rows, weights, served)


def add_up(refs, terms, count):
    total = refs[terms[0][0]][terms[0][1]:terms[0][1] + count]
    for ref, start in terms[1:]:
        total = total + refs[ref][start:start + count]
    return total


def sum_kernel(jobs, *refs):
    at = 0
    for terms, count in jobs:
        refs[-1][at:at + count] = add_up(refs, terms, count)
        at += count


def summed(arrays, jobs, cost, after):
    size = sum(count for _, count in jobs)
    vmem = pl.BlockSpec(memory_space=pltpu.VMEM)
    return pl.pallas_call(
        functools.partial(sum_kernel, jobs),
        out_shape=message(size),
        in_specs=[vmem] * (len(arrays) + len(after)),
        out_specs=vmem,
        compiler_params=pltpu.CompilerParams(vmem_limit_bytes=8 * MIB),
        cost_estimate=estimate(cost),
        name="summed",
    )(*arrays, *after)


def final_kernel(terms, powers, *refs):
    out = refs[-1]
    users, blocks = out.shape[0], out.shape[2] // 128
    steps = users // 8
    scale = lax.rsqrt(add_up(refs, powers, 1)[0] + epsilon)
    total = add_up(refs, terms, 2 * blocks * steps)
    for half in range(2):
        for block in range(blocks):
            start = (half * blocks + block) * steps
            value = total[start:start + steps].reshape(users, 128)
            factor = scale[block:block + 1, :]
            value = jnp.where(factor > 0.0, value * factor, 0.0)
            out[:, half, block * 128:(block + 1) * 128] = value


def finish(arrays, terms, powers, users, columns):
    vmem = pl.BlockSpec(memory_space=pltpu.VMEM)
    return pl.pallas_call(
        functools.partial(final_kernel, terms, powers),
        out_shape=jax.ShapeDtypeStruct((users, 2, columns), jnp.float32),
        in_specs=[vmem] * len(arrays),
        out_specs=vmem,
        compiler_params=pltpu.CompilerParams(vmem_limit_bytes=8 * MIB),
        name="finish",
    )(*arrays)


def message_order(chips):
    steps = []
    for step in range(chips):
        size = 1 << (chips - 1 - step)
        first = (1 << chips) - 2 * size
        steps.append(list(range(first, first + size)))
    if chips < 3:
        return [(step, slots) for step, slots in enumerate(steps)]
    quarter, half = len(steps[0]) // 4, len(steps[1]) // 2
    parts = [steps[0][at * quarter:(at + 1) * quarter] for at in range(4)]
    order = [
        (0, parts[0]),
        (0, parts[2]),
        (1, steps[1][:half]),
        (0, parts[1] + parts[3]),
        (2, steps[2]),
        (1, steps[1][half:]),
    ]
    return order + [(step, steps[step]) for step in range(3, chips)]


def on_device(channel, precoder, visible, cluster):
    devices = lax.axis_size("ap")
    bits = devices.bit_length() - 1
    users, columns = channel.shape[3], precoder.shape[2]
    tiles = (users // 8) * (columns // 128) * 2
    orders = chip_orders(bits)
    flat = precoder.reshape(-1, columns)
    half = devices // 4

    def swap(value, bit_of):
        return lax.ppermute(value, "ap", [(i, i ^ (1 << bit_of[i & 1])) for i in range(devices)])

    arrays = []
    terms = [[] for _ in range(2 * half)]
    powers = []

    def add(array, slots, power):
        for at, slot in enumerate(slots):
            terms[slot].append((len(arrays), at * tiles))
        if power:
            powers.append((len(arrays), len(slots) * tiles))
        arrays.append(array)

    def total(slots, power, cost=8192, after=()):
        jobs = [(list(terms[slot]), tiles) for slot in slots] + ([(list(powers), 1)] if power else [])
        used = sorted({array for parts, _ in jobs for array, _ in parts})
        jobs = [([(used.index(array), start) for array, start in parts], count) for parts, count in jobs]
        return summed([arrays[array] for array in used], jobs, cost, after)

    quarter = half // 4
    sent, rows, weights, served = first_products(bits, quarter, visible, cluster.T, channel, flat)
    came = swap(sent, (0, 0))
    add(sent, [], False)
    powers.append((0, quarter * tiles))
    products = functools.partial(next_products, users, rows=rows, weights=weights, served=served)
    first, count = quarter, 4 * quarter
    send, kept = products(((0, first, count), (1, 0, quarter)), cost=COSTS[0])
    add(kept, range(quarter), False)
    add(came, range(quarter), True)
    come = swap(send, (0, 0))
    add(products(((1, first, count),), cost=COSTS[1])[0], range(first, first + count), False)
    add(come, range(first, first + count), False)
    first, count = 5 * quarter, 3 * quarter
    come = swap(products(((0, first, count),), cost=COSTS[2])[0], (0, 0))
    add(products(((1, first, count),), cost=COSTS[3])[0], range(first, first + count), False)
    add(come, range(first, first + count), False)
    with_power = set()
    last = 2 * half - 1
    for number, (step, slots) in enumerate(message_order(bits - 1)):
        power = step not in with_power
        with_power.add(step)
        after = [now] if number in (3, 5) else []
        now = total(slots, power, COSTS[4 + number] if number < 6 else 8192, after)
        came = swap(now, (orders[0][step], orders[1][step]))
        slots = [slot + (1 << (bits - 2 - step)) for slot in slots]
        add(came, slots, power)
    used = sorted({array for array, _ in terms[last] + powers})
    return finish(
        [arrays[array] for array in used],
        [(used.index(array), start) for array, start in terms[last]],
        [(used.index(array), start) for array, start in powers],
        users, columns,
    )


def solution(mesh):
    in_specs = (
        P(("parts", "ap"), None, None, None, None),
        P(None, ("parts", "ap"), None),
        P(("parts", "ap"), None),
        P("parts", None),
    )
    out_specs = P(("parts", "ap"), None, None)
    return jax.shard_map(
        on_device, mesh=mesh, in_specs=in_specs, out_specs=out_specs, check_vma=False
    )
```

```python
import functools

import jax
import jax.numpy as jnp
from jax import lax
from jax.experimental import pallas as pl
from jax.experimental.pallas import tpu as pltpu
from jax.sharding import PartitionSpec as P

epsilon = 1e-06
MIB = 1 << 20


COSTS = (8192 * MIB, 65536 * MIB, 64 * MIB, 64 * MIB) + (
    1024 * MIB, 64 * MIB, 64 * MIB, 65536 * MIB, 65536 * MIB, 1024 * MIB
)


def chip_orders(bits):
    first = list(range(1, bits))
    second = list(first)
    if bits > 2:
        second[0], second[1] = second[1], second[0]
    return second, first


def place_of(group, me, core, bits):
    away = [1 - (((group ^ me) >> bit) & 1) for bit in range(1, bits)]
    if bits > 2:
        swapped = core == 0
        away[:2] = [jnp.where(swapped, away[1], away[0]), jnp.where(swapped, away[0], away[1])]
    place = 0
    for value in away:
        place = place * 2 + value
    return place


def write_products(users, rows, weights, served, out):
    slots, antennas = rows.shape[0] // users, rows.shape[1] // 2
    blocks, steps = weights.shape[1] // 128, users // 8
    group = max(size for size in range(1, 9) if slots % size == 0)
    for base in range(0, slots, group):
        plain = rows[base * users:(base + group) * users, :]
        turned = jnp.concatenate([-plain[:, antennas:], plain[:, :antennas]], axis=1)
        both = jnp.concatenate([plain, turned], axis=0)
        value = jnp.dot(both, weights, preferred_element_type=jnp.float32)
        value = jnp.where(served, value, 0.0)
        for half in range(2):
            for slot in range(group):
                top = (half * group + slot) * users
                for block in range(blocks):
                    piece = value[top:top + users, block * 128:(block + 1) * 128]
                    start = (((base + slot) * 2 + half) * blocks + block) * steps
                    out[start:start + steps] = piece.reshape(steps, 8, 128)


def power_tile(weights, served):
    wide = weights.astype(jnp.float32)
    power = jnp.sum(wide * wide, axis=0, keepdims=True)
    power = jnp.where(served, power, 0.0)
    blocks = power.shape[1] // 128
    pieces = [power[:, block * 128:(block + 1) * 128] for block in range(blocks)]
    return jnp.concatenate(pieces + [jnp.zeros((8 - blocks, 128), jnp.float32)], axis=0)


def first_kernel(
    bits, visible, cluster, channel, precoder,
    out, rows, weights, served,
    seen, names, raw, sems,
):
    me = lax.axis_index("ap")
    held, users, antennas = raw.shape[1], raw.shape[3], raw.shape[4]
    loads = [
        pltpu.make_async_copy(visible, seen, sems.at[0]),
        pltpu.make_async_copy(channel, raw, sems.at[1]),
        pltpu.make_async_copy(cluster, names, sems.at[2]),
        pltpu.make_async_copy(precoder, weights, sems.at[3]),
    ]
    for load in loads:
        load.start()
    rows[...] = jnp.zeros_like(rows)
    loads[0].wait()
    places = []
    for v in range(held):
        core = seen[0, v] & 1
        places.append((1 - (core ^ (me & 1)), place_of(seen[0, v], me, core, bits) * users))
    loads[1].wait()
    for v, (keep, place) in enumerate(places):
        at = pl.ds(pl.multiple_of(place, users), users)
        rows[keep, at, 0:antennas] = raw[0, v, 0]
        rows[keep, at, antennas:2 * antennas] = raw[0, v, 1]
    loads[2].wait()
    here = jnp.max((names[...] == me).astype(jnp.float32), axis=0, keepdims=True)
    served[...] = here
    loads[3].wait()
    mask = here > 0.0
    size = (out.shape[0] // (weights.shape[1] // 128) // 2) * 8
    write_products(users, rows.at[0, 0:size], weights[...], mask, out)
    out[out.shape[0] - 1] = power_tile(weights[...], mask)


def next_kernel(users, jobs, rows, weights, served, *outs):
    for (keep, first, slots), out in zip(jobs, outs):
        mine = rows.at[keep, first * users:(first + slots) * users]
        write_products(users, mine, weights[...], served[...] > 0.0, out)


def message(tiles):
    return jax.ShapeDtypeStruct((tiles, 8, 128), jnp.float32)


def estimate(size=8192):
    return pl.CostEstimate(flops=size, bytes_accessed=size, transcendentals=0)


def first_products(bits, first, visible, cluster, channel, precoder):
    users, antennas = channel.shape[3], channel.shape[4]
    columns = precoder.shape[1]
    slots = 1 << (bits - 1)
    tiles = first * (users // 8) * (columns // 128) * 2
    vmem = pl.BlockSpec(memory_space=pltpu.VMEM)
    hbm = pl.BlockSpec(memory_space=pltpu.HBM)
    operands = (visible, cluster, channel, precoder)
    return pl.pallas_call(
        functools.partial(first_kernel, bits),
        out_shape=(
            message(tiles + 1),
            jax.ShapeDtypeStruct((2, slots * users, 2 * antennas), jnp.bfloat16),
            jax.ShapeDtypeStruct(precoder.shape, jnp.bfloat16),
            jax.ShapeDtypeStruct((1, columns), jnp.float32),
        ),
        in_specs=[hbm] * 4,
        out_specs=(vmem,) * 4,
        scratch_shapes=[
            pltpu.SMEM(visible.shape, jnp.int32),
            pltpu.VMEM(cluster.shape, jnp.int32),
            pltpu.VMEM(channel.shape, jnp.bfloat16),
            pltpu.SemaphoreType.DMA((4,)),
        ],
        compiler_params=pltpu.CompilerParams(vmem_limit_bytes=52 * MIB if slots > 8 else 24 * MIB),
        cost_estimate=estimate(),
        name="first_products",
    )(*[pltpu.with_memory_space_constraint(operand, pltpu.HBM) for operand in operands])


def next_products(users, jobs, cost, rows, weights, served):
    vmem = pl.BlockSpec(memory_space=pltpu.VMEM)
    big = max(slots for _, _, slots in jobs) > 8
    tiles = (users // 8) * (weights.shape[1] // 128) * 2
    return pl.pallas_call(
        functools.partial(next_kernel, users, jobs),
        out_shape=[message(slots * tiles) for _, _, slots in jobs],
        in_specs=[vmem] * 3,
        out_specs=[vmem] * len(jobs),
        compiler_params=pltpu.CompilerParams(vmem_limit_bytes=48 * MIB if big else 16 * MIB),
        cost_estimate=estimate(cost),
        name="next_products",
    )(rows, weights, served)


def add_up(refs, terms, count):
    total = refs[terms[0][0]][terms[0][1]:terms[0][1] + count]
    for ref, start in terms[1:]:
        total = total + refs[ref][start:start + count]
    return total


def sum_kernel(jobs, *refs):
    at = 0
    for terms, count in jobs:
        refs[-1][at:at + count] = add_up(refs, terms, count)
        at += count


def summed(arrays, jobs, cost, after):
    size = sum(count for _, count in jobs)
    vmem = pl.BlockSpec(memory_space=pltpu.VMEM)
    return pl.pallas_call(
        functools.partial(sum_kernel, jobs),
        out_shape=message(size),
        in_specs=[vmem] * (len(arrays) + len(after)),
        out_specs=vmem,
        compiler_params=pltpu.CompilerParams(vmem_limit_bytes=8 * MIB),
        cost_estimate=estimate(cost),
        name="summed",
    )(*arrays, *after)


def final_kernel(terms, powers, *refs):
    out = refs[-1]
    users, blocks = out.shape[0], out.shape[2] // 128
    steps = users // 8
    scale = lax.rsqrt(add_up(refs, powers, 1)[0] + epsilon)
    total = add_up(refs, terms, 2 * blocks * steps)
    for half in range(2):
        for block in range(blocks):
            start = (half * blocks + block) * steps
            value = total[start:start + steps].reshape(users, 128)
            factor = scale[block:block + 1, :]
            value = jnp.where(factor > 0.0, value * factor, 0.0)
            out[:, half, block * 128:(block + 1) * 128] = value


def finish(arrays, terms, powers, users, columns):
    vmem = pl.BlockSpec(memory_space=pltpu.VMEM)
    return pl.pallas_call(
        functools.partial(final_kernel, terms, powers),
        out_shape=jax.ShapeDtypeStruct((users, 2, columns), jnp.float32),
        in_specs=[vmem] * len(arrays),
        out_specs=vmem,
        compiler_params=pltpu.CompilerParams(vmem_limit_bytes=8 * MIB),
        name="finish",
    )(*arrays)


def message_order(chips):
    steps = []
    for step in range(chips):
        size = 1 << (chips - 1 - step)
        first = (1 << chips) - 2 * size
        steps.append(list(range(first, first + size)))
    if chips < 3:
        return [(step, slots) for step, slots in enumerate(steps)]
    quarter, half = len(steps[0]) // 4, len(steps[1]) // 2
    parts = [steps[0][at * quarter:(at + 1) * quarter] for at in range(4)]
    order = [
        (0, parts[0]),
        (0, parts[2]),
        (1, steps[1][:half]),
        (0, parts[1] + parts[3]),
        (2, steps[2]),
        (1, steps[1][half:]),
    ]
    return order + [(step, steps[step]) for step in range(3, chips)]


def on_device(channel, precoder, visible, cluster):
    devices = lax.axis_size("ap")
    bits = devices.bit_length() - 1
    users, columns = channel.shape[3], precoder.shape[2]
    tiles = (users // 8) * (columns // 128) * 2
    orders = chip_orders(bits)
    flat = precoder.reshape(-1, columns)
    half = devices // 4

    def swap(value, bit_of):
        return lax.ppermute(value, "ap", [(i, i ^ (1 << bit_of[i & 1])) for i in range(devices)])

    arrays = []
    terms = [[] for _ in range(2 * half)]
    powers = []

    def add(array, slots, power):
        for at, slot in enumerate(slots):
            terms[slot].append((len(arrays), at * tiles))
        if power:
            powers.append((len(arrays), len(slots) * tiles))
        arrays.append(array)

    def total(slots, power, cost=8192, after=()):
        jobs = [(list(terms[slot]), tiles) for slot in slots] + ([(list(powers), 1)] if power else [])
        used = sorted({array for parts, _ in jobs for array, _ in parts})
        jobs = [([(used.index(array), start) for array, start in parts], count) for parts, count in jobs]
        return summed([arrays[array] for array in used], jobs, cost, after)

    quarter = half // 4
    sent, rows, weights, served = first_products(bits, quarter, visible, cluster.T, channel, flat)
    came = swap(sent, (0, 0))
    add(sent, [], False)
    powers.append((0, quarter * tiles))
    products = functools.partial(next_products, users, rows=rows, weights=weights, served=served)
    first, count = quarter, 4 * quarter
    send, kept = products(((0, first, count), (1, 0, quarter)), cost=COSTS[0])
    add(kept, range(quarter), False)
    add(came, range(quarter), True)
    come = swap(send, (0, 0))
    add(products(((1, first, count),), cost=COSTS[1])[0], range(first, first + count), False)
    add(come, range(first, first + count), False)
    first, count = 5 * quarter, 3 * quarter
    come = swap(products(((0, first, count),), cost=COSTS[2])[0], (0, 0))
    add(products(((1, first, count),), cost=COSTS[3])[0], range(first, first + count), False)
    add(come, range(first, first + count), False)
    with_power = set()
    last = 2 * half - 1
    for number, (step, slots) in enumerate(message_order(bits - 1)):
        power = step not in with_power
        with_power.add(step)
        after = [now, came_second] if number == 3 else [now] if number == 5 else []
        now = total(slots, power, COSTS[4 + number] if number < 6 else 8192, after)
        came = swap(now, (orders[0][step], orders[1][step]))
        if number == 1:
            came_second = came
        slots = [slot + (1 << (bits - 2 - step)) for slot in slots]
        add(came, slots, power)
    used = sorted({array for array, _ in terms[last] + powers})
    return finish(
        [arrays[array] for array in used],
        [(used.index(array), start) for array, start in terms[last]],
        [(used.index(array), start) for array, start in powers],
        users, columns,
    )


def solution(mesh):
    in_specs = (
        P(("parts", "ap"), None, None, None, None),
        P(None, ("parts", "ap"), None),
        P(("parts", "ap"), None),
        P("parts", None),
    )
    out_specs = P(("parts", "ap"), None, None)
    return jax.shard_map(
        on_device, mesh=mesh, in_specs=in_specs, out_specs=out_specs, check_vma=False
    )
```

```python
import functools

import jax
import jax.numpy as jnp
from jax import lax
from jax.experimental import pallas as pl
from jax.experimental.pallas import tpu as pltpu
from jax.sharding import PartitionSpec as P

epsilon = 1e-06
MIB = 1 << 20
LOADS = 4


COSTS = (8192, 64 * MIB, 65536 * MIB, 8192 * MIB) + (
    64 * MIB, 1024 * MIB, 1024 * MIB, 65536 * MIB, 1024 * MIB, 8192 * MIB
)


def chip_orders(bits):
    first = list(range(1, bits))
    second = list(first)
    if bits > 2:
        second[0], second[1] = second[1], second[0]
    return second, first


def place_of(group, me, core, bits):
    away = [1 - (((group ^ me) >> bit) & 1) for bit in range(1, bits)]
    if bits > 2:
        swapped = core == 0
        away[:2] = [jnp.where(swapped, away[1], away[0]), jnp.where(swapped, away[0], away[1])]
    place = 0
    for value in away:
        place = place * 2 + value
    return place


def left_side(rows):
    antennas = rows.shape[1] // 2
    turned = jnp.concatenate([-rows[:, antennas:], rows[:, :antennas]], axis=1)
    return jnp.concatenate([rows, turned], axis=0)


def put_products(value, served, users, base, out):
    blocks, steps = value.shape[1] // 128, users // 8
    group = value.shape[0] // users // 2
    value = jnp.where(served, value, 0.0)
    for half in range(2):
        for slot in range(group):
            top = (half * group + slot) * users
            for block in range(blocks):
                piece = value[top:top + users, block * 128:(block + 1) * 128]
                start = (((base + slot) * 2 + half) * blocks + block) * steps
                out[start:start + steps] = piece.reshape(steps, 8, 128)


def write_products(users, rows, weights, served, out):
    slots = rows.shape[0] // users
    group = max(size for size in range(1, 9) if slots % size == 0)
    for base in range(0, slots, group):
        both = left_side(rows[base * users:(base + group) * users, :])
        value = jnp.dot(both, weights, preferred_element_type=jnp.float32)
        put_products(value, served, users, base, out)


def square_sum(weights):
    wide = weights.astype(jnp.float32)
    return jnp.sum(wide * wide, axis=0, keepdims=True)


def power_tile(power, served):
    power = jnp.where(served, power, 0.0)
    blocks = power.shape[1] // 128
    pieces = [power[:, block * 128:(block + 1) * 128] for block in range(blocks)]
    return jnp.concatenate(pieces + [jnp.zeros((8 - blocks, 128), jnp.float32)], axis=0)


def first_kernel(
    bits, visible, cluster, channel, precoder,
    out, rows, weights, served,
    seen, names, raw, sems,
):
    me = lax.axis_index("ap")
    held, users, antennas = raw.shape[1], raw.shape[3], raw.shape[4]
    loads = [
        pltpu.make_async_copy(visible, seen, sems.at[0]),
        pltpu.make_async_copy(channel, raw, sems.at[1]),
        pltpu.make_async_copy(cluster, names, sems.at[2]),
    ]
    depth = weights.shape[0] // LOADS
    for part in range(LOADS):
        at = pl.ds(part * depth, depth)
        loads.append(pltpu.make_async_copy(precoder.at[at], weights.at[at], sems.at[3 + part]))
    for load in loads:
        load.start()
    rows[...] = jnp.zeros_like(rows)
    loads[0].wait()
    places = []
    for v in range(held):
        core = seen[0, v] & 1
        places.append((1 - (core ^ (me & 1)), place_of(seen[0, v], me, core, bits) * users))
    loads[1].wait()
    for v, (keep, place) in enumerate(places):
        at = pl.ds(pl.multiple_of(place, users), users)
        rows[keep, at, 0:antennas] = raw[0, v, 0]
        rows[keep, at, antennas:2 * antennas] = raw[0, v, 1]
    loads[2].wait()
    here = jnp.max((names[...] == me).astype(jnp.float32), axis=0, keepdims=True)
    served[...] = here
    size = (out.shape[0] // (weights.shape[1] // 128) // 2) * 8
    both = left_side(rows[0, 0:size, :])
    value = power = None
    for part in range(LOADS):
        loads[3 + part].wait()
        at = slice(part * depth, (part + 1) * depth)
        block = weights[at, :]
        term = jnp.dot(both[:, at], block, preferred_element_type=jnp.float32)
        square = square_sum(block)
        value = term if value is None else value + term
        power = square if power is None else power + square
    put_products(value, here > 0.0, users, 0, out)
    out[out.shape[0] - 1] = power_tile(power, here > 0.0)


def next_kernel(users, jobs, rows, weights, served, *outs):
    for (keep, first, slots), out in zip(jobs, outs):
        mine = rows.at[keep, first * users:(first + slots) * users]
        write_products(users, mine, weights[...], served[...] > 0.0, out)


def message(tiles):
    return jax.ShapeDtypeStruct((tiles, 8, 128), jnp.float32)


def estimate(size=8192):
    return pl.CostEstimate(flops=size, bytes_accessed=size, transcendentals=0)


def first_products(bits, first, visible, cluster, channel, precoder):
    users, antennas = channel.shape[3], channel.shape[4]
    columns = precoder.shape[1]
    slots = 1 << (bits - 1)
    tiles = first * (users // 8) * (columns // 128) * 2
    vmem = pl.BlockSpec(memory_space=pltpu.VMEM)
    hbm = pl.BlockSpec(memory_space=pltpu.HBM)
    operands = (visible, cluster, channel, precoder)
    return pl.pallas_call(
        functools.partial(first_kernel, bits),
        out_shape=(
            message(tiles + 1),
            jax.ShapeDtypeStruct((2, slots * users, 2 * antennas), jnp.bfloat16),
            jax.ShapeDtypeStruct(precoder.shape, jnp.bfloat16),
            jax.ShapeDtypeStruct((1, columns), jnp.float32),
        ),
        in_specs=[hbm] * 4,
        out_specs=(vmem,) * 4,
        scratch_shapes=[
            pltpu.SMEM(visible.shape, jnp.int32),
            pltpu.VMEM(cluster.shape, jnp.int32),
            pltpu.VMEM(channel.shape, jnp.bfloat16),
            pltpu.SemaphoreType.DMA((3 + LOADS,)),
        ],
        compiler_params=pltpu.CompilerParams(vmem_limit_bytes=52 * MIB if slots > 8 else 24 * MIB),
        cost_estimate=estimate(),
        name="first_products",
    )(*[pltpu.with_memory_space_constraint(operand, pltpu.HBM) for operand in operands])


def next_products(users, jobs, cost, rows, weights, served):
    vmem = pl.BlockSpec(memory_space=pltpu.VMEM)
    big = max(slots for _, _, slots in jobs) > 8
    tiles = (users // 8) * (weights.shape[1] // 128) * 2
    return pl.pallas_call(
        functools.partial(next_kernel, users, jobs),
        out_shape=[message(slots * tiles) for _, _, slots in jobs],
        in_specs=[vmem] * 3,
        out_specs=[vmem] * len(jobs),
        compiler_params=pltpu.CompilerParams(vmem_limit_bytes=48 * MIB if big else 16 * MIB),
        cost_estimate=estimate(cost),
        name="next_products",
    )(rows, weights, served)


def add_up(refs, terms, count):
    total = refs[terms[0][0]][terms[0][1]:terms[0][1] + count]
    for ref, start in terms[1:]:
        total = total + refs[ref][start:start + count]
    return total


def sum_kernel(jobs, *refs):
    at = 0
    for terms, count in jobs:
        refs[-1][at:at + count] = add_up(refs, terms, count)
        at += count


def summed(arrays, jobs, cost, after):
    size = sum(count for _, count in jobs)
    vmem = pl.BlockSpec(memory_space=pltpu.VMEM)
    return pl.pallas_call(
        functools.partial(sum_kernel, jobs),
        out_shape=message(size),
        in_specs=[vmem] * (len(arrays) + len(after)),
        out_specs=vmem,
        compiler_params=pltpu.CompilerParams(vmem_limit_bytes=8 * MIB),
        cost_estimate=estimate(cost),
        name="summed",
    )(*arrays, *after)


def final_kernel(terms, powers, *refs):
    out = refs[-1]
    users, blocks = out.shape[0], out.shape[2] // 128
    steps = users // 8
    scale = lax.rsqrt(add_up(refs, powers, 1)[0] + epsilon)
    total = add_up(refs, terms, 2 * blocks * steps)
    for half in range(2):
        for block in range(blocks):
            start = (half * blocks + block) * steps
            value = total[start:start + steps].reshape(users, 128)
            factor = scale[block:block + 1, :]
            value = jnp.where(factor > 0.0, value * factor, 0.0)
            out[:, half, block * 128:(block + 1) * 128] = value


def finish(arrays, terms, powers, users, columns):
    vmem = pl.BlockSpec(memory_space=pltpu.VMEM)
    return pl.pallas_call(
        functools.partial(final_kernel, terms, powers),
        out_shape=jax.ShapeDtypeStruct((users, 2, columns), jnp.float32),
        in_specs=[vmem] * len(arrays),
        out_specs=vmem,
        compiler_params=pltpu.CompilerParams(vmem_limit_bytes=8 * MIB),
        name="finish",
    )(*arrays)


def message_order(chips):
    steps = []
    for step in range(chips):
        size = 1 << (chips - 1 - step)
        first = (1 << chips) - 2 * size
        steps.append(list(range(first, first + size)))
    if chips < 3:
        return [(step, slots) for step, slots in enumerate(steps)]
    quarter, half = len(steps[0]) // 4, len(steps[1]) // 2
    parts = [steps[0][at * quarter:(at + 1) * quarter] for at in range(4)]
    order = [
        (0, parts[0]),
        (0, parts[2]),
        (1, steps[1][:half]),
        (0, parts[1] + parts[3]),
        (2, steps[2]),
        (1, steps[1][half:]),
    ]
    return order + [(step, steps[step]) for step in range(3, chips)]


def on_device(channel, precoder, visible, cluster):
    devices = lax.axis_size("ap")
    bits = devices.bit_length() - 1
    users, columns = channel.shape[3], precoder.shape[2]
    tiles = (users // 8) * (columns // 128) * 2
    orders = chip_orders(bits)
    flat = precoder.reshape(-1, columns)
    half = devices // 4

    def swap(value, bit_of):
        return lax.ppermute(value, "ap", [(i, i ^ (1 << bit_of[i & 1])) for i in range(devices)])

    arrays = []
    terms = [[] for _ in range(2 * half)]
    powers = []

    def add(array, slots, power):
        for at, slot in enumerate(slots):
            terms[slot].append((len(arrays), at * tiles))
        if power:
            powers.append((len(arrays), len(slots) * tiles))
        arrays.append(array)

    def total(slots, power, cost=8192, after=()):
        jobs = [(list(terms[slot]), tiles) for slot in slots] + ([(list(powers), 1)] if power else [])
        used = sorted({array for parts, _ in jobs for array, _ in parts})
        jobs = [([(used.index(array), start) for array, start in parts], count) for parts, count in jobs]
        return summed([arrays[array] for array in used], jobs, cost, after)

    quarter = half // 4
    sent, rows, weights, served = first_products(bits, quarter, visible, cluster.T, channel, flat)
    came = swap(sent, (0, 0))
    add(sent, [], False)
    powers.append((0, quarter * tiles))
    products = functools.partial(next_products, users, rows=rows, weights=weights, served=served)
    first, count = quarter, 4 * quarter
    send, kept = products(((0, first, count), (1, 0, quarter)), cost=COSTS[0])
    add(kept, range(quarter), False)
    add(came, range(quarter), True)
    come = swap(send, (0, 0))
    add(products(((1, first, count),), cost=COSTS[1])[0], range(first, first + count), False)
    add(come, range(first, first + count), False)
    first, count = 5 * quarter, 3 * quarter
    come = swap(products(((0, first, count),), cost=COSTS[2])[0], (0, 0))
    add(products(((1, first, count),), cost=COSTS[3])[0], range(first, first + count), False)
    add(come, range(first, first + count), False)
    with_power = set()
    last = 2 * half - 1
    for number, (step, slots) in enumerate(message_order(bits - 1)):
        power = step not in with_power
        with_power.add(step)
        after = [now] if number in (3, 5) else []
        now = total(slots, power, COSTS[4 + number] if number < 6 else 8192, after)
        came = swap(now, (orders[0][step], orders[1][step]))
        slots = [slot + (1 << (bits - 2 - step)) for slot in slots]
        add(came, slots, power)
    used = sorted({array for array, _ in terms[last] + powers})
    return finish(
        [arrays[array] for array in used],
        [(used.index(array), start) for array, start in terms[last]],
        [(used.index(array), start) for array, start in powers],
        users, columns,
    )


def solution(mesh):
    in_specs = (
        P(("parts", "ap"), None, None, None, None),
        P(None, ("parts", "ap"), None),
        P(("parts", "ap"), None),
        P("parts", None),
    )
    out_specs = P(("parts", "ap"), None, None)
    return jax.shard_map(
        on_device, mesh=mesh, in_specs=in_specs, out_specs=out_specs, check_vma=False
    )
```

```python
import functools

import jax
import jax.numpy as jnp
from jax import lax
from jax.experimental import pallas as pl
from jax.experimental.pallas import tpu as pltpu
from jax.sharding import PartitionSpec as P

epsilon = 1e-06
MIB = 1 << 20
LOADS = 4


COSTS = (64 * MIB, 8192 * MIB, 64 * MIB, 65536 * MIB) + (
    1024 * MIB, 64 * MIB, 64 * MIB, 64 * MIB, 8192 * MIB, 1024 * MIB
)


def chip_orders(bits):
    first = list(range(1, bits))
    second = list(first)
    if bits > 2:
        second[0], second[1] = second[1], second[0]
    return second, first


def place_of(group, me, core, bits):
    away = [1 - (((group ^ me) >> bit) & 1) for bit in range(1, bits)]
    if bits > 2:
        swapped = core == 0
        away[:2] = [jnp.where(swapped, away[1], away[0]), jnp.where(swapped, away[0], away[1])]
    place = 0
    for value in away:
        place = place * 2 + value
    return place


def left_side(rows):
    antennas = rows.shape[1] // 2
    turned = jnp.concatenate([-rows[:, antennas:], rows[:, :antennas]], axis=1)
    return jnp.concatenate([rows, turned], axis=0)


def put_products(value, served, users, base, out):
    blocks, steps = value.shape[1] // 128, users // 8
    group = value.shape[0] // users // 2
    value = jnp.where(served, value, 0.0)
    for half in range(2):
        for slot in range(group):
            top = (half * group + slot) * users
            for block in range(blocks):
                piece = value[top:top + users, block * 128:(block + 1) * 128]
                start = (((base + slot) * 2 + half) * blocks + block) * steps
                out[start:start + steps] = piece.reshape(steps, 8, 128)


def write_products(users, rows, weights, served, out):
    slots = rows.shape[0] // users
    group = max(size for size in range(1, 9) if slots % size == 0)
    for base in range(0, slots, group):
        both = left_side(rows[base * users:(base + group) * users, :])
        value = jnp.dot(both, weights, preferred_element_type=jnp.float32)
        put_products(value, served, users, base, out)


def square_sum(weights):
    wide = weights.astype(jnp.float32)
    return jnp.sum(wide * wide, axis=0, keepdims=True)


def power_tile(power, served):
    power = jnp.where(served, power, 0.0)
    blocks = power.shape[1] // 128
    pieces = [power[:, block * 128:(block + 1) * 128] for block in range(blocks)]
    return jnp.concatenate(pieces + [jnp.zeros((8 - blocks, 128), jnp.float32)], axis=0)


def first_kernel(
    bits, visible, cluster, channel, precoder,
    out, rows, weights, served,
    seen, names, raw, sems,
):
    me = lax.axis_index("ap")
    held, users, antennas = raw.shape[1], raw.shape[3], raw.shape[4]
    loads = [
        pltpu.make_async_copy(visible, seen, sems.at[0]),
        pltpu.make_async_copy(channel, raw, sems.at[1]),
        pltpu.make_async_copy(cluster, names, sems.at[2]),
    ]
    depth = weights.shape[0] // LOADS
    for part in range(LOADS):
        at = pl.ds(part * depth, depth)
        loads.append(pltpu.make_async_copy(precoder.at[at], weights.at[at], sems.at[3 + part]))
    for load in loads:
        load.start()
    rows[...] = jnp.zeros_like(rows)
    loads[0].wait()
    places = []
    for v in range(held):
        core = seen[0, v] & 1
        places.append((1 - (core ^ (me & 1)), place_of(seen[0, v], me, core, bits) * users))
    loads[1].wait()
    for v, (keep, place) in enumerate(places):
        at = pl.ds(pl.multiple_of(place, users), users)
        rows[keep, at, 0:antennas] = raw[0, v, 0]
        rows[keep, at, antennas:2 * antennas] = raw[0, v, 1]
    loads[2].wait()
    here = jnp.max((names[...] == me).astype(jnp.float32), axis=0, keepdims=True)
    served[...] = here
    size = (out.shape[0] // (weights.shape[1] // 128) // 2) * 8
    both = left_side(rows[0, 0:size, :])
    value = power = None
    for part in range(LOADS):
        loads[3 + part].wait()
        at = slice(part * depth, (part + 1) * depth)
        block = weights[at, :]
        term = jnp.dot(both[:, at], block, preferred_element_type=jnp.float32)
        square = square_sum(block)
        value = term if value is None else value + term
        power = square if power is None else power + square
    put_products(value, here > 0.0, users, 0, out)
    out[out.shape[0] - 1] = power_tile(power, here > 0.0)


def next_kernel(users, jobs, rows, weights, served, *refs):
    for (keep, first, slots), out in zip(jobs, refs[-len(jobs):]):
        mine = rows.at[keep, first * users:(first + slots) * users]
        write_products(users, mine, weights[...], served[...] > 0.0, out)


def message(tiles):
    return jax.ShapeDtypeStruct((tiles, 8, 128), jnp.float32)


def estimate(size=8192):
    return pl.CostEstimate(flops=size, bytes_accessed=size, transcendentals=0)


def first_products(bits, first, visible, cluster, channel, precoder):
    users, antennas = channel.shape[3], channel.shape[4]
    columns = precoder.shape[1]
    slots = 1 << (bits - 1)
    tiles = first * (users // 8) * (columns // 128) * 2
    vmem = pl.BlockSpec(memory_space=pltpu.VMEM)
    hbm = pl.BlockSpec(memory_space=pltpu.HBM)
    operands = (visible, cluster, channel, precoder)
    return pl.pallas_call(
        functools.partial(first_kernel, bits),
        out_shape=(
            message(tiles + 1),
            jax.ShapeDtypeStruct((2, slots * users, 2 * antennas), jnp.bfloat16),
            jax.ShapeDtypeStruct(precoder.shape, jnp.bfloat16),
            jax.ShapeDtypeStruct((1, columns), jnp.float32),
        ),
        in_specs=[hbm] * 4,
        out_specs=(vmem,) * 4,
        scratch_shapes=[
            pltpu.SMEM(visible.shape, jnp.int32),
            pltpu.VMEM(cluster.shape, jnp.int32),
            pltpu.VMEM(channel.shape, jnp.bfloat16),
            pltpu.SemaphoreType.DMA((3 + LOADS,)),
        ],
        compiler_params=pltpu.CompilerParams(vmem_limit_bytes=52 * MIB if slots > 8 else 24 * MIB),
        cost_estimate=estimate(),
        name="first_products",
    )(*[pltpu.with_memory_space_constraint(operand, pltpu.HBM) for operand in operands])


def next_products(users, jobs, cost, rows, weights, served, after=()):
    vmem = pl.BlockSpec(memory_space=pltpu.VMEM)
    big = max(slots for _, _, slots in jobs) > 8
    tiles = (users // 8) * (weights.shape[1] // 128) * 2
    return pl.pallas_call(
        functools.partial(next_kernel, users, jobs),
        out_shape=[message(slots * tiles) for _, _, slots in jobs],
        in_specs=[vmem] * (3 + len(after)),
        out_specs=[vmem] * len(jobs),
        compiler_params=pltpu.CompilerParams(vmem_limit_bytes=48 * MIB if big else 16 * MIB),
        cost_estimate=estimate(cost),
        name="next_products",
    )(rows, weights, served, *after)


def add_up(refs, terms, count):
    total = refs[terms[0][0]][terms[0][1]:terms[0][1] + count]
    for ref, start in terms[1:]:
        total = total + refs[ref][start:start + count]
    return total


def sum_kernel(jobs, *refs):
    at = 0
    for terms, count in jobs:
        refs[-1][at:at + count] = add_up(refs, terms, count)
        at += count


def summed(arrays, jobs, cost, after):
    size = sum(count for _, count in jobs)
    vmem = pl.BlockSpec(memory_space=pltpu.VMEM)
    return pl.pallas_call(
        functools.partial(sum_kernel, jobs),
        out_shape=message(size),
        in_specs=[vmem] * (len(arrays) + len(after)),
        out_specs=vmem,
        compiler_params=pltpu.CompilerParams(vmem_limit_bytes=8 * MIB),
        cost_estimate=estimate(cost),
        name="summed",
    )(*arrays, *after)


def final_kernel(terms, powers, *refs):
    out = refs[-1]
    users, blocks = out.shape[0], out.shape[2] // 128
    steps = users // 8
    scale = lax.rsqrt(add_up(refs, powers, 1)[0] + epsilon)
    total = add_up(refs, terms, 2 * blocks * steps)
    for half in range(2):
        for block in range(blocks):
            start = (half * blocks + block) * steps
            value = total[start:start + steps].reshape(users, 128)
            factor = scale[block:block + 1, :]
            value = jnp.where(factor > 0.0, value * factor, 0.0)
            out[:, half, block * 128:(block + 1) * 128] = value


def finish(arrays, terms, powers, users, columns):
    vmem = pl.BlockSpec(memory_space=pltpu.VMEM)
    return pl.pallas_call(
        functools.partial(final_kernel, terms, powers),
        out_shape=jax.ShapeDtypeStruct((users, 2, columns), jnp.float32),
        in_specs=[vmem] * len(arrays),
        out_specs=vmem,
        compiler_params=pltpu.CompilerParams(vmem_limit_bytes=8 * MIB),
        name="finish",
    )(*arrays)


def message_order(chips):
    steps = []
    for step in range(chips):
        size = 1 << (chips - 1 - step)
        first = (1 << chips) - 2 * size
        steps.append(list(range(first, first + size)))
    if chips < 3:
        return [(step, slots) for step, slots in enumerate(steps)]
    quarter, half = len(steps[0]) // 4, len(steps[1]) // 2
    parts = [steps[0][at * quarter:(at + 1) * quarter] for at in range(4)]
    order = [
        (0, parts[0]),
        (0, parts[2]),
        (1, steps[1][:half]),
        (0, parts[1] + parts[3]),
        (2, steps[2]),
        (1, steps[1][half:]),
    ]
    return order + [(step, steps[step]) for step in range(3, chips)]


def on_device(channel, precoder, visible, cluster):
    devices = lax.axis_size("ap")
    bits = devices.bit_length() - 1
    users, columns = channel.shape[3], precoder.shape[2]
    tiles = (users // 8) * (columns // 128) * 2
    orders = chip_orders(bits)
    flat = precoder.reshape(-1, columns)
    half = devices // 4

    def swap(value, bit_of):
        return lax.ppermute(value, "ap", [(i, i ^ (1 << bit_of[i & 1])) for i in range(devices)])

    arrays = []
    terms = [[] for _ in range(2 * half)]
    powers = []

    def add(array, slots, power):
        for at, slot in enumerate(slots):
            terms[slot].append((len(arrays), at * tiles))
        if power:
            powers.append((len(arrays), len(slots) * tiles))
        arrays.append(array)

    def total(slots, power, cost=8192, after=()):
        jobs = [(list(terms[slot]), tiles) for slot in slots] + ([(list(powers), 1)] if power else [])
        used = sorted({array for parts, _ in jobs for array, _ in parts})
        jobs = [([(used.index(array), start) for array, start in parts], count) for parts, count in jobs]
        return summed([arrays[array] for array in used], jobs, cost, after)

    quarter = half // 4
    sent, rows, weights, served = first_products(bits, quarter, visible, cluster.T, channel, flat)
    came = swap(sent, (0, 0))
    add(sent, [], False)
    powers.append((0, quarter * tiles))
    products = functools.partial(next_products, users, rows=rows, weights=weights, served=served)
    first, count = quarter, 4 * quarter
    send, kept = products(((0, first, count), (1, 0, quarter)), cost=COSTS[0])
    add(kept, range(quarter), False)
    add(came, range(quarter), True)
    come = swap(send, (0, 0))
    add(products(((1, first, count),), cost=COSTS[1])[0], range(first, first + count), False)
    add(come, range(first, first + count), False)
    with_power = set()
    last = 2 * half - 1
    for number, (step, slots) in enumerate(message_order(bits - 1)):
        if number == 3:
            first, count = 5 * quarter, 3 * quarter
            send = products(((0, first, count),), cost=COSTS[2], after=[now])[0]
            come = swap(send, (0, 0))
            mine = products(((1, first, count),), cost=COSTS[3], after=[send])[0]
            add(mine, range(first, first + count), False)
            add(come, range(first, first + count), False)
        power = step not in with_power
        with_power.add(step)
        after = [mine] if number == 3 else [now] if number in (2, 5) else []
        now = total(slots, power, COSTS[4 + number] if number < 6 else 8192, after)
        came = swap(now, (orders[0][step], orders[1][step]))
        slots = [slot + (1 << (bits - 2 - step)) for slot in slots]
        add(came, slots, power)
    used = sorted({array for array, _ in terms[last] + powers})
    return finish(
        [arrays[array] for array in used],
        [(used.index(array), start) for array, start in terms[last]],
        [(used.index(array), start) for array, start in powers],
        users, columns,
    )


def solution(mesh):
    in_specs = (
        P(("parts", "ap"), None, None, None, None),
        P(None, ("parts", "ap"), None),
        P(("parts", "ap"), None),
        P("parts", None),
    )
    out_specs = P(("parts", "ap"), None, None)
    return jax.shard_map(
        on_device, mesh=mesh, in_specs=in_specs, out_specs=out_specs, check_vma=False
    )
```

```python
import functools

import jax
import jax.numpy as jnp
from jax import lax
from jax.experimental import pallas as pl
from jax.experimental.pallas import tpu as pltpu
from jax.sharding import PartitionSpec as P

epsilon = 1e-06
MIB = 1 << 20
LOADS = 4


COSTS = (64 * MIB, 8192 * MIB, 64 * MIB, 65536 * MIB) + (
    1024 * MIB, 64 * MIB, 64 * MIB, 64 * MIB, 64 * MIB, 8192 * MIB, 1024 * MIB
)


def chip_orders(bits):
    first = list(range(1, bits))
    second = list(first)
    if bits > 2:
        second[0], second[1] = second[1], second[0]
    return second, first


def place_of(group, me, core, bits):
    away = [1 - (((group ^ me) >> bit) & 1) for bit in range(1, bits)]
    if bits > 2:
        swapped = core == 0
        away[:2] = [jnp.where(swapped, away[1], away[0]), jnp.where(swapped, away[0], away[1])]
    place = 0
    for value in away:
        place = place * 2 + value
    return place


def left_side(rows):
    antennas = rows.shape[1] // 2
    turned = jnp.concatenate([-rows[:, antennas:], rows[:, :antennas]], axis=1)
    return jnp.concatenate([rows, turned], axis=0)


def put_products(value, served, users, base, out):
    blocks, steps = value.shape[1] // 128, users // 8
    group = value.shape[0] // users // 2
    value = jnp.where(served, value, 0.0)
    for half in range(2):
        for slot in range(group):
            top = (half * group + slot) * users
            for block in range(blocks):
                piece = value[top:top + users, block * 128:(block + 1) * 128]
                start = (((base + slot) * 2 + half) * blocks + block) * steps
                out[start:start + steps] = piece.reshape(steps, 8, 128)


def write_products(users, rows, weights, served, out):
    slots = rows.shape[0] // users
    group = max(size for size in range(1, 9) if slots % size == 0)
    for base in range(0, slots, group):
        both = left_side(rows[base * users:(base + group) * users, :])
        value = jnp.dot(both, weights, preferred_element_type=jnp.float32)
        put_products(value, served, users, base, out)


def square_sum(weights):
    wide = weights.astype(jnp.float32)
    return jnp.sum(wide * wide, axis=0, keepdims=True)


def power_tile(power, served):
    power = jnp.where(served, power, 0.0)
    blocks = power.shape[1] // 128
    pieces = [power[:, block * 128:(block + 1) * 128] for block in range(blocks)]
    return jnp.concatenate(pieces + [jnp.zeros((8 - blocks, 128), jnp.float32)], axis=0)


def first_kernel(
    bits, visible, cluster, channel, precoder,
    out, rows, weights, served,
    seen, names, raw, sems,
):
    me = lax.axis_index("ap")
    held, users, antennas = raw.shape[1], raw.shape[3], raw.shape[4]
    loads = [
        pltpu.make_async_copy(visible, seen, sems.at[0]),
        pltpu.make_async_copy(channel, raw, sems.at[1]),
        pltpu.make_async_copy(cluster, names, sems.at[2]),
    ]
    depth = weights.shape[0] // LOADS
    for part in range(LOADS):
        at = pl.ds(part * depth, depth)
        loads.append(pltpu.make_async_copy(precoder.at[at], weights.at[at], sems.at[3 + part]))
    for load in loads:
        load.start()
    rows[...] = jnp.zeros_like(rows)
    loads[0].wait()
    places = []
    for v in range(held):
        core = seen[0, v] & 1
        places.append((1 - (core ^ (me & 1)), place_of(seen[0, v], me, core, bits) * users))
    loads[1].wait()
    for v, (keep, place) in enumerate(places):
        at = pl.ds(pl.multiple_of(place, users), users)
        rows[keep, at, 0:antennas] = raw[0, v, 0]
        rows[keep, at, antennas:2 * antennas] = raw[0, v, 1]
    loads[2].wait()
    here = jnp.max((names[...] == me).astype(jnp.float32), axis=0, keepdims=True)
    served[...] = here
    size = (out.shape[0] // (weights.shape[1] // 128) // 2) * 8
    both = left_side(rows[0, 0:size, :])
    value = power = None
    for part in range(LOADS):
        loads[3 + part].wait()
        at = slice(part * depth, (part + 1) * depth)
        block = weights[at, :]
        term = jnp.dot(both[:, at], block, preferred_element_type=jnp.float32)
        square = square_sum(block)
        value = term if value is None else value + term
        power = square if power is None else power + square
    put_products(value, here > 0.0, users, 0, out)
    out[out.shape[0] - 1] = power_tile(power, here > 0.0)


def next_kernel(users, jobs, rows, weights, served, *refs):
    for (keep, first, slots), out in zip(jobs, refs[-len(jobs):]):
        mine = rows.at[keep, first * users:(first + slots) * users]
        write_products(users, mine, weights[...], served[...] > 0.0, out)


def message(tiles):
    return jax.ShapeDtypeStruct((tiles, 8, 128), jnp.float32)


def estimate(size=8192):
    return pl.CostEstimate(flops=size, bytes_accessed=size, transcendentals=0)


def first_products(bits, first, visible, cluster, channel, precoder):
    users, antennas = channel.shape[3], channel.shape[4]
    columns = precoder.shape[1]
    slots = 1 << (bits - 1)
    tiles = first * (users // 8) * (columns // 128) * 2
    vmem = pl.BlockSpec(memory_space=pltpu.VMEM)
    hbm = pl.BlockSpec(memory_space=pltpu.HBM)
    operands = (visible, cluster, channel, precoder)
    return pl.pallas_call(
        functools.partial(first_kernel, bits),
        out_shape=(
            message(tiles + 1),
            jax.ShapeDtypeStruct((2, slots * users, 2 * antennas), jnp.bfloat16),
            jax.ShapeDtypeStruct(precoder.shape, jnp.bfloat16),
            jax.ShapeDtypeStruct((1, columns), jnp.float32),
        ),
        in_specs=[hbm] * 4,
        out_specs=(vmem,) * 4,
        scratch_shapes=[
            pltpu.SMEM(visible.shape, jnp.int32),
            pltpu.VMEM(cluster.shape, jnp.int32),
            pltpu.VMEM(channel.shape, jnp.bfloat16),
            pltpu.SemaphoreType.DMA((3 + LOADS,)),
        ],
        compiler_params=pltpu.CompilerParams(vmem_limit_bytes=52 * MIB if slots > 8 else 24 * MIB),
        cost_estimate=estimate(),
        name="first_products",
    )(*[pltpu.with_memory_space_constraint(operand, pltpu.HBM) for operand in operands])


def next_products(users, jobs, cost, rows, weights, served, after=()):
    vmem = pl.BlockSpec(memory_space=pltpu.VMEM)
    big = max(slots for _, _, slots in jobs) > 8
    tiles = (users // 8) * (weights.shape[1] // 128) * 2
    return pl.pallas_call(
        functools.partial(next_kernel, users, jobs),
        out_shape=[message(slots * tiles) for _, _, slots in jobs],
        in_specs=[vmem] * (3 + len(after)),
        out_specs=[vmem] * len(jobs),
        compiler_params=pltpu.CompilerParams(vmem_limit_bytes=48 * MIB if big else 16 * MIB),
        cost_estimate=estimate(cost),
        name="next_products",
    )(rows, weights, served, *after)


def add_up(refs, terms, count):
    total = refs[terms[0][0]][terms[0][1]:terms[0][1] + count]
    for ref, start in terms[1:]:
        total = total + refs[ref][start:start + count]
    return total


def sum_kernel(jobs, *refs):
    at = 0
    for terms, count in jobs:
        refs[-1][at:at + count] = add_up(refs, terms, count)
        at += count


def summed(arrays, jobs, cost, after):
    size = sum(count for _, count in jobs)
    vmem = pl.BlockSpec(memory_space=pltpu.VMEM)
    return pl.pallas_call(
        functools.partial(sum_kernel, jobs),
        out_shape=message(size),
        in_specs=[vmem] * (len(arrays) + len(after)),
        out_specs=vmem,
        compiler_params=pltpu.CompilerParams(vmem_limit_bytes=8 * MIB),
        cost_estimate=estimate(cost),
        name="summed",
    )(*arrays, *after)


def final_kernel(terms, powers, *refs):
    out = refs[-1]
    users, blocks = out.shape[0], out.shape[2] // 128
    steps = users // 8
    scale = lax.rsqrt(add_up(refs, powers, 1)[0] + epsilon)
    total = add_up(refs, terms, 2 * blocks * steps)
    for half in range(2):
        for block in range(blocks):
            start = (half * blocks + block) * steps
            value = total[start:start + steps].reshape(users, 128)
            factor = scale[block:block + 1, :]
            value = jnp.where(factor > 0.0, value * factor, 0.0)
            out[:, half, block * 128:(block + 1) * 128] = value


def finish(arrays, terms, powers, users, columns):
    vmem = pl.BlockSpec(memory_space=pltpu.VMEM)
    return pl.pallas_call(
        functools.partial(final_kernel, terms, powers),
        out_shape=jax.ShapeDtypeStruct((users, 2, columns), jnp.float32),
        in_specs=[vmem] * len(arrays),
        out_specs=vmem,
        compiler_params=pltpu.CompilerParams(vmem_limit_bytes=8 * MIB),
        name="finish",
    )(*arrays)


def message_order(chips):
    steps = []
    for step in range(chips):
        size = 1 << (chips - 1 - step)
        first = (1 << chips) - 2 * size
        steps.append(list(range(first, first + size)))
    if chips < 3:
        return [(step, slots) for step, slots in enumerate(steps)]
    quarter, half = len(steps[0]) // 4, len(steps[1]) // 2
    parts = [steps[0][at * quarter:(at + 1) * quarter] for at in range(4)]
    order = [
        (0, parts[0]),
        (0, parts[2]),
        (1, steps[1][:half]),
        (0, parts[1]),
        (0, parts[3]),
        (2, steps[2]),
        (1, steps[1][half:]),
    ]
    return order + [(step, steps[step]) for step in range(3, chips)]


def on_device(channel, precoder, visible, cluster):
    devices = lax.axis_size("ap")
    bits = devices.bit_length() - 1
    users, columns = channel.shape[3], precoder.shape[2]
    tiles = (users // 8) * (columns // 128) * 2
    orders = chip_orders(bits)
    flat = precoder.reshape(-1, columns)
    half = devices // 4

    def swap(value, bit_of):
        return lax.ppermute(value, "ap", [(i, i ^ (1 << bit_of[i & 1])) for i in range(devices)])

    arrays = []
    terms = [[] for _ in range(2 * half)]
    powers = []

    def add(array, slots, power):
        for at, slot in enumerate(slots):
            terms[slot].append((len(arrays), at * tiles))
        if power:
            powers.append((len(arrays), len(slots) * tiles))
        arrays.append(array)

    def total(slots, power, cost=8192, after=()):
        jobs = [(list(terms[slot]), tiles) for slot in slots] + ([(list(powers), 1)] if power else [])
        used = sorted({array for parts, _ in jobs for array, _ in parts})
        jobs = [([(used.index(array), start) for array, start in parts], count) for parts, count in jobs]
        return summed([arrays[array] for array in used], jobs, cost, after)

    quarter = half // 4
    sent, rows, weights, served = first_products(bits, quarter, visible, cluster.T, channel, flat)
    came = swap(sent, (0, 0))
    add(sent, [], False)
    powers.append((0, quarter * tiles))
    products = functools.partial(next_products, users, rows=rows, weights=weights, served=served)
    first, count = quarter, 4 * quarter
    send, kept = products(((0, first, count), (1, 0, quarter)), cost=COSTS[0])
    add(kept, range(quarter), False)
    add(came, range(quarter), True)
    come = swap(send, (0, 0))
    add(products(((1, first, count),), cost=COSTS[1])[0], range(first, first + count), False)
    add(come, range(first, first + count), False)
    with_power = set()
    last = 2 * half - 1
    for number, (step, slots) in enumerate(message_order(bits - 1)):
        if number == 3:
            first, count = 5 * quarter, 3 * quarter
            send = products(((0, first, count),), cost=COSTS[2], after=[now])[0]
            come = swap(send, (0, 0))
            mine = products(((1, first, count),), cost=COSTS[3], after=[send])[0]
            add(mine, range(first, first + count), False)
            add(come, range(first, first + count), False)
        power = step not in with_power
        with_power.add(step)
        after = [mine] if number == 3 else [now] if number in (2, 4, 6) else []
        now = total(slots, power, COSTS[4 + number] if number < 7 else 8192, after)
        came = swap(now, (orders[0][step], orders[1][step]))
        slots = [slot + (1 << (bits - 2 - step)) for slot in slots]
        add(came, slots, power)
    used = sorted({array for array, _ in terms[last] + powers})
    return finish(
        [arrays[array] for array in used],
        [(used.index(array), start) for array, start in terms[last]],
        [(used.index(array), start) for array, start in powers],
        users, columns,
    )


def solution(mesh):
    in_specs = (
        P(("parts", "ap"), None, None, None, None),
        P(None, ("parts", "ap"), None),
        P(("parts", "ap"), None),
        P("parts", None),
    )
    out_specs = P(("parts", "ap"), None, None)
    return jax.shard_map(
        on_device, mesh=mesh, in_specs=in_specs, out_specs=out_specs, check_vma=False
    )
```

```python
import functools

import jax
import jax.numpy as jnp
from jax import lax
from jax.experimental import pallas as pl
from jax.experimental.pallas import tpu as pltpu
from jax.sharding import PartitionSpec as P

epsilon = 1e-06
MIB = 1 << 20
LOADS = 4


COSTS = (64 * MIB, 8192 * MIB, 64 * MIB, 65536 * MIB) + (
    1024 * MIB, 64 * MIB, 64 * MIB, 64 * MIB, 64 * MIB, 8192 * MIB, 1024 * MIB
)


def chip_orders(bits):
    first = list(range(1, bits))
    second = list(first)
    if bits > 2:
        second[0], second[1] = second[1], second[0]
    return first, second


def place_of(group, me, core, bits):
    away = [1 - (((group ^ me) >> bit) & 1) for bit in range(1, bits)]
    if bits > 2:
        swapped = core == 1
        away[:2] = [jnp.where(swapped, away[1], away[0]), jnp.where(swapped, away[0], away[1])]
    place = 0
    for value in away:
        place = place * 2 + value
    return place


def left_side(rows):
    antennas = rows.shape[1] // 2
    turned = jnp.concatenate([-rows[:, antennas:], rows[:, :antennas]], axis=1)
    return jnp.concatenate([rows, turned], axis=0)


def put_products(value, served, users, base, out):
    blocks, steps = value.shape[1] // 128, users // 8
    group = value.shape[0] // users // 2
    value = jnp.where(served, value, 0.0)
    for half in range(2):
        for slot in range(group):
            top = (half * group + slot) * users
            for block in range(blocks):
                piece = value[top:top + users, block * 128:(block + 1) * 128]
                start = (((base + slot) * 2 + half) * blocks + block) * steps
                out[start:start + steps] = piece.reshape(steps, 8, 128)


def write_products(users, rows, weights, served, out):
    slots = rows.shape[0] // users
    group = max(size for size in range(1, 9) if slots % size == 0)
    for base in range(0, slots, group):
        both = left_side(rows[base * users:(base + group) * users, :])
        value = jnp.dot(both, weights, preferred_element_type=jnp.float32)
        put_products(value, served, users, base, out)


def square_sum(weights):
    wide = weights.astype(jnp.float32)
    return jnp.sum(wide * wide, axis=0, keepdims=True)


def power_tile(power, served):
    power = jnp.where(served, power, 0.0)
    blocks = power.shape[1] // 128
    pieces = [power[:, block * 128:(block + 1) * 128] for block in range(blocks)]
    return jnp.concatenate(pieces + [jnp.zeros((8 - blocks, 128), jnp.float32)], axis=0)


def first_kernel(
    bits, visible, cluster, channel, precoder,
    out, rows, weights, served,
    seen, names, raw, sems,
):
    me = lax.axis_index("ap")
    held, users, antennas = raw.shape[1], raw.shape[3], raw.shape[4]
    loads = [
        pltpu.make_async_copy(visible, seen, sems.at[0]),
        pltpu.make_async_copy(channel, raw, sems.at[1]),
        pltpu.make_async_copy(cluster, names, sems.at[2]),
    ]
    depth = weights.shape[0] // LOADS
    for part in range(LOADS):
        at = pl.ds(part * depth, depth)
        loads.append(pltpu.make_async_copy(precoder.at[at], weights.at[at], sems.at[3 + part]))
    for load in loads:
        load.start()
    rows[...] = jnp.zeros_like(rows)
    loads[0].wait()
    places = []
    for v in range(held):
        core = seen[0, v] & 1
        places.append((1 - (core ^ (me & 1)), place_of(seen[0, v], me, core, bits) * users))
    loads[1].wait()
    for v, (keep, place) in enumerate(places):
        at = pl.ds(pl.multiple_of(place, users), users)
        rows[keep, at, 0:antennas] = raw[0, v, 0]
        rows[keep, at, antennas:2 * antennas] = raw[0, v, 1]
    loads[2].wait()
    here = jnp.max((names[...] == me).astype(jnp.float32), axis=0, keepdims=True)
    served[...] = here
    size = (out.shape[0] // (weights.shape[1] // 128) // 2) * 8
    both = left_side(rows[0, 0:size, :])
    value = power = None
    for part in range(LOADS):
        loads[3 + part].wait()
        at = slice(part * depth, (part + 1) * depth)
        block = weights[at, :]
        term = jnp.dot(both[:, at], block, preferred_element_type=jnp.float32)
        square = square_sum(block)
        value = term if value is None else value + term
        power = square if power is None else power + square
    put_products(value, here > 0.0, users, 0, out)
    out[out.shape[0] - 1] = power_tile(power, here > 0.0)


def next_kernel(users, jobs, rows, weights, served, *refs):
    for (keep, first, slots), out in zip(jobs, refs[-len(jobs):]):
        mine = rows.at[keep, first * users:(first + slots) * users]
        write_products(users, mine, weights[...], served[...] > 0.0, out)


def message(tiles):
    return jax.ShapeDtypeStruct((tiles, 8, 128), jnp.float32)


def estimate(size=8192):
    return pl.CostEstimate(flops=size, bytes_accessed=size, transcendentals=0)


def first_products(bits, first, visible, cluster, channel, precoder):
    users, antennas = channel.shape[3], channel.shape[4]
    columns = precoder.shape[1]
    slots = 1 << (bits - 1)
    tiles = first * (users // 8) * (columns // 128) * 2
    vmem = pl.BlockSpec(memory_space=pltpu.VMEM)
    hbm = pl.BlockSpec(memory_space=pltpu.HBM)
    operands = (visible, cluster, channel, precoder)
    return pl.pallas_call(
        functools.partial(first_kernel, bits),
        out_shape=(
            message(tiles + 1),
            jax.ShapeDtypeStruct((2, slots * users, 2 * antennas), jnp.bfloat16),
            jax.ShapeDtypeStruct(precoder.shape, jnp.bfloat16),
            jax.ShapeDtypeStruct((1, columns), jnp.float32),
        ),
        in_specs=[hbm] * 4,
        out_specs=(vmem,) * 4,
        scratch_shapes=[
            pltpu.SMEM(visible.shape, jnp.int32),
            pltpu.VMEM(cluster.shape, jnp.int32),
            pltpu.VMEM(channel.shape, jnp.bfloat16),
            pltpu.SemaphoreType.DMA((3 + LOADS,)),
        ],
        compiler_params=pltpu.CompilerParams(vmem_limit_bytes=52 * MIB if slots > 8 else 24 * MIB),
        cost_estimate=estimate(),
        name="first_products",
    )(*[pltpu.with_memory_space_constraint(operand, pltpu.HBM) for operand in operands])


def next_products(users, jobs, cost, rows, weights, served, after=()):
    vmem = pl.BlockSpec(memory_space=pltpu.VMEM)
    big = max(slots for _, _, slots in jobs) > 8
    tiles = (users // 8) * (weights.shape[1] // 128) * 2
    return pl.pallas_call(
        functools.partial(next_kernel, users, jobs),
        out_shape=[message(slots * tiles) for _, _, slots in jobs],
        in_specs=[vmem] * (3 + len(after)),
        out_specs=[vmem] * len(jobs),
        compiler_params=pltpu.CompilerParams(vmem_limit_bytes=48 * MIB if big else 16 * MIB),
        cost_estimate=estimate(cost),
        name="next_products",
    )(rows, weights, served, *after)


def add_up(refs, terms, count):
    total = refs[terms[0][0]][terms[0][1]:terms[0][1] + count]
    for ref, start in terms[1:]:
        total = total + refs[ref][start:start + count]
    return total


def sum_kernel(jobs, *refs):
    at = 0
    for terms, count in jobs:
        refs[-1][at:at + count] = add_up(refs, terms, count)
        at += count


def summed(arrays, jobs, cost, after):
    size = sum(count for _, count in jobs)
    vmem = pl.BlockSpec(memory_space=pltpu.VMEM)
    return pl.pallas_call(
        functools.partial(sum_kernel, jobs),
        out_shape=message(size),
        in_specs=[vmem] * (len(arrays) + len(after)),
        out_specs=vmem,
        compiler_params=pltpu.CompilerParams(vmem_limit_bytes=8 * MIB),
        cost_estimate=estimate(cost),
        name="summed",
    )(*arrays, *after)


def final_kernel(terms, powers, *refs):
    out = refs[-1]
    users, blocks = out.shape[0], out.shape[2] // 128
    steps = users // 8
    scale = lax.rsqrt(add_up(refs, powers, 1)[0] + epsilon)
    total = add_up(refs, terms, 2 * blocks * steps)
    for half in range(2):
        for block in range(blocks):
            start = (half * blocks + block) * steps
            value = total[start:start + steps].reshape(users, 128)
            factor = scale[block:block + 1, :]
            value = jnp.where(factor > 0.0, value * factor, 0.0)
            out[:, half, block * 128:(block + 1) * 128] = value


def finish(arrays, terms, powers, users, columns):
    vmem = pl.BlockSpec(memory_space=pltpu.VMEM)
    return pl.pallas_call(
        functools.partial(final_kernel, terms, powers),
        out_shape=jax.ShapeDtypeStruct((users, 2, columns), jnp.float32),
        in_specs=[vmem] * len(arrays),
        out_specs=vmem,
        compiler_params=pltpu.CompilerParams(vmem_limit_bytes=8 * MIB),
        name="finish",
    )(*arrays)


def message_order(chips):
    steps = []
    for step in range(chips):
        size = 1 << (chips - 1 - step)
        first = (1 << chips) - 2 * size
        steps.append(list(range(first, first + size)))
    if chips < 3:
        return [(step, slots) for step, slots in enumerate(steps)]
    quarter, half = len(steps[0]) // 4, len(steps[1]) // 2
    parts = [steps[0][at * quarter:(at + 1) * quarter] for at in range(4)]
    order = [
        (0, parts[0]),
        (0, parts[2]),
        (1, steps[1][:half]),
        (0, parts[1]),
        (0, parts[3]),
        (2, steps[2]),
        (1, steps[1][half:]),
    ]
    return order + [(step, steps[step]) for step in range(3, chips)]


def on_device(channel, precoder, visible, cluster):
    devices = lax.axis_size("ap")
    bits = devices.bit_length() - 1
    users, columns = channel.shape[3], precoder.shape[2]
    tiles = (users // 8) * (columns // 128) * 2
    orders = chip_orders(bits)
    flat = precoder.reshape(-1, columns)
    half = devices // 4

    def swap(value, bit_of):
        return lax.ppermute(value, "ap", [(i, i ^ (1 << bit_of[i & 1])) for i in range(devices)])

    arrays = []
    terms = [[] for _ in range(2 * half)]
    powers = []

    def add(array, slots, power):
        for at, slot in enumerate(slots):
            terms[slot].append((len(arrays), at * tiles))
        if power:
            powers.append((len(arrays), len(slots) * tiles))
        arrays.append(array)

    def total(slots, power, cost=8192, after=()):
        jobs = [(list(terms[slot]), tiles) for slot in slots] + ([(list(powers), 1)] if power else [])
        used = sorted({array for parts, _ in jobs for array, _ in parts})
        jobs = [([(used.index(array), start) for array, start in parts], count) for parts, count in jobs]
        return summed([arrays[array] for array in used], jobs, cost, after)

    quarter = half // 4
    sent, rows, weights, served = first_products(bits, quarter, visible, cluster.T, channel, flat)
    came = swap(sent, (0, 0))
    add(sent, [], False)
    powers.append((0, quarter * tiles))
    products = functools.partial(next_products, users, rows=rows, weights=weights, served=served)
    first, count = quarter, 4 * quarter
    send, kept = products(((0, first, count), (1, 0, quarter)), cost=COSTS[0])
    add(kept, range(quarter), False)
    add(came, range(quarter), True)
    come = swap(send, (0, 0))
    add(products(((1, first, count),), cost=COSTS[1])[0], range(first, first + count), False)
    add(come, range(first, first + count), False)
    with_power = set()
    last = 2 * half - 1
    for number, (step, slots) in enumerate(message_order(bits - 1)):
        if number == 3:
            first, count = 5 * quarter, 3 * quarter
            send = products(((0, first, count),), cost=COSTS[2], after=[now])[0]
            come = swap(send, (0, 0))
            mine = products(((1, first, count),), cost=COSTS[3], after=[send])[0]
            add(mine, range(first, first + count), False)
            add(come, range(first, first + count), False)
        power = step not in with_power
        with_power.add(step)
        after = [mine] if number == 3 else [now] if number in (2, 4, 6) else []
        now = total(slots, power, COSTS[4 + number] if number < 7 else 8192, after)
        came = swap(now, (orders[0][step], orders[1][step]))
        slots = [slot + (1 << (bits - 2 - step)) for slot in slots]
        add(came, slots, power)
    used = sorted({array for array, _ in terms[last] + powers})
    return finish(
        [arrays[array] for array in used],
        [(used.index(array), start) for array, start in terms[last]],
        [(used.index(array), start) for array, start in powers],
        users, columns,
    )


def solution(mesh):
    in_specs = (
        P(("parts", "ap"), None, None, None, None),
        P(None, ("parts", "ap"), None),
        P(("parts", "ap"), None),
        P("parts", None),
    )
    out_specs = P(("parts", "ap"), None, None)
    return jax.shard_map(
        on_device, mesh=mesh, in_specs=in_specs, out_specs=out_specs, check_vma=False
    )
```

```python
import functools

import jax
import jax.numpy as jnp
from jax import lax
from jax.experimental import pallas as pl
from jax.experimental.pallas import tpu as pltpu
from jax.sharding import PartitionSpec as P

epsilon = 1e-06
MIB = 1 << 20
LOADS = 4


COSTS = (64 * MIB, 8192 * MIB, 64 * MIB, 65536 * MIB) + (
    1024 * MIB, 64 * MIB, 64 * MIB, 64 * MIB, 64 * MIB, 8192 * MIB, 1024 * MIB
)


def chip_orders(bits):
    first = list(range(1, bits))
    second = list(first)
    if bits > 2:
        second[0], second[1] = second[1], second[0]
    return second, first


def place_of(group, me, core, bits):
    away = [1 - (((group ^ me) >> bit) & 1) for bit in range(1, bits)]
    if bits > 2:
        swapped = core == 0
        away[:2] = [jnp.where(swapped, away[1], away[0]), jnp.where(swapped, away[0], away[1])]
    place = 0
    for value in away:
        place = place * 2 + value
    return place


def left_side(rows):
    antennas = rows.shape[1] // 2
    turned = jnp.concatenate([-rows[:, antennas:], rows[:, :antennas]], axis=1)
    return jnp.concatenate([rows, turned], axis=0)


def put_products(value, served, users, base, out):
    blocks, steps = value.shape[1] // 128, users // 8
    group = value.shape[0] // users // 2
    value = jnp.where(served, value, 0.0)
    for half in range(2):
        for slot in range(group):
            top = (half * group + slot) * users
            for block in range(blocks):
                piece = value[top:top + users, block * 128:(block + 1) * 128]
                start = (((base + slot) * 2 + half) * blocks + block) * steps
                out[start:start + steps] = piece.reshape(steps, 8, 128)


def write_products(users, rows, weights, served, out):
    slots = rows.shape[0] // users
    group = max(size for size in range(1, 9) if slots % size == 0)
    for base in range(0, slots, group):
        both = left_side(rows[base * users:(base + group) * users, :])
        value = jnp.dot(both, weights, preferred_element_type=jnp.float32)
        put_products(value, served, users, base, out)


def square_sum(weights):
    wide = weights.astype(jnp.float32)
    return jnp.sum(wide * wide, axis=0, keepdims=True)


def power_tile(power, served):
    power = jnp.where(served, power, 0.0)
    blocks = power.shape[1] // 128
    pieces = [power[:, block * 128:(block + 1) * 128] for block in range(blocks)]
    return jnp.concatenate(pieces + [jnp.zeros((8 - blocks, 128), jnp.float32)], axis=0)


def first_kernel(
    bits, visible, cluster, channel, precoder,
    out, rows, weights, served,
    seen, names, raw, sems,
):
    me = lax.axis_index("ap")
    held, users, antennas = raw.shape[1], raw.shape[3], raw.shape[4]
    loads = [
        pltpu.make_async_copy(visible, seen, sems.at[0]),
        pltpu.make_async_copy(channel, raw, sems.at[1]),
        pltpu.make_async_copy(cluster, names, sems.at[2]),
    ]
    depth = weights.shape[0] // LOADS
    for part in range(LOADS):
        at = pl.ds(part * depth, depth)
        loads.append(pltpu.make_async_copy(precoder.at[at], weights.at[at], sems.at[3 + part]))
    for load in loads:
        load.start()
    rows[...] = jnp.zeros_like(rows)
    loads[0].wait()
    places = []
    for v in range(held):
        core = seen[0, v] & 1
        places.append((1 - (core ^ (me & 1)), place_of(seen[0, v], me, core, bits) * users))
    loads[1].wait()
    for v, (keep, place) in enumerate(places):
        at = pl.ds(pl.multiple_of(place, users), users)
        rows[keep, at, 0:antennas] = raw[0, v, 0]
        rows[keep, at, antennas:2 * antennas] = raw[0, v, 1]
    loads[2].wait()
    here = jnp.max((names[...] == me).astype(jnp.float32), axis=0, keepdims=True)
    served[...] = here
    size = (out.shape[0] // (weights.shape[1] // 128) // 2) * 8
    both = left_side(rows[0, 0:size, :])
    value = power = None
    for part in range(LOADS):
        loads[3 + part].wait()
        at = slice(part * depth, (part + 1) * depth)
        block = weights[at, :]
        term = jnp.dot(both[:, at], block, preferred_element_type=jnp.float32)
        square = square_sum(block)
        value = term if value is None else value + term
        power = square if power is None else power + square
    put_products(value, here > 0.0, users, 0, out)
    out[out.shape[0] - 1] = power_tile(power, here > 0.0)


def next_kernel(users, jobs, rows, weights, served, *refs):
    for (keep, first, slots), out in zip(jobs, refs[-len(jobs):]):
        mine = rows.at[keep, first * users:(first + slots) * users]
        write_products(users, mine, weights[...], served[...] > 0.0, out)


def message(tiles):
    return jax.ShapeDtypeStruct((tiles, 8, 128), jnp.float32)


def estimate(size=8192):
    return pl.CostEstimate(flops=size, bytes_accessed=size, transcendentals=0)


def first_products(bits, first, visible, cluster, channel, precoder):
    users, antennas = channel.shape[3], channel.shape[4]
    columns = precoder.shape[1]
    slots = 1 << (bits - 1)
    tiles = first * (users // 8) * (columns // 128) * 2
    vmem = pl.BlockSpec(memory_space=pltpu.VMEM)
    hbm = pl.BlockSpec(memory_space=pltpu.HBM)
    operands = (visible, cluster, channel, precoder)
    return pl.pallas_call(
        functools.partial(first_kernel, bits),
        out_shape=(
            message(tiles + 1),
            jax.ShapeDtypeStruct((2, slots * users, 2 * antennas), jnp.bfloat16),
            jax.ShapeDtypeStruct(precoder.shape, jnp.bfloat16),
            jax.ShapeDtypeStruct((1, columns), jnp.float32),
        ),
        in_specs=[hbm] * 4,
        out_specs=(vmem,) * 4,
        scratch_shapes=[
            pltpu.SMEM(visible.shape, jnp.int32),
            pltpu.VMEM(cluster.shape, jnp.int32),
            pltpu.VMEM(channel.shape, jnp.bfloat16),
            pltpu.SemaphoreType.DMA((3 + LOADS,)),
        ],
        compiler_params=pltpu.CompilerParams(vmem_limit_bytes=52 * MIB if slots > 8 else 24 * MIB),
        cost_estimate=estimate(),
        name="first_products",
    )(*[pltpu.with_memory_space_constraint(operand, pltpu.HBM) for operand in operands])


def next_products(users, jobs, cost, rows, weights, served, after=()):
    vmem = pl.BlockSpec(memory_space=pltpu.VMEM)
    big = max(slots for _, _, slots in jobs) > 8
    tiles = (users // 8) * (weights.shape[1] // 128) * 2
    return pl.pallas_call(
        functools.partial(next_kernel, users, jobs),
        out_shape=[message(slots * tiles) for _, _, slots in jobs],
        in_specs=[vmem] * (3 + len(after)),
        out_specs=[vmem] * len(jobs),
        compiler_params=pltpu.CompilerParams(vmem_limit_bytes=48 * MIB if big else 16 * MIB),
        cost_estimate=estimate(cost),
        name="next_products",
    )(rows, weights, served, *after)


def add_up(refs, terms, count):
    total = refs[terms[0][0]][terms[0][1]:terms[0][1] + count]
    for ref, start in terms[1:]:
        total = total + refs[ref][start:start + count]
    return total


def sum_kernel(jobs, *refs):
    at = 0
    for terms, count in jobs:
        refs[-1][at:at + count] = add_up(refs, terms, count)
        at += count


def summed(arrays, jobs, cost, after):
    size = sum(count for _, count in jobs)
    vmem = pl.BlockSpec(memory_space=pltpu.VMEM)
    return pl.pallas_call(
        functools.partial(sum_kernel, jobs),
        out_shape=message(size),
        in_specs=[vmem] * (len(arrays) + len(after)),
        out_specs=vmem,
        compiler_params=pltpu.CompilerParams(vmem_limit_bytes=8 * MIB),
        cost_estimate=estimate(cost),
        name="summed",
    )(*arrays, *after)


def final_kernel(terms, powers, *refs):
    out = refs[-1]
    users, blocks = out.shape[0], out.shape[2] // 128
    steps = users // 8
    scale = lax.rsqrt(add_up(refs, powers, 1)[0] + epsilon)
    for half in range(2):
        total = add_up(refs, terms[half], blocks * steps)
        for block in range(blocks):
            start = block * steps
            value = total[start:start + steps].reshape(users, 128)
            factor = scale[block:block + 1, :]
            value = jnp.where(factor > 0.0, value * factor, 0.0)
            out[:, half, block * 128:(block + 1) * 128] = value


def finish(arrays, terms, powers, users, columns):
    vmem = pl.BlockSpec(memory_space=pltpu.VMEM)
    return pl.pallas_call(
        functools.partial(final_kernel, terms, powers),
        out_shape=jax.ShapeDtypeStruct((users, 2, columns), jnp.float32),
        in_specs=[vmem] * len(arrays),
        out_specs=vmem,
        compiler_params=pltpu.CompilerParams(vmem_limit_bytes=8 * MIB),
        name="finish",
    )(*arrays)


def message_order(chips):
    steps = []
    for step in range(chips):
        size = 1 << (chips - 1 - step)
        first = (1 << chips) - 2 * size
        steps.append([(slot, part) for slot in range(first, first + size) for part in range(2)])
    if chips < 3:
        return [(step, pieces) for step, pieces in enumerate(steps)]
    quarter, half = len(steps[0]) // 4, len(steps[1]) // 2
    parts = [steps[0][at * quarter:(at + 1) * quarter] for at in range(4)]
    order = [
        (0, parts[0]),
        (0, parts[2] + parts[1][::2]),
        (1, steps[1][:half]),
        (0, parts[1][1::2]),
        (0, parts[3]),
        (2, steps[2]),
        (1, steps[1][half:]),
    ]
    return order + [(step, steps[step]) for step in range(3, chips)]


def on_device(channel, precoder, visible, cluster):
    devices = lax.axis_size("ap")
    bits = devices.bit_length() - 1
    users, columns = channel.shape[3], precoder.shape[2]
    tiles = (users // 8) * (columns // 128)
    orders = chip_orders(bits)
    flat = precoder.reshape(-1, columns)
    half = devices // 4

    def swap(value, bit_of):
        return lax.ppermute(value, "ap", [(i, i ^ (1 << bit_of[i & 1])) for i in range(devices)])

    arrays = []
    terms = {(slot, part): [] for slot in range(2 * half) for part in range(2)}
    powers = []

    def add(array, pieces, power):
        for at, piece in enumerate(pieces):
            terms[piece].append((len(arrays), at * tiles))
        if power:
            powers.append((len(arrays), len(pieces) * tiles))
        arrays.append(array)

    def pieces_of(first, count):
        return [(slot, part) for slot in range(first, first + count) for part in range(2)]

    def total(pieces, power, cost=8192, after=()):
        jobs = [(list(terms[piece]), tiles) for piece in pieces]
        jobs += [(list(powers), 1)] * int(power)
        used = sorted({array for parts, _ in jobs for array, _ in parts})
        jobs = [([(used.index(array), start) for array, start in parts], count) for parts, count in jobs]
        return summed([arrays[array] for array in used], jobs, cost, after)

    quarter = half // 4
    sent, rows, weights, served = first_products(bits, quarter, visible, cluster.T, channel, flat)
    came = swap(sent, (0, 0))
    add(sent, [], False)
    powers.append((0, 2 * quarter * tiles))
    products = functools.partial(next_products, users, rows=rows, weights=weights, served=served)
    first, count = quarter, 4 * quarter
    send, kept = products(((0, first, count), (1, 0, quarter)), cost=COSTS[0])
    add(kept, pieces_of(0, quarter), False)
    add(came, pieces_of(0, quarter), True)
    come = swap(send, (0, 0))
    add(products(((1, first, count),), cost=COSTS[1])[0], pieces_of(first, count), False)
    add(come, pieces_of(first, count), False)
    with_power = set()
    last = [(2 * half - 1, part) for part in range(2)]
    for number, (step, pieces) in enumerate(message_order(bits - 1)):
        if number == 3:
            first, count = 5 * quarter, 3 * quarter
            send = products(((0, first, count),), cost=COSTS[2], after=[now])[0]
            come = swap(send, (0, 0))
            mine = products(((1, first, count),), cost=COSTS[3], after=[send])[0]
            add(mine, pieces_of(first, count), False)
            add(come, pieces_of(first, count), False)
        power = step not in with_power
        with_power.add(step)
        after = [mine] if number == 3 else [now] if number in (2, 4, 6) else []
        now = total(pieces, power, COSTS[4 + number] if number < 7 else 8192, after)
        came = swap(now, (orders[0][step], orders[1][step]))
        pieces = [(slot + (1 << (bits - 2 - step)), part) for slot, part in pieces]
        add(came, pieces, power)
    used = sorted({array for parts in [terms[piece] for piece in last] + [powers] for array, _ in parts})
    return finish(
        [arrays[array] for array in used],
        [[(used.index(array), start) for array, start in terms[piece]] for piece in last],
        [(used.index(array), start) for array, start in powers],
        users, columns,
    )


def solution(mesh):
    in_specs = (
        P(("parts", "ap"), None, None, None, None),
        P(None, ("parts", "ap"), None),
        P(("parts", "ap"), None),
        P("parts", None),
    )
    out_specs = P(("parts", "ap"), None, None)
    return jax.shard_map(
        on_device, mesh=mesh, in_specs=in_specs, out_specs=out_specs, check_vma=False
    )
```

```python
import functools

import jax
import jax.numpy as jnp
from jax import lax
from jax.experimental import pallas as pl
from jax.experimental.pallas import tpu as pltpu
from jax.sharding import PartitionSpec as P

epsilon = 1e-06
MIB = 1 << 20
LOADS = 4


COSTS = (64 * MIB, 8192 * MIB, 64 * MIB, 65536 * MIB) + (
    1024 * MIB, 64 * MIB, 64 * MIB, 64 * MIB, 8192 * MIB, 1024 * MIB
)


def chip_orders(bits):
    first = list(range(1, bits))
    second = list(first)
    if bits > 2:
        second[0], second[1] = second[1], second[0]
    return second, first


def place_of(group, me, core, bits):
    away = [1 - (((group ^ me) >> bit) & 1) for bit in range(1, bits)]
    if bits > 2:
        swapped = core == 0
        away[:2] = [jnp.where(swapped, away[1], away[0]), jnp.where(swapped, away[0], away[1])]
    place = 0
    for value in away:
        place = place * 2 + value
    return place


def left_side(rows):
    antennas = rows.shape[1] // 2
    turned = jnp.concatenate([-rows[:, antennas:], rows[:, :antennas]], axis=1)
    return jnp.concatenate([rows, turned], axis=0)


def put_products(value, served, users, base, out):
    blocks, steps = value.shape[1] // 128, users // 8
    group = value.shape[0] // users // 2
    value = jnp.where(served, value, 0.0)
    for half in range(2):
        for slot in range(group):
            top = (half * group + slot) * users
            for block in range(blocks):
                piece = value[top:top + users, block * 128:(block + 1) * 128]
                start = (((base + slot) * 2 + half) * blocks + block) * steps
                out[start:start + steps] = piece.reshape(steps, 8, 128)


def write_products(users, rows, weights, served, out):
    slots = rows.shape[0] // users
    group = max(size for size in range(1, 9) if slots % size == 0)
    for base in range(0, slots, group):
        both = left_side(rows[base * users:(base + group) * users, :])
        value = jnp.dot(both, weights, preferred_element_type=jnp.float32)
        put_products(value, served, users, base, out)


def square_sum(weights):
    wide = weights.astype(jnp.float32)
    return jnp.sum(wide * wide, axis=0, keepdims=True)


def power_tile(power, served):
    power = jnp.where(served, power, 0.0)
    blocks = power.shape[1] // 128
    pieces = [power[:, block * 128:(block + 1) * 128] for block in range(blocks)]
    return jnp.concatenate(pieces + [jnp.zeros((8 - blocks, 128), jnp.float32)], axis=0)


def first_kernel(
    bits, visible, cluster, channel, precoder,
    out, rows, weights, served,
    seen, names, raw, sems,
):
    me = lax.axis_index("ap")
    held, users, antennas = raw.shape[1], raw.shape[3], raw.shape[4]
    loads = [
        pltpu.make_async_copy(visible, seen, sems.at[0]),
        pltpu.make_async_copy(channel, raw, sems.at[1]),
        pltpu.make_async_copy(cluster, names, sems.at[2]),
    ]
    depth = weights.shape[0] // LOADS
    for part in range(LOADS):
        at = pl.ds(part * depth, depth)
        loads.append(pltpu.make_async_copy(precoder.at[at], weights.at[at], sems.at[3 + part]))
    for load in loads:
        load.start()
    rows[...] = jnp.zeros_like(rows)
    loads[0].wait()
    places = []
    for v in range(held):
        core = seen[0, v] & 1
        places.append((1 - (core ^ (me & 1)), place_of(seen[0, v], me, core, bits) * users))
    loads[1].wait()
    for v, (keep, place) in enumerate(places):
        at = pl.ds(pl.multiple_of(place, users), users)
        rows[keep, at, 0:antennas] = raw[0, v, 0]
        rows[keep, at, antennas:2 * antennas] = raw[0, v, 1]
    loads[2].wait()
    here = jnp.max((names[...] == me).astype(jnp.float32), axis=0, keepdims=True)
    served[...] = here
    size = (out.shape[0] // (weights.shape[1] // 128) // 2) * 8
    both = left_side(rows[0, 0:size, :])
    value = power = None
    for part in range(LOADS):
        loads[3 + part].wait()
        at = slice(part * depth, (part + 1) * depth)
        block = weights[at, :]
        term = jnp.dot(both[:, at], block, preferred_element_type=jnp.float32)
        square = square_sum(block)
        value = term if value is None else value + term
        power = square if power is None else power + square
    put_products(value, here > 0.0, users, 0, out)
    out[out.shape[0] - 1] = power_tile(power, here > 0.0)


def next_kernel(users, jobs, rows, weights, served, *refs):
    for (keep, first, slots), out in zip(jobs, refs[-len(jobs):]):
        mine = rows.at[keep, first * users:(first + slots) * users]
        write_products(users, mine, weights[...], served[...] > 0.0, out)


def message(tiles):
    return jax.ShapeDtypeStruct((tiles, 8, 128), jnp.float32)


def estimate(size=8192):
    return pl.CostEstimate(flops=size, bytes_accessed=size, transcendentals=0)


def first_products(bits, first, visible, cluster, channel, precoder):
    users, antennas = channel.shape[3], channel.shape[4]
    columns = precoder.shape[1]
    slots = 1 << (bits - 1)
    tiles = first * (users // 8) * (columns // 128) * 2
    vmem = pl.BlockSpec(memory_space=pltpu.VMEM)
    hbm = pl.BlockSpec(memory_space=pltpu.HBM)
    operands = (visible, cluster, channel, precoder)
    return pl.pallas_call(
        functools.partial(first_kernel, bits),
        out_shape=(
            message(tiles + 1),
            jax.ShapeDtypeStruct((2, slots * users, 2 * antennas), jnp.bfloat16),
            jax.ShapeDtypeStruct(precoder.shape, jnp.bfloat16),
            jax.ShapeDtypeStruct((1, columns), jnp.float32),
        ),
        in_specs=[hbm] * 4,
        out_specs=(vmem,) * 4,
        scratch_shapes=[
            pltpu.SMEM(visible.shape, jnp.int32),
            pltpu.VMEM(cluster.shape, jnp.int32),
            pltpu.VMEM(channel.shape, jnp.bfloat16),
            pltpu.SemaphoreType.DMA((3 + LOADS,)),
        ],
        compiler_params=pltpu.CompilerParams(vmem_limit_bytes=52 * MIB if slots > 8 else 24 * MIB),
        cost_estimate=estimate(),
        name="first_products",
    )(*[pltpu.with_memory_space_constraint(operand, pltpu.HBM) for operand in operands])


def next_products(users, jobs, cost, rows, weights, served, after=()):
    vmem = pl.BlockSpec(memory_space=pltpu.VMEM)
    big = max(slots for _, _, slots in jobs) > 8
    tiles = (users // 8) * (weights.shape[1] // 128) * 2
    return pl.pallas_call(
        functools.partial(next_kernel, users, jobs),
        out_shape=[message(slots * tiles) for _, _, slots in jobs],
        in_specs=[vmem] * (3 + len(after)),
        out_specs=[vmem] * len(jobs),
        compiler_params=pltpu.CompilerParams(vmem_limit_bytes=48 * MIB if big else 16 * MIB),
        cost_estimate=estimate(cost),
        name="next_products",
    )(rows, weights, served, *after)


def add_up(refs, terms, count):
    total = refs[terms[0][0]][terms[0][1]:terms[0][1] + count]
    for ref, start in terms[1:]:
        total = total + refs[ref][start:start + count]
    return total


def sum_kernel(jobs, *refs):
    at = 0
    for terms, count in jobs:
        refs[-1][at:at + count] = add_up(refs, terms, count)
        at += count


def summed(arrays, jobs, cost, after):
    size = sum(count for _, count in jobs)
    vmem = pl.BlockSpec(memory_space=pltpu.VMEM)
    return pl.pallas_call(
        functools.partial(sum_kernel, jobs),
        out_shape=message(size),
        in_specs=[vmem] * (len(arrays) + len(after)),
        out_specs=vmem,
        compiler_params=pltpu.CompilerParams(vmem_limit_bytes=8 * MIB),
        cost_estimate=estimate(cost),
        name="summed",
    )(*arrays, *after)


def final_kernel(terms, powers, *refs):
    out = refs[-1]
    users, blocks = out.shape[0], out.shape[2] // 128
    steps = users // 8
    scale = lax.rsqrt(add_up(refs, powers, 1)[0] + epsilon)
    total = add_up(refs, terms, 2 * blocks * steps)
    for half in range(2):
        for block in range(blocks):
            start = (half * blocks + block) * steps
            value = total[start:start + steps].reshape(users, 128)
            factor = scale[block:block + 1, :]
            value = jnp.where(factor > 0.0, value * factor, 0.0)
            out[:, half, block * 128:(block + 1) * 128] = value


def finish(arrays, terms, powers, users, columns):
    vmem = pl.BlockSpec(memory_space=pltpu.VMEM)
    return pl.pallas_call(
        functools.partial(final_kernel, terms, powers),
        out_shape=jax.ShapeDtypeStruct((users, 2, columns), jnp.float32),
        in_specs=[vmem] * len(arrays),
        out_specs=vmem,
        compiler_params=pltpu.CompilerParams(vmem_limit_bytes=8 * MIB),
        name="finish",
    )(*arrays)


def message_order(chips):
    steps = []
    for step in range(chips):
        size = 1 << (chips - 1 - step)
        first = (1 << chips) - 2 * size
        steps.append(list(range(first, first + size)))
    if chips < 3:
        return [(step, slots) for step, slots in enumerate(steps)]
    quarter, half = len(steps[0]) // 4, len(steps[1]) // 2
    parts = [steps[0][at * quarter:(at + 1) * quarter] for at in range(4)]
    order = [
        (0, parts[0]),
        (0, parts[1] + parts[2]),
        (1, steps[1][:half]),
        (0, parts[3]),
        (2, steps[2]),
        (1, steps[1][half:]),
    ]
    return order + [(step, steps[step]) for step in range(3, chips)]


def on_device(channel, precoder, visible, cluster):
    devices = lax.axis_size("ap")
    bits = devices.bit_length() - 1
    users, columns = channel.shape[3], precoder.shape[2]
    tiles = (users // 8) * (columns // 128) * 2
    orders = chip_orders(bits)
    flat = precoder.reshape(-1, columns)
    half = devices // 4

    def swap(value, bit_of):
        return lax.ppermute(value, "ap", [(i, i ^ (1 << bit_of[i & 1])) for i in range(devices)])

    arrays = []
    terms = [[] for _ in range(2 * half)]
    powers = []

    def add(array, slots, power):
        for at, slot in enumerate(slots):
            terms[slot].append((len(arrays), at * tiles))
        if power:
            powers.append((len(arrays), len(slots) * tiles))
        arrays.append(array)

    def total(slots, power, cost=8192, after=()):
        jobs = [(list(terms[slot]), tiles) for slot in slots] + ([(list(powers), 1)] if power else [])
        used = sorted({array for parts, _ in jobs for array, _ in parts})
        jobs = [([(used.index(array), start) for array, start in parts], count) for parts, count in jobs]
        return summed([arrays[array] for array in used], jobs, cost, after)

    quarter = half // 4
    sent, rows, weights, served = first_products(bits, quarter, visible, cluster.T, channel, flat)
    came = swap(sent, (0, 0))
    add(sent, [], False)
    powers.append((0, quarter * tiles))
    products = functools.partial(next_products, users, rows=rows, weights=weights, served=served)
    first, count = quarter, 4 * quarter
    send, kept = products(((0, first, count), (1, 0, quarter)), cost=COSTS[0])
    add(kept, range(quarter), False)
    add(came, range(quarter), True)
    come = swap(send, (0, 0))
    add(products(((1, first, count),), cost=COSTS[1])[0], range(first, first + count), False)
    add(come, range(first, first + count), False)
    with_power = set()
    last = 2 * half - 1
    for number, (step, slots) in enumerate(message_order(bits - 1)):
        if number == 3:
            first, count = 5 * quarter, 3 * quarter
            send = products(((0, first, count),), cost=COSTS[2], after=[now])[0]
            come = swap(send, (0, 0))
            mine = products(((1, first, count),), cost=COSTS[3], after=[send])[0]
            add(mine, range(first, first + count), False)
            add(come, range(first, first + count), False)
        power = step not in with_power
        with_power.add(step)
        after = [mine] if number == 3 else [now] if number in (2, 5) else []
        now = total(slots, power, COSTS[4 + number] if number < 6 else 8192, after)
        came = swap(now, (orders[0][step], orders[1][step]))
        slots = [slot + (1 << (bits - 2 - step)) for slot in slots]
        add(came, slots, power)
    used = sorted({array for array, _ in terms[last] + powers})
    return finish(
        [arrays[array] for array in used],
        [(used.index(array), start) for array, start in terms[last]],
        [(used.index(array), start) for array, start in powers],
        users, columns,
    )


def solution(mesh):
    in_specs = (
        P(("parts", "ap"), None, None, None, None),
        P(None, ("parts", "ap"), None),
        P(("parts", "ap"), None),
        P("parts", None),
    )
    out_specs = P(("parts", "ap"), None, None)
    return jax.shard_map(
        on_device, mesh=mesh, in_specs=in_specs, out_specs=out_specs, check_vma=False
    )
```

```python
import functools

import jax
import jax.numpy as jnp
from jax import lax
from jax.experimental import pallas as pl
from jax.experimental.pallas import tpu as pltpu
from jax.sharding import PartitionSpec as P

epsilon = 1e-06
MIB = 1 << 20
LOADS = 4


COSTS = (64 * MIB, 8192 * MIB, 64 * MIB, 65536 * MIB) + (
    1024 * MIB, 64 * MIB, 64 * MIB, 64 * MIB, 8192 * MIB, 1024 * MIB
)


def chip_orders(bits):
    first = list(range(1, bits))
    second = list(first)
    if bits > 2:
        second[0], second[1] = second[1], second[0]
    return second, first


def place_of(group, me, core, bits):
    away = [1 - (((group ^ me) >> bit) & 1) for bit in range(1, bits)]
    if bits > 2:
        swapped = core == 0
        away[:2] = [jnp.where(swapped, away[1], away[0]), jnp.where(swapped, away[0], away[1])]
    place = 0
    for value in away:
        place = place * 2 + value
    return place


def left_side(rows):
    antennas = rows.shape[1] // 2
    turned = jnp.concatenate([-rows[:, antennas:], rows[:, :antennas]], axis=1)
    return jnp.concatenate([rows, turned], axis=0)


def put_products(value, served, users, base, out):
    blocks, steps = value.shape[1] // 128, users // 8
    group = value.shape[0] // users // 2
    value = jnp.where(served, value, 0.0)
    for half in range(2):
        for slot in range(group):
            top = (half * group + slot) * users
            for block in range(blocks):
                piece = value[top:top + users, block * 128:(block + 1) * 128]
                start = (((base + slot) * 2 + half) * blocks + block) * steps
                out[start:start + steps] = piece.reshape(steps, 8, 128)


def write_products(users, rows, weights, served, out):
    slots = rows.shape[0] // users
    group = max(size for size in range(1, 9) if slots % size == 0)
    for base in range(0, slots, group):
        both = left_side(rows[base * users:(base + group) * users, :])
        value = jnp.dot(both, weights, preferred_element_type=jnp.float32)
        put_products(value, served, users, base, out)


def square_sum(weights):
    wide = weights.astype(jnp.float32)
    return jnp.sum(wide * wide, axis=0, keepdims=True)


def power_tile(power, served):
    power = jnp.where(served, power, 0.0)
    blocks = power.shape[1] // 128
    pieces = [power[:, block * 128:(block + 1) * 128] for block in range(blocks)]
    return jnp.concatenate(pieces + [jnp.zeros((8 - blocks, 128), jnp.float32)], axis=0)


def first_kernel(
    bits, visible, cluster, channel, precoder,
    out, rows, weights, served,
    seen, names, raw, sems,
):
    me = lax.axis_index("ap")
    held, users, antennas = raw.shape[1], raw.shape[3], raw.shape[4]
    loads = [
        pltpu.make_async_copy(visible, seen, sems.at[0]),
        pltpu.make_async_copy(channel, raw, sems.at[1]),
        pltpu.make_async_copy(cluster, names, sems.at[2]),
    ]
    depth = weights.shape[0] // LOADS
    for part in range(LOADS):
        at = pl.ds(part * depth, depth)
        loads.append(pltpu.make_async_copy(precoder.at[at], weights.at[at], sems.at[3 + part]))
    for load in loads:
        load.start()
    rows[...] = jnp.zeros_like(rows)
    loads[0].wait()
    places = []
    for v in range(held):
        core = seen[0, v] & 1
        places.append((1 - (core ^ (me & 1)), place_of(seen[0, v], me, core, bits) * users))
    loads[1].wait()
    for v, (keep, place) in enumerate(places):
        at = pl.ds(pl.multiple_of(place, users), users)
        rows[keep, at, 0:antennas] = raw[0, v, 0]
        rows[keep, at, antennas:2 * antennas] = raw[0, v, 1]
    loads[2].wait()
    here = jnp.max((names[...] == me).astype(jnp.float32), axis=0, keepdims=True)
    served[...] = here
    size = (out.shape[0] // (weights.shape[1] // 128) // 2) * 8
    both = left_side(rows[0, 0:size, :])
    value = power = None
    for part in range(LOADS):
        loads[3 + part].wait()
        at = slice(part * depth, (part + 1) * depth)
        block = weights[at, :]
        term = jnp.dot(both[:, at], block, preferred_element_type=jnp.float32)
        square = square_sum(block)
        value = term if value is None else value + term
        power = square if power is None else power + square
    put_products(value, here > 0.0, users, 0, out)
    out[out.shape[0] - 1] = power_tile(power, here > 0.0)


def next_kernel(users, jobs, rows, weights, served, *refs):
    for (keep, first, slots), out in zip(jobs, refs[-len(jobs):]):
        mine = rows.at[keep, first * users:(first + slots) * users]
        write_products(users, mine, weights[...], served[...] > 0.0, out)


def message(tiles):
    return jax.ShapeDtypeStruct((tiles, 8, 128), jnp.float32)


def estimate(size=8192):
    return pl.CostEstimate(flops=size, bytes_accessed=size, transcendentals=0)


def first_products(bits, first, visible, cluster, channel, precoder):
    users, antennas = channel.shape[3], channel.shape[4]
    columns = precoder.shape[1]
    slots = 1 << (bits - 1)
    tiles = first * (users // 8) * (columns // 128) * 2
    vmem = pl.BlockSpec(memory_space=pltpu.VMEM)
    hbm = pl.BlockSpec(memory_space=pltpu.HBM)
    operands = (visible, cluster, channel, precoder)
    return pl.pallas_call(
        functools.partial(first_kernel, bits),
        out_shape=(
            message(tiles + 1),
            jax.ShapeDtypeStruct((2, slots * users, 2 * antennas), jnp.bfloat16),
            jax.ShapeDtypeStruct(precoder.shape, jnp.bfloat16),
            jax.ShapeDtypeStruct((1, columns), jnp.float32),
        ),
        in_specs=[hbm] * 4,
        out_specs=(vmem,) * 4,
        scratch_shapes=[
            pltpu.SMEM(visible.shape, jnp.int32),
            pltpu.VMEM(cluster.shape, jnp.int32),
            pltpu.VMEM(channel.shape, jnp.bfloat16),
            pltpu.SemaphoreType.DMA((3 + LOADS,)),
        ],
        compiler_params=pltpu.CompilerParams(vmem_limit_bytes=52 * MIB if slots > 8 else 24 * MIB),
        cost_estimate=estimate(),
        name="first_products",
    )(*[pltpu.with_memory_space_constraint(operand, pltpu.HBM) for operand in operands])


def next_products(users, jobs, cost, rows, weights, served, after=()):
    vmem = pl.BlockSpec(memory_space=pltpu.VMEM)
    big = max(slots for _, _, slots in jobs) > 8
    tiles = (users // 8) * (weights.shape[1] // 128) * 2
    return pl.pallas_call(
        functools.partial(next_kernel, users, jobs),
        out_shape=[message(slots * tiles) for _, _, slots in jobs],
        in_specs=[vmem] * (3 + len(after)),
        out_specs=[vmem] * len(jobs),
        compiler_params=pltpu.CompilerParams(vmem_limit_bytes=48 * MIB if big else 16 * MIB),
        cost_estimate=estimate(cost),
        name="next_products",
    )(rows, weights, served, *after)


def add_up(refs, terms, count):
    total = refs[terms[0][0]][terms[0][1]:terms[0][1] + count]
    for ref, start in terms[1:]:
        total = total + refs[ref][start:start + count]
    return total


def sum_kernel(jobs, *refs):
    at = 0
    for terms, count in jobs:
        refs[-1][at:at + count] = add_up(refs, terms, count)
        at += count


def summed(arrays, jobs, cost, after):
    size = sum(count for _, count in jobs)
    vmem = pl.BlockSpec(memory_space=pltpu.VMEM)
    return pl.pallas_call(
        functools.partial(sum_kernel, jobs),
        out_shape=message(size),
        in_specs=[vmem] * (len(arrays) + len(after)),
        out_specs=vmem,
        compiler_params=pltpu.CompilerParams(vmem_limit_bytes=8 * MIB),
        cost_estimate=estimate(cost),
        name="summed",
    )(*arrays, *after)


def final_kernel(terms, powers, *refs):
    out = refs[-1]
    users, blocks = out.shape[0], out.shape[2] // 128
    steps = users // 8
    scale = lax.rsqrt(add_up(refs, powers, 1)[0] + epsilon)
    total = add_up(refs, terms, 2 * blocks * steps)
    for half in range(2):
        for block in range(blocks):
            start = (half * blocks + block) * steps
            value = total[start:start + steps].reshape(users, 128)
            factor = scale[block:block + 1, :]
            value = jnp.where(factor > 0.0, value * factor, 0.0)
            out[:, half, block * 128:(block + 1) * 128] = value


def finish(arrays, terms, powers, users, columns):
    vmem = pl.BlockSpec(memory_space=pltpu.VMEM)
    return pl.pallas_call(
        functools.partial(final_kernel, terms, powers),
        out_shape=jax.ShapeDtypeStruct((users, 2, columns), jnp.float32),
        in_specs=[vmem] * len(arrays),
        out_specs=vmem,
        compiler_params=pltpu.CompilerParams(vmem_limit_bytes=8 * MIB),
        name="finish",
    )(*arrays)


def message_order(chips):
    steps = []
    for step in range(chips):
        size = 1 << (chips - 1 - step)
        first = (1 << chips) - 2 * size
        steps.append(list(range(first, first + size)))
    if chips < 3:
        return [(step, slots) for step, slots in enumerate(steps)]
    quarter, half = len(steps[0]) // 4, len(steps[1]) // 2
    parts = [steps[0][at * quarter:(at + 1) * quarter] for at in range(4)]
    order = [
        (0, parts[0]),
        (0, parts[1] + parts[2]),
        (1, steps[1][:half]),
        (0, parts[3]),
        (2, steps[2]),
        (1, steps[1][half:]),
    ]
    return order + [(step, steps[step]) for step in range(3, chips)]


def on_device(channel, precoder, visible, cluster):
    devices = lax.axis_size("ap")
    bits = devices.bit_length() - 1
    users, columns = channel.shape[3], precoder.shape[2]
    tiles = (users // 8) * (columns // 128) * 2
    orders = chip_orders(bits)
    flat = precoder.reshape(-1, columns)
    half = devices // 4

    def swap(value, bit_of):
        return lax.ppermute(value, "ap", [(i, i ^ (1 << bit_of[i & 1])) for i in range(devices)])

    arrays = []
    terms = [[] for _ in range(2 * half)]
    powers = []

    def add(array, slots, power):
        for at, slot in enumerate(slots):
            terms[slot].append((len(arrays), at * tiles))
        if power:
            powers.append((len(arrays), len(slots) * tiles))
        arrays.append(array)

    def total(slots, power, cost=8192, after=()):
        jobs = [(list(terms[slot]), tiles) for slot in slots] + ([(list(powers), 1)] if power else [])
        used = sorted({array for parts, _ in jobs for array, _ in parts})
        jobs = [([(used.index(array), start) for array, start in parts], count) for parts, count in jobs]
        return summed([arrays[array] for array in used], jobs, cost, after)

    quarter = half // 4
    sent, rows, weights, served = first_products(bits, quarter, visible, cluster.T, channel, flat)
    came = swap(sent, (0, 0))
    add(sent, [], False)
    powers.append((0, quarter * tiles))
    products = functools.partial(next_products, users, rows=rows, weights=weights, served=served)
    first, count = quarter, 4 * quarter
    send, kept = products(((0, first, count), (1, 0, quarter)), cost=COSTS[0])
    add(kept, range(quarter), False)
    add(came, range(quarter), True)
    come = swap(send, (0, 0))
    add(products(((1, first, count),), cost=COSTS[1])[0], range(first, first + count), False)
    add(come, range(first, first + count), False)
    with_power = set()
    last = 2 * half - 1
    for number, (step, slots) in enumerate(message_order(bits - 1)):
        if number == 3:
            first, count = 5 * quarter, 3 * quarter
            send = products(((0, first, count),), cost=COSTS[2], after=[now])[0]
            come = swap(send, (0, 0))
            mine = products(((1, first, count),), cost=COSTS[3], after=[send])[0]
            add(mine, range(first, first + count), False)
            add(come, range(first, first + count), False)
        power = step not in with_power
        with_power.add(step)
        after = [mine] if number == 3 else [now, came_late] if number == 5 else [now] if number == 2 else []
        now = total(slots, power, COSTS[4 + number] if number < 6 else 8192, after)
        came = swap(now, (orders[0][step], orders[1][step]))
        if number == 3:
            came_late = came
        slots = [slot + (1 << (bits - 2 - step)) for slot in slots]
        add(came, slots, power)
    used = sorted({array for array, _ in terms[last] + powers})
    return finish(
        [arrays[array] for array in used],
        [(used.index(array), start) for array, start in terms[last]],
        [(used.index(array), start) for array, start in powers],
        users, columns,
    )


def solution(mesh):
    in_specs = (
        P(("parts", "ap"), None, None, None, None),
        P(None, ("parts", "ap"), None),
        P(("parts", "ap"), None),
        P("parts", None),
    )
    out_specs = P(("parts", "ap"), None, None)
    return jax.shard_map(
        on_device, mesh=mesh, in_specs=in_specs, out_specs=out_specs, check_vma=False
    )
```

```python
import functools

import jax
import jax.numpy as jnp
from jax import lax
from jax.experimental import pallas as pl
from jax.experimental.pallas import tpu as pltpu
from jax.sharding import PartitionSpec as P

epsilon = 1e-06
MIB = 1 << 20
LOADS = 4


COSTS = (64 * MIB, 8192 * MIB, 64 * MIB, 65536 * MIB) + (
    1024 * MIB, 64 * MIB, 64 * MIB, 64 * MIB, 64 * MIB, 8192 * MIB, 1024 * MIB
)


def chip_orders(bits):
    first = list(range(1, bits))
    second = list(first)
    if bits > 2:
        second[0], second[1] = second[1], second[0]
    return second, first


def place_of(group, me, core, bits):
    away = [1 - (((group ^ me) >> bit) & 1) for bit in range(1, bits)]
    if bits > 2:
        swapped = core == 0
        away[:2] = [jnp.where(swapped, away[1], away[0]), jnp.where(swapped, away[0], away[1])]
    place = 0
    for value in away:
        place = place * 2 + value
    return place


def left_side(rows):
    antennas = rows.shape[1] // 2
    turned = jnp.concatenate([-rows[:, antennas:], rows[:, :antennas]], axis=1)
    return jnp.concatenate([rows, turned], axis=0)


def put_products(value, served, users, base, out):
    blocks, steps = value.shape[1] // 128, users // 8
    group = value.shape[0] // users // 2
    value = jnp.where(served, value, 0.0)
    for half in range(2):
        for slot in range(group):
            top = (half * group + slot) * users
            for block in range(blocks):
                piece = value[top:top + users, block * 128:(block + 1) * 128]
                start = (((base + slot) * 2 + half) * blocks + block) * steps
                out[start:start + steps] = piece.reshape(steps, 8, 128)


def write_products(users, rows, weights, served, out):
    slots = rows.shape[0] // users
    group = max(size for size in range(1, 9) if slots % size == 0)
    for base in range(0, slots, group):
        both = left_side(rows[base * users:(base + group) * users, :])
        value = jnp.dot(both, weights, preferred_element_type=jnp.float32)
        put_products(value, served, users, base, out)


def square_sum(weights):
    wide = weights.astype(jnp.float32)
    return jnp.sum(wide * wide, axis=0, keepdims=True)


def power_tile(power, served):
    power = jnp.where(served, power, 0.0)
    blocks = power.shape[1] // 128
    pieces = [power[:, block * 128:(block + 1) * 128] for block in range(blocks)]
    return jnp.concatenate(pieces + [jnp.zeros((8 - blocks, 128), jnp.float32)], axis=0)


def first_kernel(
    bits, visible, cluster, channel, precoder,
    out, rows, weights, served,
    seen, names, raw, sems,
):
    me = lax.axis_index("ap")
    held, users, antennas = raw.shape[1], raw.shape[3], raw.shape[4]
    loads = [
        pltpu.make_async_copy(visible, seen, sems.at[0]),
        pltpu.make_async_copy(channel, raw, sems.at[1]),
        pltpu.make_async_copy(cluster, names, sems.at[2]),
    ]
    depth = weights.shape[0] // LOADS
    for part in range(LOADS):
        at = pl.ds(part * depth, depth)
        loads.append(pltpu.make_async_copy(precoder.at[at], weights.at[at], sems.at[3 + part]))
    for load in loads:
        load.start()
    rows[...] = jnp.zeros_like(rows)
    loads[0].wait()
    places = []
    for v in range(held):
        core = seen[0, v] & 1
        places.append((1 - (core ^ (me & 1)), place_of(seen[0, v], me, core, bits) * users))
    loads[1].wait()
    for v, (keep, place) in enumerate(places):
        at = pl.ds(pl.multiple_of(place, users), users)
        rows[keep, at, 0:antennas] = raw[0, v, 0]
        rows[keep, at, antennas:2 * antennas] = raw[0, v, 1]
    loads[2].wait()
    here = jnp.max((names[...] == me).astype(jnp.float32), axis=0, keepdims=True)
    served[...] = here
    size = (out.shape[0] // (weights.shape[1] // 128) // 2) * 8
    both = left_side(rows[0, 0:size, :])
    value = power = None
    for part in range(LOADS):
        loads[3 + part].wait()
        at = slice(part * depth, (part + 1) * depth)
        block = weights[at, :]
        term = jnp.dot(both[:, at], block, preferred_element_type=jnp.float32)
        square = square_sum(block)
        value = term if value is None else value + term
        power = square if power is None else power + square
    put_products(value, here > 0.0, users, 0, out)
    out[out.shape[0] - 1] = power_tile(power, here > 0.0)


def next_kernel(users, jobs, rows, weights, served, *refs):
    for (keep, first, slots), out in zip(jobs, refs[-len(jobs):]):
        mine = rows.at[keep, first * users:(first + slots) * users]
        write_products(users, mine, weights[...], served[...] > 0.0, out)


def message(tiles):
    return jax.ShapeDtypeStruct((tiles, 8, 128), jnp.float32)


def estimate(size=8192):
    return pl.CostEstimate(flops=size, bytes_accessed=size, transcendentals=0)


def first_products(bits, first, visible, cluster, channel, precoder):
    users, antennas = channel.shape[3], channel.shape[4]
    columns = precoder.shape[1]
    slots = 1 << (bits - 1)
    tiles = first * (users // 8) * (columns // 128) * 2
    vmem = pl.BlockSpec(memory_space=pltpu.VMEM)
    hbm = pl.BlockSpec(memory_space=pltpu.HBM)
    operands = (visible, cluster, channel, precoder)
    return pl.pallas_call(
        functools.partial(first_kernel, bits),
        out_shape=(
            message(tiles + 1),
            jax.ShapeDtypeStruct((2, slots * users, 2 * antennas), jnp.bfloat16),
            jax.ShapeDtypeStruct(precoder.shape, jnp.bfloat16),
            jax.ShapeDtypeStruct((1, columns), jnp.float32),
        ),
        in_specs=[hbm] * 4,
        out_specs=(vmem,) * 4,
        scratch_shapes=[
            pltpu.SMEM(visible.shape, jnp.int32),
            pltpu.VMEM(cluster.shape, jnp.int32),
            pltpu.VMEM(channel.shape, jnp.bfloat16),
            pltpu.SemaphoreType.DMA((3 + LOADS,)),
        ],
        compiler_params=pltpu.CompilerParams(vmem_limit_bytes=52 * MIB if slots > 8 else 24 * MIB),
        cost_estimate=estimate(),
        name="first_products",
    )(*[pltpu.with_memory_space_constraint(operand, pltpu.HBM) for operand in operands])


def next_products(users, jobs, cost, rows, weights, served, after=()):
    vmem = pl.BlockSpec(memory_space=pltpu.VMEM)
    big = max(slots for _, _, slots in jobs) > 8
    tiles = (users // 8) * (weights.shape[1] // 128) * 2
    return pl.pallas_call(
        functools.partial(next_kernel, users, jobs),
        out_shape=[message(slots * tiles) for _, _, slots in jobs],
        in_specs=[vmem] * (3 + len(after)),
        out_specs=[vmem] * len(jobs),
        compiler_params=pltpu.CompilerParams(vmem_limit_bytes=48 * MIB if big else 16 * MIB),
        cost_estimate=estimate(cost),
        name="next_products",
    )(rows, weights, served, *after)


def add_up(refs, terms, count):
    total = refs[terms[0][0]][terms[0][1]:terms[0][1] + count]
    for ref, start in terms[1:]:
        total = total + refs[ref][start:start + count]
    return total


def sum_kernel(jobs, *refs):
    at = 0
    for terms, count in jobs:
        refs[-1][at:at + count] = add_up(refs, terms, count)
        at += count


def summed(arrays, jobs, cost, after):
    size = sum(count for _, count in jobs)
    vmem = pl.BlockSpec(memory_space=pltpu.VMEM)
    return pl.pallas_call(
        functools.partial(sum_kernel, jobs),
        out_shape=message(size),
        in_specs=[vmem] * (len(arrays) + len(after)),
        out_specs=vmem,
        compiler_params=pltpu.CompilerParams(vmem_limit_bytes=8 * MIB),
        cost_estimate=estimate(cost),
        name="summed",
    )(*arrays, *after)


def final_kernel(terms, powers, *refs):
    out = refs[-1]
    users, blocks = out.shape[0], out.shape[2] // 128
    steps = users // 8
    scale = lax.rsqrt(add_up(refs, powers, 1)[0] + epsilon)
    for half in range(2):
        total = add_up(refs, terms[half], blocks * steps)
        for block in range(blocks):
            start = block * steps
            value = total[start:start + steps].reshape(users, 128)
            factor = scale[block:block + 1, :]
            value = jnp.where(factor > 0.0, value * factor, 0.0)
            out[:, half, block * 128:(block + 1) * 128] = value


def finish(arrays, terms, powers, users, columns):
    vmem = pl.BlockSpec(memory_space=pltpu.VMEM)
    return pl.pallas_call(
        functools.partial(final_kernel, terms, powers),
        out_shape=jax.ShapeDtypeStruct((users, 2, columns), jnp.float32),
        in_specs=[vmem] * len(arrays),
        out_specs=vmem,
        compiler_params=pltpu.CompilerParams(vmem_limit_bytes=8 * MIB),
        name="finish",
    )(*arrays)


def message_order(chips):
    steps = []
    for step in range(chips):
        size = 1 << (chips - 1 - step)
        first = (1 << chips) - 2 * size
        steps.append([(slot, part) for slot in range(first, first + size) for part in range(2)])
    if chips < 3:
        return [(step, pieces) for step, pieces in enumerate(steps)]
    quarter, half = len(steps[0]) // 4, len(steps[1]) // 2
    parts = [steps[0][at * quarter:(at + 1) * quarter] for at in range(4)]
    order = [
        (0, parts[0]),
        (0, parts[2] + parts[3][::2]),
        (1, steps[1][:half]),
        (0, parts[1]),
        (0, parts[3][1::2]),
        (2, steps[2]),
        (1, steps[1][half:]),
    ]
    return order + [(step, steps[step]) for step in range(3, chips)]


def on_device(channel, precoder, visible, cluster):
    devices = lax.axis_size("ap")
    bits = devices.bit_length() - 1
    users, columns = channel.shape[3], precoder.shape[2]
    tiles = (users // 8) * (columns // 128)
    orders = chip_orders(bits)
    flat = precoder.reshape(-1, columns)
    half = devices // 4

    def swap(value, bit_of):
        return lax.ppermute(value, "ap", [(i, i ^ (1 << bit_of[i & 1])) for i in range(devices)])

    arrays = []
    terms = {(slot, part): [] for slot in range(2 * half) for part in range(2)}
    powers = []

    def add(array, pieces, power):
        for at, piece in enumerate(pieces):
            terms[piece].append((len(arrays), at * tiles))
        if power:
            powers.append((len(arrays), len(pieces) * tiles))
        arrays.append(array)

    def pieces_of(first, count):
        return [(slot, part) for slot in range(first, first + count) for part in range(2)]

    def total(pieces, power, cost=8192, after=()):
        jobs = [(list(terms[piece]), tiles) for piece in pieces]
        jobs += [(list(powers), 1)] * int(power)
        used = sorted({array for parts, _ in jobs for array, _ in parts})
        jobs = [([(used.index(array), start) for array, start in parts], count) for parts, count in jobs]
        return summed([arrays[array] for array in used], jobs, cost, after)

    quarter = half // 4
    sent, rows, weights, served = first_products(bits, quarter, visible, cluster.T, channel, flat)
    came = swap(sent, (0, 0))
    add(sent, [], False)
    powers.append((0, 2 * quarter * tiles))
    products = functools.partial(next_products, users, rows=rows, weights=weights, served=served)
    first, count = quarter, 4 * quarter
    send, kept = products(((0, first, count), (1, 0, quarter)), cost=COSTS[0])
    add(kept, pieces_of(0, quarter), False)
    add(came, pieces_of(0, quarter), True)
    come = swap(send, (0, 0))
    add(products(((1, first, count),), cost=COSTS[1])[0], pieces_of(first, count), False)
    add(come, pieces_of(first, count), False)
    with_power = set()
    last = [(2 * half - 1, part) for part in range(2)]
    for number, (step, pieces) in enumerate(message_order(bits - 1)):
        if number == 3:
            first, count = 5 * quarter, 3 * quarter
            send = products(((0, first, count),), cost=COSTS[2], after=[now])[0]
            come = swap(send, (0, 0))
            mine = products(((1, first, count),), cost=COSTS[3], after=[send])[0]
            add(mine, pieces_of(first, count), False)
            add(come, pieces_of(first, count), False)
        power = step not in with_power
        with_power.add(step)
        after = [mine] if number == 3 else [now] if number in (2, 4, 6) else []
        now = total(pieces, power, COSTS[4 + number] if number < 7 else 8192, after)
        came = swap(now, (orders[0][step], orders[1][step]))
        pieces = [(slot + (1 << (bits - 2 - step)), part) for slot, part in pieces]
        add(came, pieces, power)
    used = sorted({array for parts in [terms[piece] for piece in last] + [powers] for array, _ in parts})
    return finish(
        [arrays[array] for array in used],
        [[(used.index(array), start) for array, start in terms[piece]] for piece in last],
        [(used.index(array), start) for array, start in powers],
        users, columns,
    )


def solution(mesh):
    in_specs = (
        P(("parts", "ap"), None, None, None, None),
        P(None, ("parts", "ap"), None),
        P(("parts", "ap"), None),
        P("parts", None),
    )
    out_specs = P(("parts", "ap"), None, None)
    return jax.shard_map(
        on_device, mesh=mesh, in_specs=in_specs, out_specs=out_specs, check_vma=False
    )
```

```python
import functools

import jax
import jax.numpy as jnp
from jax import lax
from jax.experimental import pallas as pl
from jax.experimental.pallas import tpu as pltpu
from jax.sharding import PartitionSpec as P

epsilon = 1e-06
MIB = 1 << 20
LOADS = 8


COSTS = (64 * MIB, 8192 * MIB, 64 * MIB, 65536 * MIB) + (
    1024 * MIB, 64 * MIB, 64 * MIB, 64 * MIB, 64 * MIB, 8192 * MIB, 1024 * MIB
)


def chip_orders(bits):
    first = list(range(1, bits))
    second = list(first)
    if bits > 2:
        second[0], second[1] = second[1], second[0]
    return second, first


def place_of(group, me, core, bits):
    away = [1 - (((group ^ me) >> bit) & 1) for bit in range(1, bits)]
    if bits > 2:
        swapped = core == 0
        away[:2] = [jnp.where(swapped, away[1], away[0]), jnp.where(swapped, away[0], away[1])]
    place = 0
    for value in away:
        place = place * 2 + value
    return place


def left_side(rows):
    antennas = rows.shape[1] // 2
    turned = jnp.concatenate([-rows[:, antennas:], rows[:, :antennas]], axis=1)
    return jnp.concatenate([rows, turned], axis=0)


def put_products(value, served, users, base, out):
    blocks, steps = value.shape[1] // 128, users // 8
    group = value.shape[0] // users // 2
    value = jnp.where(served, value, 0.0)
    for half in range(2):
        for slot in range(group):
            top = (half * group + slot) * users
            for block in range(blocks):
                piece = value[top:top + users, block * 128:(block + 1) * 128]
                start = (((base + slot) * 2 + half) * blocks + block) * steps
                out[start:start + steps] = piece.reshape(steps, 8, 128)


def write_products(users, rows, weights, served, out):
    slots = rows.shape[0] // users
    group = max(size for size in range(1, 9) if slots % size == 0)
    for base in range(0, slots, group):
        both = left_side(rows[base * users:(base + group) * users, :])
        value = jnp.dot(both, weights, preferred_element_type=jnp.float32)
        put_products(value, served, users, base, out)


def square_sum(weights):
    wide = weights.astype(jnp.float32)
    return jnp.sum(wide * wide, axis=0, keepdims=True)


def power_tile(power, served):
    power = jnp.where(served, power, 0.0)
    blocks = power.shape[1] // 128
    pieces = [power[:, block * 128:(block + 1) * 128] for block in range(blocks)]
    return jnp.concatenate(pieces + [jnp.zeros((8 - blocks, 128), jnp.float32)], axis=0)


def first_kernel(
    bits, visible, cluster, channel, precoder,
    out, rows, weights, served,
    seen, names, raw, sems,
):
    me = lax.axis_index("ap")
    held, users, antennas = raw.shape[1], raw.shape[3], raw.shape[4]
    loads = [
        pltpu.make_async_copy(visible, seen, sems.at[0]),
        pltpu.make_async_copy(channel, raw, sems.at[1]),
        pltpu.make_async_copy(cluster, names, sems.at[2]),
    ]
    depth = weights.shape[0] // LOADS
    for part in range(LOADS):
        at = pl.ds(part * depth, depth)
        loads.append(pltpu.make_async_copy(precoder.at[at], weights.at[at], sems.at[3 + part]))
    for load in loads:
        load.start()
    rows[...] = jnp.zeros_like(rows)
    loads[0].wait()
    places = []
    for v in range(held):
        core = seen[0, v] & 1
        places.append((1 - (core ^ (me & 1)), place_of(seen[0, v], me, core, bits) * users))
    loads[1].wait()
    for v, (keep, place) in enumerate(places):
        at = pl.ds(pl.multiple_of(place, users), users)
        rows[keep, at, 0:antennas] = raw[0, v, 0]
        rows[keep, at, antennas:2 * antennas] = raw[0, v, 1]
    loads[2].wait()
    here = jnp.max((names[...] == me).astype(jnp.float32), axis=0, keepdims=True)
    served[...] = here
    size = (out.shape[0] // (weights.shape[1] // 128) // 2) * 8
    both = left_side(rows[0, 0:size, :])
    value = power = None
    for part in range(LOADS):
        loads[3 + part].wait()
        at = slice(part * depth, (part + 1) * depth)
        block = weights[at, :]
        term = jnp.dot(both[:, at], block, preferred_element_type=jnp.float32)
        square = square_sum(block)
        value = term if value is None else value + term
        power = square if power is None else power + square
    put_products(value, here > 0.0, users, 0, out)
    out[out.shape[0] - 1] = power_tile(power, here > 0.0)


def next_kernel(users, jobs, rows, weights, served, *refs):
    for (keep, first, slots), out in zip(jobs, refs[-len(jobs):]):
        mine = rows.at[keep, first * users:(first + slots) * users]
        write_products(users, mine, weights[...], served[...] > 0.0, out)


def message(tiles):
    return jax.ShapeDtypeStruct((tiles, 8, 128), jnp.float32)


def estimate(size=8192):
    return pl.CostEstimate(flops=size, bytes_accessed=size, transcendentals=0)


def first_products(bits, first, visible, cluster, channel, precoder):
    users, antennas = channel.shape[3], channel.shape[4]
    columns = precoder.shape[1]
    slots = 1 << (bits - 1)
    tiles = first * (users // 8) * (columns // 128) * 2
    vmem = pl.BlockSpec(memory_space=pltpu.VMEM)
    hbm = pl.BlockSpec(memory_space=pltpu.HBM)
    operands = (visible, cluster, channel, precoder)
    return pl.pallas_call(
        functools.partial(first_kernel, bits),
        out_shape=(
            message(tiles + 1),
            jax.ShapeDtypeStruct((2, slots * users, 2 * antennas), jnp.bfloat16),
            jax.ShapeDtypeStruct(precoder.shape, jnp.bfloat16),
            jax.ShapeDtypeStruct((1, columns), jnp.float32),
        ),
        in_specs=[hbm] * 4,
        out_specs=(vmem,) * 4,
        scratch_shapes=[
            pltpu.SMEM(visible.shape, jnp.int32),
            pltpu.VMEM(cluster.shape, jnp.int32),
            pltpu.VMEM(channel.shape, jnp.bfloat16),
            pltpu.SemaphoreType.DMA((3 + LOADS,)),
        ],
        compiler_params=pltpu.CompilerParams(vmem_limit_bytes=52 * MIB if slots > 8 else 24 * MIB),
        cost_estimate=estimate(),
        name="first_products",
    )(*[pltpu.with_memory_space_constraint(operand, pltpu.HBM) for operand in operands])


def next_products(users, jobs, cost, rows, weights, served, after=()):
    vmem = pl.BlockSpec(memory_space=pltpu.VMEM)
    big = max(slots for _, _, slots in jobs) > 8
    tiles = (users // 8) * (weights.shape[1] // 128) * 2
    return pl.pallas_call(
        functools.partial(next_kernel, users, jobs),
        out_shape=[message(slots * tiles) for _, _, slots in jobs],
        in_specs=[vmem] * (3 + len(after)),
        out_specs=[vmem] * len(jobs),
        compiler_params=pltpu.CompilerParams(vmem_limit_bytes=48 * MIB if big else 16 * MIB),
        cost_estimate=estimate(cost),
        name="next_products",
    )(rows, weights, served, *after)


def add_up(refs, terms, count):
    total = refs[terms[0][0]][terms[0][1]:terms[0][1] + count]
    for ref, start in terms[1:]:
        total = total + refs[ref][start:start + count]
    return total


def sum_kernel(jobs, *refs):
    at = 0
    for terms, count in jobs:
        refs[-1][at:at + count] = add_up(refs, terms, count)
        at += count


def summed(arrays, jobs, cost, after):
    size = sum(count for _, count in jobs)
    vmem = pl.BlockSpec(memory_space=pltpu.VMEM)
    return pl.pallas_call(
        functools.partial(sum_kernel, jobs),
        out_shape=message(size),
        in_specs=[vmem] * (len(arrays) + len(after)),
        out_specs=vmem,
        compiler_params=pltpu.CompilerParams(vmem_limit_bytes=8 * MIB),
        cost_estimate=estimate(cost),
        name="summed",
    )(*arrays, *after)


def final_kernel(terms, powers, *refs):
    out = refs[-1]
    users, blocks = out.shape[0], out.shape[2] // 128
    steps = users // 8
    scale = lax.rsqrt(add_up(refs, powers, 1)[0] + epsilon)
    total = add_up(refs, terms, 2 * blocks * steps)
    for half in range(2):
        for block in range(blocks):
            start = (half * blocks + block) * steps
            value = total[start:start + steps].reshape(users, 128)
            factor = scale[block:block + 1, :]
            value = jnp.where(factor > 0.0, value * factor, 0.0)
            out[:, half, block * 128:(block + 1) * 128] = value


def finish(arrays, terms, powers, users, columns):
    vmem = pl.BlockSpec(memory_space=pltpu.VMEM)
    return pl.pallas_call(
        functools.partial(final_kernel, terms, powers),
        out_shape=jax.ShapeDtypeStruct((users, 2, columns), jnp.float32),
        in_specs=[vmem] * len(arrays),
        out_specs=vmem,
        compiler_params=pltpu.CompilerParams(vmem_limit_bytes=8 * MIB),
        name="finish",
    )(*arrays)


def message_order(chips):
    steps = []
    for step in range(chips):
        size = 1 << (chips - 1 - step)
        first = (1 << chips) - 2 * size
        steps.append(list(range(first, first + size)))
    if chips < 3:
        return [(step, slots) for step, slots in enumerate(steps)]
    quarter, half = len(steps[0]) // 4, len(steps[1]) // 2
    parts = [steps[0][at * quarter:(at + 1) * quarter] for at in range(4)]
    order = [
        (0, parts[0]),
        (0, parts[2]),
        (1, steps[1][:half]),
        (0, parts[1]),
        (0, parts[3]),
        (2, steps[2]),
        (1, steps[1][half:]),
    ]
    return order + [(step, steps[step]) for step in range(3, chips)]


def on_device(channel, precoder, visible, cluster):
    devices = lax.axis_size("ap")
    bits = devices.bit_length() - 1
    users, columns = channel.shape[3], precoder.shape[2]
    tiles = (users // 8) * (columns // 128) * 2
    orders = chip_orders(bits)
    flat = precoder.reshape(-1, columns)
    half = devices // 4

    def swap(value, bit_of):
        return lax.ppermute(value, "ap", [(i, i ^ (1 << bit_of[i & 1])) for i in range(devices)])

    arrays = []
    terms = [[] for _ in range(2 * half)]
    powers = []

    def add(array, slots, power):
        for at, slot in enumerate(slots):
            terms[slot].append((len(arrays), at * tiles))
        if power:
            powers.append((len(arrays), len(slots) * tiles))
        arrays.append(array)

    def total(slots, power, cost=8192, after=()):
        jobs = [(list(terms[slot]), tiles) for slot in slots] + ([(list(powers), 1)] if power else [])
        used = sorted({array for parts, _ in jobs for array, _ in parts})
        jobs = [([(used.index(array), start) for array, start in parts], count) for parts, count in jobs]
        return summed([arrays[array] for array in used], jobs, cost, after)

    quarter = half // 4
    sent, rows, weights, served = first_products(bits, quarter, visible, cluster.T, channel, flat)
    came = swap(sent, (0, 0))
    add(sent, [], False)
    powers.append((0, quarter * tiles))
    products = functools.partial(next_products, users, rows=rows, weights=weights, served=served)
    first, count = quarter, 4 * quarter
    send, kept = products(((0, first, count), (1, 0, quarter)), cost=COSTS[0])
    add(kept, range(quarter), False)
    add(came, range(quarter), True)
    come = swap(send, (0, 0))
    add(products(((1, first, count),), cost=COSTS[1])[0], range(first, first + count), False)
    add(come, range(first, first + count), False)
    with_power = set()
    last = 2 * half - 1
    for number, (step, slots) in enumerate(message_order(bits - 1)):
        if number == 3:
            first, count = 5 * quarter, 3 * quarter
            send = products(((0, first, count),), cost=COSTS[2], after=[now])[0]
            come = swap(send, (0, 0))
            mine = products(((1, first, count),), cost=COSTS[3], after=[send])[0]
            add(mine, range(first, first + count), False)
            add(come, range(first, first + count), False)
        power = step not in with_power
        with_power.add(step)
        after = [mine] if number == 3 else [now] if number in (2, 4, 6) else []
        now = total(slots, power, COSTS[4 + number] if number < 7 else 8192, after)
        came = swap(now, (orders[0][step], orders[1][step]))
        slots = [slot + (1 << (bits - 2 - step)) for slot in slots]
        add(came, slots, power)
    used = sorted({array for array, _ in terms[last] + powers})
    return finish(
        [arrays[array] for array in used],
        [(used.index(array), start) for array, start in terms[last]],
        [(used.index(array), start) for array, start in powers],
        users, columns,
    )


def solution(mesh):
    in_specs = (
        P(("parts", "ap"), None, None, None, None),
        P(None, ("parts", "ap"), None),
        P(("parts", "ap"), None),
        P("parts", None),
    )
    out_specs = P(("parts", "ap"), None, None)
    return jax.shard_map(
        on_device, mesh=mesh, in_specs=in_specs, out_specs=out_specs, check_vma=False
    )
```
